32 devices in a mesh: seq: 8 (over z, y), row: 4 (over x, core).
Axes of the slice: x: 2, y: 2, z: 4, core: 2. Of those that a mesh axis runs over, the one named last changes fastest.
Arguments:
- tokens: bfloat16 [4, 5120, 512], P('row', 'seq'), may hold values from -6 to 6
- cotangent: bfloat16 [4, 5120, 512], P('row', 'seq'), may hold values from -6 to 6
- w_query: bfloat16 [512, 512], replicated, may hold values from -0.25 to 0.25
- w_kv: bfloat16 [512, 128], replicated, may hold values from -0.25 to 0.25
- w_route: bfloat16 [512, 8], replicated, may hold values from -0.5 to 0.5
- w_out: bfloat16 [512, 512], replicated, may hold values from -20 to 20
- w_up: bfloat16 [512, 2048], replicated, may hold values from -0.25 to 0.25
- bias_up: float32 [2048], replicated, may hold values from -3 to 3
- w_down: bfloat16 [2048, 512], replicated, may hold values from -0.125 to 0.125
- bias_down: float32 [512], replicated, may hold values from -4 to 4
- gain_one: float32 [512], replicated, may hold values from 0.5 to 1.5
- shift_one: float32 [512], replicated, may hold values from -0.15625 to 0.15625
- gain_two: float32 [512], replicated, may hold values from 0.5 to 1.5
- shift_two: float32 [512], replicated, may hold values from -3 to 3
- choices: int32 [4, 5120, 2], P('row', 'seq'), may hold values from 0 to 7, all different within a row
- segment_ids: int32 [4, 5120], P('row', 'seq'), may hold values from 0 to 3, as said below
Outputs:
- layer_out: bfloat16 [4, 5120, 512], P('row', 'seq')
- grad_tokens: float32 [4, 5120, 512], P('row', 'seq')
- grad_query: float32 [512, 512], replicated
- grad_kv: float32 [512, 128], replicated
- grad_route: float32 [512, 8], replicated
- grad_out: float32 [512, 512], replicated
- grad_up: float32 [512, 2048], replicated
- grad_bias_up: float32 [2048], replicated
- grad_down: float32 [2048, 512], replicated
- grad_bias_down: float32 [512], replicated
- grad_gain_one: float32 [512], replicated
- grad_shift_one: float32 [512], replicated
- grad_gain_two: float32 [512], replicated
- grad_shift_two: float32 [512], replicated
The draws below stay inside these ranges and needn't reach their ends.
Inputs may be any that keep to these rules, and one draw needn't show every extreme that they name: For each token, its two experts choices[t, 0] and choices[t, 1] differ; different tokens may name the same experts, and every expert is named by some token. `segment_ids`: each row holds 4 documents as contiguous runs, numbered 0 to 3 in order along the row, every one present, of uneven lengths; tokens attend to tokens of their own row with the same id.
All inputs are finite; a program needn't handle non-finite values.
Results may differ from the reference program's by a relative error of at most 0.015.
Values may be sent and summed in bfloat16 or wider, within the bound.
No kernel may reach another device: no remote copies, remote signals or barrier semaphores. Data moves between devices by JAX's collectives and lax.ppermute only.
A program may use at most 128 MiB of HBM per device.

```python
import math
import jax
import jax.numpy as jnp
from jax import lax

D = 512
HD = 64
EXPERTS = 8
FF = 2048
DOCS = 4
ROW_LEN = 5120
ROWS = 4


def draw_segment_ids(key, part):
    key = jax.random.fold_in(key, 7)
    key_weights = jax.random.fold_in(key, 1)
    key_big = jax.random.fold_in(key, 2)
    key_extra = jax.random.fold_in(key, 3)
    weights = jax.random.randint(key_weights, (ROWS, DOCS), 1, 5)
    big_index = jax.random.randint(key_big, (ROWS, 1), 0, DOCS)
    is_big = jnp.arange(DOCS, dtype=jnp.int32)[None, :] == big_index
    others = jnp.sum(jnp.where(is_big, 0, weights), axis=1, keepdims=True)
    extra = jax.random.randint(key_extra, (ROWS, 1), 1, 5)
    weights = jnp.where(is_big, 2 * others + extra, weights).astype(jnp.int32)
    running = jnp.cumsum(weights, axis=1).astype(jnp.int32)
    whole = running[:, -1:]
    bounds = running[:, :-1] * ROW_LEN // whole
    positions = jnp.arange(ROW_LEN, dtype=jnp.int32)
    return jnp.sum((positions[None, :, None] >= bounds[:, None, :]).astype(jnp.int32), axis=2).astype(jnp.int32)


def levels(stream_key, shape, cuts, smallest, largest):
    def one(dim, shards_of):
        steps = jax.random.uniform(jax.random.fold_in(jax.random.fold_in(stream_key, 6), dim), (shards_of,), jnp.float32, smallest / len(cuts), largest / len(cuts))
        return jnp.repeat(jnp.exp(steps), shape[dim] // shards_of).reshape((-1,) + (1,) * (len(shape) - dim - 1))

    level = one(*cuts[0])
    for cut in cuts[1:]:
        level = level * one(*cut)
    return level


def choose_distinct(own_key, rows, number_of, top, lift):
    order = jax.random.permutation(jax.random.fold_in(own_key, 1), number_of)
    favour = order
    for power in range(3):
        favour = favour * favour // number_of
    favour = favour * lift // number_of
    lots = jax.random.randint(jax.random.fold_in(own_key, 2), (rows, number_of), 0, 4096) + favour
    fixed_rows = jax.random.permutation(jax.random.fold_in(own_key, 3), rows)[jnp.arange(number_of) % rows]
    lots = jnp.where(jnp.arange(rows)[:, None] == fixed_rows[None, :], 1 << 14, lots)
    merit = lots * number_of + jnp.arange(number_of)
    return lax.top_k(merit.astype(jnp.int32), top)[1].astype(jnp.int32)


def scatter_about(key, extent, deviation, most, cuts=(), kind=jnp.bfloat16):
    drawn = jax.random.normal(key, extent, jnp.float32) * deviation
    if len(cuts) > 0:
        drawn = levels(key, extent, cuts, -0.22, 0.18) * drawn
    return jnp.clip(drawn, min=-most, max=most).astype(kind)


def setup_inputs(seed: int = 0) -> dict:
    arg_keys = jax.random.split(jax.random.key(seed), 17)
    tokens = scatter_about(arg_keys[0], (ROWS, ROW_LEN, D), 1.0, 6.0, ((0, 4), (1, 8)))
    cotangent = scatter_about(arg_keys[1], (ROWS, ROW_LEN, D), 1.0, 6.0, ((0, 4), (1, 8)))
    w_query = scatter_about(arg_keys[2], (D, EXPERTS * HD), D ** -0.5, 0.25)
    w_kv = scatter_about(arg_keys[3], (D, 2 * HD), D ** -0.5, 0.25)
    w_route = scatter_about(arg_keys[4], (D, EXPERTS), (0.75 * D ** -0.5), 0.5)
    w_out = scatter_about(arg_keys[5], (EXPERTS * HD, D), (0.1 * (ROW_LEN // DOCS) ** 0.5), 20.0)
    w_up = scatter_about(arg_keys[6], (D, FF), D ** -0.5, 0.25)
    bias_up = scatter_about(arg_keys[7], (FF,), 0.2, 3.0, (), jnp.float32)
    w_down = scatter_about(arg_keys[8], (FF, D), FF ** -0.5, 0.125)
    bias_down = scatter_about(arg_keys[9], (D,), 0.3, 4.0, (), jnp.float32)
    gain_one = jnp.clip(1.0 + 0.1 * jax.random.normal(arg_keys[10], (D,), jnp.float32), 0.5, 1.5)
    shift_one = scatter_about(arg_keys[11], (D,), 0.01, 0.15625, (), jnp.float32)
    gain_two = jnp.clip(1.0 + 0.1 * jax.random.normal(arg_keys[12], (D,), jnp.float32), 0.5, 1.5)
    shift_two = scatter_about(arg_keys[13], (D,), 0.2, 3.0, (), jnp.float32)
    choices = choose_distinct(arg_keys[14], ROWS * ROW_LEN, EXPERTS, 2, 2048).reshape((ROWS, ROW_LEN, 2))
    segment_ids = draw_segment_ids(jax.random.fold_in(arg_keys[16], 71), 0)
    return dict(tokens=tokens, cotangent=cotangent, w_query=w_query, w_kv=w_kv, w_route=w_route, w_out=w_out, w_up=w_up, bias_up=bias_up, w_down=w_down, bias_down=bias_down, gain_one=gain_one, shift_one=shift_one, gain_two=gain_two, shift_two=shift_two, choices=choices, segment_ids=segment_ids)


@jax.custom_vjp
def low(v):
    return lax.optimization_barrier(v.astype(jnp.bfloat16)).astype(jnp.float32)

@jax.custom_vjp
def low_back(v):
    return v

def low_keep(v):
    return (low(v), None)

def low_pass(kept, grad):
    return (grad,)

def back_keep(v):
    return (v, None)

def back_low(kept, grad):
    return (low(grad),)
low.defvjp(low_keep, low_pass)
low_back.defvjp(back_keep, back_low)
epsilon = 1e-05
highest = lax.Precision.HIGHEST

def normalize(values_in, gain, shift):
    row_mean = lax.optimization_barrier(jnp.mean(values_in, axis=-1, keepdims=True))
    centred = values_in - row_mean
    variance = lax.optimization_barrier(jnp.mean(centred * centred, axis=-1, keepdims=True))
    return centred * lax.rsqrt(variance + epsilon) * gain + shift

def row_layer(row_input, row_segments, row_choices, weights_now):
    w_query, w_kv, w_route, w_out, w_up, bias_up, w_down, bias_down, gain_one, shift_one, gain_two, shift_two = weights_now
    normed_low = low(normalize(row_input, gain_one, shift_one))
    query_all = low_back(jnp.dot(normed_low, w_query, precision=highest))
    keys_values = low_back(jnp.dot(normed_low, w_kv, precision=highest))
    logits = low_back(jnp.dot(normed_low, w_route, precision=highest))
    onehot = (row_choices[:, :, None] == jnp.arange(EXPERTS, dtype=jnp.int32)[None, None, :]).astype(jnp.float32)
    picked = jnp.einsum('tje,te->tj', onehot, logits, precision=highest)
    gate_weights = jax.nn.softmax(picked, axis=-1)
    queries = low(jnp.einsum('tje,ted->jtd', onehot, query_all.reshape(ROW_LEN, EXPERTS, HD), precision=highest))
    key_rows = low(keys_values[:, :HD])
    value_rows = low(keys_values[:, HD:])
    block_rows = math.gcd(ROW_LEN, 512)
    block_count = ROW_LEN // block_rows
    query_blocks = queries.reshape(2, block_count, block_rows, HD).transpose(1, 0, 2, 3)
    segment_blocks = row_segments.reshape(block_count, block_rows)

    def attend(pieces):
        query_block, segment_block = pieces
        scores = low_back(HD ** (-0.5) * jnp.einsum('jtd,kd->jtk', query_block, key_rows, precision=highest))
        allowed = segment_block[None, :, None] == row_segments[None, None, :]
        scores = jnp.where(allowed, scores, -1e+30)
        maxima = lax.optimization_barrier(jnp.max(scores, axis=-1, keepdims=True))
        exponent_terms = jnp.where(allowed, jnp.exp(scores - maxima), 0.0)
        probability = low(exponent_terms / lax.optimization_barrier(jnp.sum(exponent_terms, axis=-1, keepdims=True)))
        return jnp.einsum('jtk,kd->jtd', probability, value_rows, precision=highest)
    blocks_out = lax.map(jax.checkpoint(attend), (query_blocks, segment_blocks))
    head_outputs = low_back(blocks_out.transpose(1, 0, 2, 3).reshape(2, ROW_LEN, HD))
    mixed = low(jnp.einsum('tje,tj,jtd->ted', onehot, gate_weights, head_outputs, precision=highest).reshape(ROW_LEN, EXPERTS * HD))
    attended = low_back(jnp.dot(mixed, w_out, precision=highest))
    middle = row_input + attended
    second_normed = low(normalize(middle, gain_two, shift_two))
    pre_activation = low_back(jnp.dot(second_normed, w_up, precision=highest) + bias_up)
    activated = low(jax.nn.gelu(pre_activation, approximate=True))
    branch_ffn = low_back(jnp.dot(activated, w_down, precision=highest) + bias_down)
    return middle + branch_ffn

def reference(tokens, cotangent, w_query, w_kv, w_route, w_out, w_up, bias_up, w_down, bias_down, gain_one, shift_one, gain_two, shift_two, choices, segment_ids):
    inputs_f = tokens.astype(jnp.float32)
    weights_f = tuple((weight.astype(jnp.float32) for weight in (w_query, w_kv, w_route, w_out, w_up, bias_up, w_down, bias_down, gain_one, shift_one, gain_two, shift_two)))

    def forward(inputs_now, weights_now):

        def row_step(state, pieces):
            row_input, row_segments, row_choices = pieces
            return (state, row_layer(row_input, row_segments, row_choices, weights_now))
        _, outputs = lax.scan(row_step, jnp.zeros((), jnp.float32), (inputs_now, segment_ids, choices))
        return outputs
    outputs, pullback = jax.vjp(forward, inputs_f, weights_f)
    grad_inputs, grad_weights = pullback(cotangent.astype(jnp.float32))
    return (outputs.astype(jnp.bfloat16), grad_inputs, grad_weights[0], grad_weights[1], grad_weights[2], grad_weights[3], grad_weights[4], grad_weights[5], grad_weights[6], grad_weights[7], grad_weights[8], grad_weights[9], grad_weights[10], grad_weights[11])
```

```python
import functools

import jax
import jax.numpy as jnp
from jax import lax
from jax.experimental import pallas as pl
from jax.experimental.pallas import tpu as pltpu
from jax.sharding import PartitionSpec as P

f32 = jnp.float32
bf16 = jnp.bfloat16
epsilon = 1e-05
lanes = 128
half = 64
chunk = 128
pad_rows = 16
stat_rows = 80
masked = -2e30
lowest = -1e30
mib = 1 << 20


def nn(a, b):
    return lax.dot_general(a, b, (((1,), (0,)), ((), ())), preferred_element_type=f32)


def nt(a, b):
    return lax.dot_general(a, b, (((1,), (1,)), ((), ())), preferred_element_type=f32)


def tn(a, b):
    return lax.dot_general(a, b, (((0,), (0,)), ((), ())), preferred_element_type=f32)


def lane_ids(rows):
    return lax.broadcasted_iota(jnp.int32, (rows, lanes), 1)


def swap(values):
    return pltpu.roll(values, half, 1)


def column(row):
    return jnp.transpose(jnp.broadcast_to(row, (lanes, row.shape[1])), (1, 0))


def to_rows(row):
    count = row.shape[1] // lanes
    pieces = [row[:, i * lanes : (i + 1) * lanes] for i in range(count)]
    return jnp.concatenate(pieces + [jnp.zeros((8 - count, lanes), f32)], axis=0)


def from_rows(block, count):
    return jnp.concatenate([block[i : i + 1] for i in range(count)], axis=1)


def wide(values, count):
    return jnp.concatenate([values] * count, axis=1)


def normalized(x):
    centred = x - jnp.mean(x, axis=-1, keepdims=True)
    inverse = lax.rsqrt(jnp.mean(centred * centred, axis=-1, keepdims=True) + epsilon)
    return centred * inverse, inverse


def normalized_back(upstream, unit, inverse, gain):
    scaled = upstream * gain
    inner = (
        scaled
        - jnp.mean(scaled, axis=-1, keepdims=True)
        - unit * jnp.mean(scaled * unit, axis=-1, keepdims=True)
    )
    grad_gain = jnp.sum(upstream * unit, axis=0, keepdims=True)
    return inverse * inner, grad_gain, jnp.sum(upstream, axis=0, keepdims=True)


def project_kernel(tok, wq, wkv, wroute, gain, shift, choice, seg, kvm, qm, n_out, gates, picks):
    rows = tok.shape[0]
    unit, _ = normalized(tok[...].astype(f32))
    normed = (unit * gain[...] + shift[...]).astype(bf16)
    n_out[...] = normed
    ids = to_rows(seg[...].astype(f32))
    ids = jnp.concatenate([ids, jnp.zeros((pad_rows - 8, lanes), f32)], axis=0).astype(bf16)
    kvm[0:rows, :] = nn(normed, wkv[...]).astype(bf16)
    kvm[rows : rows + pad_rows, :] = ids
    qm[rows : rows + pad_rows, :] = ids
    first = column(choice[0:1, :].astype(f32)).astype(jnp.int32)
    second = column(choice[1:2, :].astype(f32)).astype(jnp.int32)
    picks[0] = first
    picks[1] = second
    lane = lane_ids(rows)
    low = lane < half
    query_all = nn(normed, wq[...])
    pairs = query_all.shape[1] // lanes
    one = jnp.zeros((rows, lanes), f32)
    two = jnp.zeros((rows, lanes), f32)
    for g in range(pairs):
        part = query_all[:, g * lanes : (g + 1) * lanes]
        one = jnp.where(first // 2 == g, part, one)
        two = jnp.where(second // 2 == g, part, two)
    one = jnp.where(first % 2 == 0, one, swap(one))
    two = jnp.where(second % 2 == 1, two, swap(two))
    scale = half ** (-0.5)
    qm[0:rows, :] = (jnp.where(low, one, two).astype(bf16).astype(f32) * scale).astype(bf16)
    logits = nt(normed, wroute[...])
    experts = logits.shape[1]
    slot = lax.broadcasted_iota(jnp.int32, (rows, experts), 1)
    picked_one = jnp.sum(jnp.where(slot == first[:, :experts], logits, 0.0), axis=1, keepdims=True)
    picked_two = jnp.sum(jnp.where(slot == second[:, :experts], logits, 0.0), axis=1, keepdims=True)
    top = jnp.maximum(picked_one, picked_two)
    exp_one = jnp.exp(picked_one - top)
    exp_two = jnp.exp(picked_two - top)
    gates[...] = jnp.where(low, exp_one, exp_two) / (exp_one + exp_two)


def id_range(message, rows):
    block = message[rows : rows + pad_rows, :][0:8].astype(f32)
    count = rows // lanes
    keep = lax.broadcasted_iota(jnp.int32, (8, lanes), 0) < count
    return jnp.min(jnp.where(keep, block, 1e9)), jnp.max(jnp.where(keep, block, -1e9))


def id_row(message, rows):
    block = message[rows : rows + pad_rows, :][0:8].astype(f32)
    return from_rows(block, rows // lanes)


def stack_slots(packed, place):
    low = lane_ids(packed.shape[0]) < half
    other = swap(packed.astype(f32)).astype(packed.dtype)
    zero = jnp.zeros_like(packed)
    if place == 0:
        return jnp.where(low, packed, zero), jnp.where(low, other, zero)
    return jnp.where(low, zero, other), jnp.where(low, zero, packed)


def store_stack(ref, packed, place):
    rows = packed.shape[0]
    one, two = stack_slots(packed, place)
    for c in range(rows // chunk):
        ref[2 * c * chunk : (2 * c + 1) * chunk, :] = one[c * chunk : (c + 1) * chunk]
        ref[(2 * c + 1) * chunk : (2 * c + 2) * chunk, :] = two[c * chunk : (c + 1) * chunk]


def over_pieces(parts, rows, own, visit):
    own_low, own_high = id_range(own, rows)
    for index, part in enumerate(parts):
        count = part.shape[0]

        def one(i, index=index, part=part):
            message = part.at[i]
            low, high = id_range(message, rows)
            meets = (low <= own_high) & (high >= own_low)
            uniform = (low == high) & (own_low == own_high) & meets

            @pl.when(uniform)
            def _():
                visit(index, i, message, True)

            @pl.when(meets & jnp.logical_not(uniform))
            def _():
                visit(index, i, message, False)

        if count == 1:
            one(0)
        else:
            pl.loop(0, count)(one)


def forward_kernel(piece_count, qm, own, *rest):
    parts = rest[:piece_count]
    heads, lse, stack, peak, total, seg = rest[piece_count:]
    rows = qm.shape[0] - pad_rows
    chunks = rows // chunk
    store_stack(stack, qm[0:rows, :], 0)
    peak[...] = jnp.full(peak.shape, lowest, f32)
    total[...] = jnp.zeros(total.shape, f32)
    seg[...] = column(id_row(own, rows))

    def visit(index, i, message, uniform):
        kv = message[0:rows, :]
        low = lane_ids(rows) < half
        values = jnp.where(low, jnp.ones_like(kv), kv)
        if not uniform:
            key_ids = id_row(message, rows)

        @pl.loop(0, chunks)
        def _(c):
            at = pl.ds(pl.multiple_of(c * 2 * chunk, 2 * chunk), 2 * chunk)
            scores = nt(stack[at, :], kv)
            if not uniform:
                mine = seg[pl.ds(pl.multiple_of(c * chunk, chunk), chunk), :]
                allowed = wide(jnp.concatenate([mine, mine], axis=0), rows // lanes) == key_ids
                scores = jnp.where(allowed, scores, masked)
            before = peak[at, :]
            now = jnp.maximum(before, jnp.max(scores, axis=1, keepdims=True))
            peak[at, :] = now
            weights = jnp.exp(scores - wide(now, rows // lanes)).astype(bf16)
            total[at, :] = total[at, :] * jnp.exp(before - now) + nn(weights, values)

    over_pieces(parts, rows, own, visit)
    low = lane_ids(chunk) < half
    for c in range(chunks):
        one = total[2 * c * chunk : (2 * c + 1) * chunk, :]
        two = total[(2 * c + 1) * chunk : (2 * c + 2) * chunk, :]
        one_other, two_other = swap(one), swap(two)
        heads[c * chunk : (c + 1) * chunk, :] = jnp.where(low, one_other, two) / jnp.where(
            low, one, two_other
        )
        for j, (whole, other) in enumerate(((one, one_other), (two, two_other))):
            at = slice((2 * c + j) * chunk, (2 * c + j + 1) * chunk)
            lse[at, :] = peak[at, :] + jnp.log(jnp.where(low, whole, other))


def query_back_kernel(
    piece_count, qm, dom, lse, delta, normed, picks, wq, dlog, wroute, own, *rest
):
    parts = rest[:piece_count]
    grad_wq, grad_n, stack, stack_do, total, seg = rest[piece_count:]
    rows = qm.shape[0] - pad_rows
    chunks = rows // chunk
    store_stack(stack, qm[0:rows, :], 0)
    store_stack(stack_do, dom[0:rows, :], 1)
    total[...] = jnp.zeros(total.shape, f32)
    seg[...] = column(id_row(own, rows))
    across = rows // lanes

    def visit(index, i, message, uniform):
        kv = message[0:rows, :]
        if not uniform:
            key_ids = id_row(message, rows)

        @pl.loop(0, chunks)
        def _(c):
            at = pl.ds(pl.multiple_of(c * 2 * chunk, 2 * chunk), 2 * chunk)
            scores = nt(stack[at, :], kv) - wide(lse[at, :], across)
            if not uniform:
                mine = seg[pl.ds(pl.multiple_of(c * chunk, chunk), chunk), :]
                allowed = wide(jnp.concatenate([mine, mine], axis=0), across) == key_ids
                scores = jnp.where(allowed, scores, masked)
            prob = jnp.exp(scores)
            grad_prob = nt(stack_do[at, :], kv) - wide(delta[at, :], across)
            total[at, :] += nn((prob * grad_prob).astype(bf16), kv)

    over_pieces(parts, rows, own, visit)
    low = lane_ids(rows) < half
    first = picks[0]
    second = picks[1]
    one = jnp.concatenate(
        [total[2 * c * chunk : (2 * c + 1) * chunk, :] for c in range(chunks)], axis=0
    )
    two = jnp.concatenate(
        [total[(2 * c + 1) * chunk : (2 * c + 2) * chunk, :] for c in range(chunks)], axis=0
    )
    scale = half ** (-0.5)
    one = jnp.where(low, one, swap(one)) * scale
    two = jnp.where(low, two, swap(two)) * scale
    spread = spread_slots(one, two, first, second, normed.shape[1] // lanes).astype(bf16)
    grad_wq[...] = tn(normed[...], spread).astype(bf16)
    grad_n[...] = nt(spread, wq[...]) + nn(dlog[...], wroute[...])


def spread_slots(one, two, first, second, pairs):
    upper = (lane_ids(one.shape[0]) >= half).astype(jnp.int32)
    out = []
    for g in range(pairs):
        expert = 2 * g + upper
        out.append(jnp.where(first == expert, one, jnp.where(second == expert, two, 0.0)))
    return jnp.concatenate(out, axis=1)


def key_back_kernel(piece_count, own, *rest):
    q_parts = rest[:piece_count]
    do_parts = rest[piece_count : 2 * piece_count]
    grad_kv, keys, values, total_k, total_v, seg = rest[2 * piece_count :]
    rows = own.shape[0] - pad_rows
    chunks = rows // chunk
    across = rows // lanes
    kv = own[0:rows, :]
    low = lane_ids(rows) < half
    other = swap(kv.astype(f32)).astype(bf16)
    zero = jnp.zeros_like(kv)
    pairs = ((jnp.where(low, kv, zero), jnp.where(low, zero, other)), (jnp.where(low, other, zero), jnp.where(low, zero, kv)))
    for ref, (one, two) in ((keys, pairs[0]), (values, pairs[1])):
        for c in range(chunks):
            ref[2 * c * chunk : (2 * c + 1) * chunk, :] = one[c * chunk : (c + 1) * chunk]
            ref[(2 * c + 1) * chunk : (2 * c + 2) * chunk, :] = two[c * chunk : (c + 1) * chunk]
    total_k[...] = jnp.zeros(total_k.shape, f32)
    total_v[...] = jnp.zeros(total_v.shape, f32)
    seg[...] = column(id_row(own, rows))

    def visit(index, i, message, uniform):
        queries = message[0:rows, :]
        sent = do_parts[index].at[i]
        grads = sent[0:rows, :]
        stats = sent[rows : rows + stat_rows, :].astype(f32)

        def stat(first, terms):
            block = stats[first * 8 : first * 8 + 8]
            for t in range(1, terms):
                block = block + stats[(first + t) * 8 : (first + t) * 8 + 8]
            return from_rows(block, across)

        lse = (stat(0, 3), stat(3, 3))
        delta = (stat(6, 2), stat(8, 2))
        if not uniform:
            query_ids = id_row(message, rows)

        def spread(pair):
            return jnp.concatenate(
                [jnp.broadcast_to(pair[0], (chunk, rows)), jnp.broadcast_to(pair[1], (chunk, rows))],
                axis=0,
            )

        @pl.loop(0, chunks)
        def _(c):
            at = pl.ds(pl.multiple_of(c * 2 * chunk, 2 * chunk), 2 * chunk)
            scores = nt(keys[at, :], queries) - spread(lse)
            if not uniform:
                mine = seg[pl.ds(pl.multiple_of(c * chunk, chunk), chunk), :]
                allowed = wide(jnp.concatenate([mine, mine], axis=0), across) == query_ids
                scores = jnp.where(allowed, scores, masked)
            prob = jnp.exp(scores)
            grad_prob = nt(values[at, :], grads) - spread(delta)
            total_v[at, :] += nn(prob.astype(bf16), grads)
            total_k[at, :] += nn((prob * grad_prob).astype(bf16), queries)

    over_pieces(q_parts, rows, own, visit)
    low = lane_ids(chunk) < half
    for c in range(chunks):
        one = slice(2 * c * chunk, (2 * c + 1) * chunk)
        two = slice((2 * c + 1) * chunk, (2 * c + 2) * chunk)
        key_one, key_two = total_k[one, :], total_k[two, :]
        value_one, value_two = total_v[one, :], total_v[two, :]
        grad_kv[c * chunk : (c + 1) * chunk, :] = jnp.where(
            low, key_one + swap(key_two), swap(value_one) + value_two
        ).astype(bf16)


def middle_kernel(
    tok, cot, heads, gates, picks, lse, normed, wout, wup, bup, wdown, bdown, gain, shift,
    layer_out, grad_up, grad_down, grad_out, grad_mid, dom, delta_out, dlog, grad_route,
    grad_bup, grad_small,
    second_n, second_t, total_y, total_n, mid_keep, mixed_keep,
):
    rows = tok.shape[0]
    width = tok.shape[1]
    lane = lane_ids(rows)
    low = lane < half
    first = picks[0]
    second = picks[1]
    gated = gates[...] * heads[...]
    turned = swap(gated)
    pairs = width // lanes
    mixed = spread_slots(
        jnp.where(low, gated, turned), jnp.where(low, turned, gated), first, second, pairs
    ).astype(bf16)
    mixed_keep[...] = mixed
    middle = tok[...].astype(f32) + nn(mixed, wout[...])
    mid_keep[...] = middle
    unit, _ = normalized(middle)
    n_two = (unit * gain[...] + shift[...]).astype(bf16)
    second_n[...] = n_two
    second_t[...] = n_two.T
    total_y[...] = jnp.zeros(total_y.shape, f32)
    total_n[...] = jnp.zeros(total_n.shape, f32)
    step = 256
    hidden = wup.shape[1]
    root = 0.7978845608028654
    cubic = 0.044715

    @pl.loop(0, hidden // step)
    def _(f):
        at = pl.ds(pl.multiple_of(f * step, step), step)
        up = wup[:, at]
        down = wdown[at, :]
        dy = cot[...]
        pre = nn(second_n[...], up) + bup[:, at]
        square = pre * pre
        bent = jnp.tanh(root * (pre + cubic * (square * pre)))
        act = (0.5 * pre * (1.0 + bent)).astype(bf16)
        slope = 0.5 * (1.0 + bent) + (0.5 * root) * pre * (1.0 - bent * bent) * (
            1.0 + (3.0 * cubic) * square
        )
        total_y[...] += nn(act, down)
        grad_down[at, :] = tn(act, dy).astype(bf16)
        grad_pre = (nt(dy, down) * slope).astype(bf16)
        grad_bup[:, at] = jnp.sum(grad_pre.astype(f32), axis=0, keepdims=True)
        grad_up[:, at] = nn(second_t[...], grad_pre).astype(bf16)
        total_n[...] += nt(grad_pre, up)

    middle = mid_keep[...]
    layer_out[...] = (middle + total_y[...] + bdown[...]).astype(bf16)
    unit, inverse = normalized(middle)
    back, grad_gain, grad_shift = normalized_back(total_n[...], unit, inverse, gain[...])
    dy = cot[...].astype(f32)
    grad_middle = dy + back
    grad_mid[...] = grad_middle
    grad_small[0:1, :] = jnp.sum(dy, axis=0, keepdims=True)
    grad_small[1:2, :] = grad_gain
    grad_small[2:3, :] = grad_shift
    grad_small[3:8, :] = jnp.zeros((5, width), f32)
    grad_low = grad_middle.astype(bf16)
    grad_out[...] = tn(mixed_keep[...], grad_low).astype(bf16)
    grad_mixed = nt(grad_low, wout[...])
    one = jnp.zeros((rows, lanes), f32)
    two = jnp.zeros((rows, lanes), f32)
    for g in range(pairs):
        part = grad_mixed[:, g * lanes : (g + 1) * lanes]
        one = jnp.where(first // 2 == g, part, one)
        two = jnp.where(second // 2 == g, part, two)
    one = jnp.where(first % 2 == 0, one, swap(one))
    two = jnp.where(second % 2 == 1, two, swap(two))
    slots = jnp.where(low, one, two)
    head_values = heads[...]
    gate = gates[...]
    grad_heads = (gate * slots).astype(bf16)
    dom[0:rows, :] = grad_heads
    gated_grad = slots * head_values
    gate_one = jnp.sum(jnp.where(low, gated_grad, 0.0), axis=1, keepdims=True)
    gate_two = jnp.sum(jnp.where(low, 0.0, gated_grad), axis=1, keepdims=True)
    grad_gate = jnp.where(low, gate_one, gate_two)
    weighted = gate * grad_gate
    mean_grad = weighted + swap(weighted)
    grad_logit = gate * (grad_gate - mean_grad)
    logit_other = swap(grad_logit)
    logit_one = jnp.where(low, grad_logit, logit_other)
    logit_two = jnp.where(low, logit_other, grad_logit)
    grad_logits = jnp.where(
        lane == first, logit_one, jnp.where(lane == second, logit_two, 0.0)
    ).astype(bf16)
    experts = dlog.shape[1]
    dlog[...] = grad_logits[:, :experts]
    grad_route[...] = tn(grad_logits, normed[...])[:experts, :]
    carried = grad_heads.astype(f32) * head_values
    deltas = (
        jnp.sum(jnp.where(low, carried, 0.0), axis=1, keepdims=True),
        jnp.sum(jnp.where(low, 0.0, carried), axis=1, keepdims=True),
    )
    terms = []
    for j in range(2):
        wide_delta = jnp.broadcast_to(deltas[j], (rows, lanes))
        parts = []
        for c in range(rows // chunk):
            at = slice((2 * c + j) * chunk, (2 * c + j + 1) * chunk)
            delta_out[at, :] = wide_delta[c * chunk : (c + 1) * chunk]
            parts.append(lse[at, :])
        terms.append((split(row_of(jnp.concatenate(parts, axis=0)), 3), split(row_of(wide_delta), 2)))
    blocks = terms[0][0] + terms[1][0] + terms[0][1] + terms[1][1]
    dom[rows : rows + stat_rows, :] = jnp.concatenate(
        [to_rows(b) for b in blocks], axis=0
    ).astype(bf16)


def row_of(replicated):
    return jnp.transpose(replicated, (1, 0))[0:1, :]


def split(row, terms):
    out = []
    for _ in range(terms):
        part = row.astype(bf16).astype(f32)
        out.append(part)
        row = row - part
    return out


def final_kernel(tok, normed, grad_n, grad_kv, grad_mid, wkv, gain, grad_tokens, grad_wkv, small):
    width = tok.shape[1]
    low = grad_kv[...]
    grad_wkv[...] = tn(normed[...], low)
    upstream = grad_n[...] + nt(low, wkv[...])
    unit, inverse = normalized(tok[...].astype(f32))
    back, grad_gain, grad_shift = normalized_back(upstream, unit, inverse, gain[...])
    grad_tokens[...] = grad_mid[...] + back
    small[0:1, :] = grad_gain
    small[1:2, :] = grad_shift
    small[2:8, :] = jnp.zeros((6, width), f32)


def call(kernel, out_shape, scratch, limit, flops, *operands):
    moved = sum(x.size * x.dtype.itemsize for x in operands)
    whole = pl.BlockSpec(memory_space=pltpu.VMEM)
    return pl.pallas_call(
        kernel,
        out_shape=out_shape,
        in_specs=[whole] * len(operands),
        out_specs=jax.tree.map(lambda _: whole, out_shape),
        scratch_shapes=scratch,
        compiler_params=pltpu.CompilerParams(vmem_limit_bytes=limit),
        cost_estimate=pl.CostEstimate(flops=flops, bytes_accessed=moved, transcendentals=0),
    )(*operands)


def shape(dims, dtype):
    return jax.ShapeDtypeStruct(tuple(dims), dtype)


def gather(message, size):
    if size > 16:
        return [lax.all_gather(message, "seq", axis=0, tiled=False)]
    parts = [message[None]]
    for offset in range(1, size):
        if size & (size - 1) == 0:
            pairs = [(i, i ^ offset) for i in range(size)]
        else:
            pairs = [(i, (i + offset) % size) for i in range(size)]
        parts.append(lax.ppermute(message, "seq", pairs)[None])
    return parts


def local(
    tokens, cotangent, w_query, w_kv, w_route, w_out, w_up, bias_up, w_down, bias_down,
    gain_one, shift_one, gain_two, shift_two, choices, segment_ids,
):
    size = lax.axis_size("seq")
    tok, cot = tokens[0], cotangent[0]
    rows, width = tok.shape
    hidden = w_up.shape[1]
    route = w_route.T
    experts = route.shape[0]
    row = lambda v: v.reshape(1, -1)
    message = shape((rows + pad_rows, lanes), bf16)
    kvm, qm, normed, gates, picks = call(
        project_kernel,
        (message, message, shape((rows, width), bf16), shape((rows, lanes), f32), shape((2, rows, lanes), jnp.int32)),
        [], 32 * mib, 2 * rows * width * (width + lanes),
        tok, w_query, w_kv, route, row(gain_one), row(shift_one), choices[0].T, segment_ids,
    )
    kv_parts = gather(kvm, size)
    q_parts = gather(qm, size)
    count = len(kv_parts)
    stacked = (2 * rows, lanes)
    attention_flops = 2 * 2 * rows * rows * size * lanes
    heads, lse = call(
        functools.partial(forward_kernel, count),
        (shape((rows, lanes), f32), shape(stacked, f32)),
        [pltpu.VMEM(stacked, bf16), pltpu.VMEM(stacked, f32), pltpu.VMEM(stacked, f32), pltpu.VMEM((rows, lanes), f32)],
        40 * mib, 2 * attention_flops,
        qm, kvm, *kv_parts,
    )
    (
        layer_out, grad_up, grad_down, grad_out, grad_mid, dom, delta, dlog, grad_route, grad_bup, small_two,
    ) = call(
        middle_kernel,
        (
            shape((rows, width), bf16), shape((width, hidden), bf16), shape((hidden, width), bf16),
            shape((width, width), bf16), shape((rows, width), f32), shape((rows + stat_rows, lanes), bf16),
            shape(stacked, f32), shape((rows, experts), bf16), shape((experts, width), f32),
            shape((1, hidden), f32), shape((8, width), f32),
        ),
        [
            pltpu.VMEM((rows, width), bf16), pltpu.VMEM((width, rows), bf16), pltpu.VMEM((rows, width), f32),
            pltpu.VMEM((rows, width), f32), pltpu.VMEM((rows, width), f32), pltpu.VMEM((rows, width), bf16),
        ],
        56 * mib, 12 * rows * width * hidden,
        tok, cot, heads, gates, picks, lse, normed, w_out, w_up, row(bias_up), w_down, row(bias_down),
        row(gain_two), row(shift_two),
    )
    grad_up, grad_down, grad_out = lax.psum((grad_up, grad_down, grad_out), ("seq", "row"))
    do_parts = gather(dom, size)
    grad_wq, grad_n = call(
        functools.partial(query_back_kernel, count),
        (shape((width, width), bf16), shape((rows, width), f32)),
        [pltpu.VMEM(stacked, bf16), pltpu.VMEM(stacked, bf16), pltpu.VMEM(stacked, f32), pltpu.VMEM((rows, lanes), f32)],
        40 * mib, 3 * attention_flops,
        qm, dom, lse, delta, normed, picks, w_query, dlog, route, kvm, *kv_parts,
    )
    grad_kv = call(
        functools.partial(key_back_kernel, count),
        shape((rows, lanes), bf16),
        [
            pltpu.VMEM(stacked, bf16), pltpu.VMEM(stacked, bf16), pltpu.VMEM(stacked, f32),
            pltpu.VMEM(stacked, f32), pltpu.VMEM((rows, lanes), f32),
        ],
        56 * mib, 4 * attention_flops,
        kvm, *q_parts, *do_parts,
    )
    grad_tokens, grad_wkv, small_one = call(
        final_kernel,
        (shape((rows, width), f32), shape((width, lanes), f32), shape((8, width), f32)),
        [], 32 * mib, 4 * rows * width * lanes,
        tok, normed, grad_n, grad_kv, grad_mid, w_kv, row(gain_one),
    )
    grad_wq, grad_wkv, grad_route, grad_bup, small_two, small_one = lax.psum(
        (grad_wq.astype(f32), grad_wkv, grad_route, grad_bup, small_two, small_one), ("seq", "row")
    )
    return (
        layer_out[None],
        grad_tokens[None],
        grad_wq,
        grad_wkv,
        grad_route.T,
        grad_out.astype(f32),
        grad_up.astype(f32),
        grad_bup.reshape(-1),
        grad_down.astype(f32),
        small_two[0],
        small_one[0],
        small_one[1],
        small_two[1],
        small_two[2],
    )


def solution(mesh):
    split_tokens = P("row", "seq", None)
    placed = (split_tokens, split_tokens) + (P(),) * 12 + (split_tokens, P("row", "seq"))
    return jax.shard_map(
        local,
        mesh=mesh,
        in_specs=placed,
        out_specs=(split_tokens, split_tokens) + (P(),) * 12,
        check_vma=False,
    )
```

```python
import functools

import jax
import jax.numpy as jnp
from jax import lax
from jax.experimental import pallas as pl
from jax.experimental.pallas import tpu as pltpu
from jax.sharding import PartitionSpec as P

f32 = jnp.float32
bf16 = jnp.bfloat16
epsilon = 1e-05
lanes = 128
half = 64
chunk = 128
pad_rows = 16
stat_rows = 80
masked = -2e30
lowest = -1e30
mib = 1 << 20


def nn(a, b):
    return lax.dot_general(a, b, (((1,), (0,)), ((), ())), preferred_element_type=f32)


def nt(a, b):
    return lax.dot_general(a, b, (((1,), (1,)), ((), ())), preferred_element_type=f32)


def tn(a, b):
    return lax.dot_general(a, b, (((0,), (0,)), ((), ())), preferred_element_type=f32)


def lane_ids(rows):
    return lax.broadcasted_iota(jnp.int32, (rows, lanes), 1)


def swap(values):
    return pltpu.roll(values, half, 1)


def column(row):
    return jnp.transpose(jnp.broadcast_to(row, (lanes, row.shape[1])), (1, 0))


def to_rows(row):
    count = row.shape[1] // lanes
    pieces = [row[:, i * lanes : (i + 1) * lanes] for i in range(count)]
    return jnp.concatenate(pieces + [jnp.zeros((8 - count, lanes), f32)], axis=0)


def from_rows(block, count):
    return jnp.concatenate([block[i : i + 1] for i in range(count)], axis=1)


def wide(values, count):
    return jnp.concatenate([values] * count, axis=1)


def normalized(x):
    centred = x - jnp.mean(x, axis=-1, keepdims=True)
    inverse = lax.rsqrt(jnp.mean(centred * centred, axis=-1, keepdims=True) + epsilon)
    return centred * inverse, inverse


def normalized_back(upstream, unit, inverse, gain):
    scaled = upstream * gain
    inner = (
        scaled
        - jnp.mean(scaled, axis=-1, keepdims=True)
        - unit * jnp.mean(scaled * unit, axis=-1, keepdims=True)
    )
    grad_gain = jnp.sum(upstream * unit, axis=0, keepdims=True)
    return inverse * inner, grad_gain, jnp.sum(upstream, axis=0, keepdims=True)


def project_kernel(tok, wq, wkv, wroute, gain, shift, choice, seg, kvm, qm, n_out, gates, picks):
    rows = tok.shape[0]
    unit, _ = normalized(tok[...].astype(f32))
    normed = (unit * gain[...] + shift[...]).astype(bf16)
    n_out[...] = normed
    ids = to_rows(seg[...].astype(f32))
    ids = jnp.concatenate([ids, jnp.zeros((pad_rows - 8, lanes), f32)], axis=0).astype(bf16)
    kvm[0:rows, :] = nn(normed, wkv[...]).astype(bf16)
    kvm[rows : rows + pad_rows, :] = ids
    qm[rows : rows + pad_rows, :] = ids
    first = column(choice[0:1, :].astype(f32)).astype(jnp.int32)
    second = column(choice[1:2, :].astype(f32)).astype(jnp.int32)
    picks[0] = first
    picks[1] = second
    lane = lane_ids(rows)
    low = lane < half
    query_all = nn(normed, wq[...])
    pairs = query_all.shape[1] // lanes
    one = jnp.zeros((rows, lanes), f32)
    two = jnp.zeros((rows, lanes), f32)
    for g in range(pairs):
        part = query_all[:, g * lanes : (g + 1) * lanes]
        one = jnp.where(first // 2 == g, part, one)
        two = jnp.where(second // 2 == g, part, two)
    one = jnp.where(first % 2 == 0, one, swap(one))
    two = jnp.where(second % 2 == 1, two, swap(two))
    scale = half ** (-0.5)
    qm[0:rows, :] = (jnp.where(low, one, two).astype(bf16).astype(f32) * scale).astype(bf16)
    logits = nt(normed, wroute[...])
    experts = logits.shape[1]
    slot = lax.broadcasted_iota(jnp.int32, (rows, experts), 1)
    picked_one = jnp.sum(jnp.where(slot == first[:, :experts], logits, 0.0), axis=1, keepdims=True)
    picked_two = jnp.sum(jnp.where(slot == second[:, :experts], logits, 0.0), axis=1, keepdims=True)
    top = jnp.maximum(picked_one, picked_two)
    exp_one = jnp.exp(picked_one - top)
    exp_two = jnp.exp(picked_two - top)
    gates[...] = jnp.where(low, exp_one, exp_two) / (exp_one + exp_two)


def id_range(message, rows):
    block = message[rows : rows + pad_rows, :][0:8].astype(f32)
    count = rows // lanes
    keep = lax.broadcasted_iota(jnp.int32, (8, lanes), 0) < count
    return jnp.min(jnp.where(keep, block, 1e9)), jnp.max(jnp.where(keep, block, -1e9))


def id_row(message, rows):
    block = message[rows : rows + pad_rows, :][0:8].astype(f32)
    return from_rows(block, rows // lanes)


def stack_slots(packed, place):
    low = lane_ids(packed.shape[0]) < half
    other = swap(packed.astype(f32)).astype(packed.dtype)
    zero = jnp.zeros_like(packed)
    if place == 0:
        return jnp.where(low, packed, zero), jnp.where(low, other, zero)
    return jnp.where(low, zero, other), jnp.where(low, zero, packed)


def store_stack(ref, packed, place):
    rows = packed.shape[0]
    one, two = stack_slots(packed, place)
    for c in range(rows // chunk):
        ref[2 * c * chunk : (2 * c + 1) * chunk, :] = one[c * chunk : (c + 1) * chunk]
        ref[(2 * c + 1) * chunk : (2 * c + 2) * chunk, :] = two[c * chunk : (c + 1) * chunk]


def over_pieces(parts, rows, own, visit):
    own_low, own_high = id_range(own, rows)
    for index, part in enumerate(parts):
        count = part.shape[0]

        def one(i, index=index, part=part):
            message = part.at[i]
            low, high = id_range(message, rows)
            meets = (low <= own_high) & (high >= own_low)
            uniform = (low == high) & (own_low == own_high) & meets

            @pl.when(uniform)
            def _():
                visit(index, i, message, True)

            @pl.when(meets & jnp.logical_not(uniform))
            def _():
                visit(index, i, message, False)

        if count == 1:
            one(0)
        else:
            pl.loop(0, count)(one)


def forward_kernel(piece_count, first, last, qm, own, *rest):
    parts = rest[:piece_count]
    rest = rest[piece_count:]
    if not first:
        total_in, peak_in = rest[:2]
        rest = rest[2:]
    if last:
        heads, lse, total, peak, stack, seg = rest
    else:
        total, peak, stack, seg = rest
    rows = qm.shape[0] - pad_rows
    chunks = rows // chunk
    across = rows // lanes
    store_stack(stack, qm[0:rows, :], 0)
    if first:
        peak[...] = jnp.full(peak.shape, lowest, f32)
        total[...] = jnp.zeros(total.shape, f32)
    else:
        peak[...] = peak_in[...]
        total[...] = total_in[...]
    seg[...] = column(id_row(own, rows))

    def visit(index, i, message, uniform):
        kv = message[0:rows, :]
        low = lane_ids(rows) < half
        values = jnp.where(low, jnp.ones_like(kv), kv)
        if not uniform:
            key_ids = id_row(message, rows)

        @pl.loop(0, chunks)
        def _(c):
            at = pl.ds(pl.multiple_of(c * 2 * chunk, 2 * chunk), 2 * chunk)
            scores = nt(stack[at, :], kv)
            if not uniform:
                mine = seg[pl.ds(pl.multiple_of(c * chunk, chunk), chunk), :]
                allowed = wide(jnp.concatenate([mine, mine], axis=0), across) == key_ids
                scores = jnp.where(allowed, scores, masked)
            before = peak[at, :]
            now = jnp.maximum(before, jnp.max(scores, axis=1, keepdims=True))
            peak[at, :] = now
            weights = jnp.exp(scores - wide(now, across)).astype(bf16)
            total[at, :] = total[at, :] * jnp.exp(before - now) + nn(weights, values)

    over_pieces(parts, rows, own, visit)
    if not last:
        return
    low = lane_ids(chunk) < half
    for c in range(chunks):
        one = total[2 * c * chunk : (2 * c + 1) * chunk, :]
        two = total[(2 * c + 1) * chunk : (2 * c + 2) * chunk, :]
        one_other, two_other = swap(one), swap(two)
        heads[c * chunk : (c + 1) * chunk, :] = jnp.where(low, one_other, two) / jnp.where(
            low, one, two_other
        )
        for j, (whole, other) in enumerate(((one, one_other), (two, two_other))):
            at = slice((2 * c + j) * chunk, (2 * c + j + 1) * chunk)
            lse[at, :] = peak[at, :] + jnp.log(jnp.where(low, whole, other))


def query_back_kernel(spread_out, piece_count, first, last, qm, dom, lse, delta, own, *rest):
    parts = rest[:piece_count]
    rest = rest[piece_count:]
    if not first:
        total_in = rest[0]
        rest = rest[1:]
    if last:
        normed, picks, wq, dlog, wroute, keep, send, grad_n, total, stack, stack_do, seg = rest
    else:
        total, stack, stack_do, seg = rest
    rows = qm.shape[0] - pad_rows
    chunks = rows // chunk
    store_stack(stack, qm[0:rows, :], 0)
    store_stack(stack_do, dom[0:rows, :], 1)
    total[...] = jnp.zeros(total.shape, f32) if first else total_in[...]
    seg[...] = column(id_row(own, rows))
    across = rows // lanes

    def visit(index, i, message, uniform):
        kv = message[0:rows, :]
        if not uniform:
            key_ids = id_row(message, rows)

        @pl.loop(0, chunks)
        def _(c):
            at = pl.ds(pl.multiple_of(c * 2 * chunk, 2 * chunk), 2 * chunk)
            scores = nt(stack[at, :], kv) - wide(lse[at, :], across)
            if not uniform:
                mine = seg[pl.ds(pl.multiple_of(c * chunk, chunk), chunk), :]
                allowed = wide(jnp.concatenate([mine, mine], axis=0), across) == key_ids
                scores = jnp.where(allowed, scores, masked)
            prob = jnp.exp(scores)
            grad_prob = nt(stack_do[at, :], kv) - wide(delta[at, :], across)
            total[at, :] += nn((prob * grad_prob).astype(bf16), kv)

    over_pieces(parts, rows, own, visit)
    if not last:
        return
    low = lane_ids(rows) < half
    first_pick = picks[0]
    second_pick = picks[1]
    one = jnp.concatenate(
        [total[2 * c * chunk : (2 * c + 1) * chunk, :] for c in range(chunks)], axis=0
    )
    two = jnp.concatenate(
        [total[(2 * c + 1) * chunk : (2 * c + 2) * chunk, :] for c in range(chunks)], axis=0
    )
    scale = half ** (-0.5)
    one = jnp.where(low, one, swap(one)) * scale
    two = jnp.where(low, two, swap(two)) * scale
    spread = spread_slots(one, two, first_pick, second_pick, normed.shape[1] // lanes).astype(bf16)
    whole = tn(normed[...], spread).astype(bf16)
    core = place(spread_out)[0]
    middle = whole.shape[1] // 2
    count = whole.shape[0] // parts_of
    for i in range(parts_of):
        for side in range(2):
            at = slice(((i // 2) * 2 + side) * count, ((i // 2) * 2 + side + 1) * count)
            value = whole[i * count : (i + 1) * count, side * middle : (side + 1) * middle]
            if spread_out:

                @pl.when(core == i % 2)
                def _(at=at, value=value):
                    keep[at, :] = value

                @pl.when(core != i % 2)
                def _(at=at, value=value):
                    send[at, :] = value
            else:
                (keep, send)[i % 2][at, :] = value
    grad_n[...] = nt(spread, wq[...]) + nn(dlog[...], wroute[...])


def spread_slots(one, two, first, second, pairs):
    upper = (lane_ids(one.shape[0]) >= half).astype(jnp.int32)
    out = []
    for g in range(pairs):
        expert = 2 * g + upper
        out.append(jnp.where(first == expert, one, jnp.where(second == expert, two, 0.0)))
    return jnp.concatenate(out, axis=1)


def key_back_kernel(piece_count, first, last, own, *rest):
    q_parts = rest[:piece_count]
    do_parts = rest[piece_count : 2 * piece_count]
    rest = rest[2 * piece_count :]
    if not first:
        k_in, v_in = rest[:2]
        rest = rest[2:]
    if last:
        grad_kv = rest[0]
        rest = rest[1:]
    total_k, total_v, keys, values, seg = rest
    rows = own.shape[0] - pad_rows
    chunks = rows // chunk
    across = rows // lanes
    kv = own[0:rows, :]
    store_stack_other(keys, kv, 0)
    store_stack_other(values, kv, 1)
    if first:
        total_k[...] = jnp.zeros(total_k.shape, f32)
        total_v[...] = jnp.zeros(total_v.shape, f32)
    else:
        total_k[...] = k_in[...]
        total_v[...] = v_in[...]
    seg[...] = column(id_row(own, rows))

    def visit(index, i, message, uniform):
        queries = message[0:rows, :]
        sent = do_parts[index].at[i]
        grads = sent[0:rows, :]
        stats = sent[rows : rows + stat_rows, :].astype(f32)

        def stat(first, terms):
            block = stats[first * 8 : first * 8 + 8]
            for t in range(1, terms):
                block = block + stats[(first + t) * 8 : (first + t) * 8 + 8]
            return from_rows(block, across)

        lse = (stat(0, 3), stat(3, 3))
        delta = (stat(6, 2), stat(8, 2))
        if not uniform:
            query_ids = id_row(message, rows)

        def spread(pair):
            return jnp.concatenate(
                [jnp.broadcast_to(pair[0], (chunk, rows)), jnp.broadcast_to(pair[1], (chunk, rows))],
                axis=0,
            )

        @pl.loop(0, chunks)
        def _(c):
            at = pl.ds(pl.multiple_of(c * 2 * chunk, 2 * chunk), 2 * chunk)
            scores = nt(keys[at, :], queries) - spread(lse)
            if not uniform:
                mine = seg[pl.ds(pl.multiple_of(c * chunk, chunk), chunk), :]
                allowed = wide(jnp.concatenate([mine, mine], axis=0), across) == query_ids
                scores = jnp.where(allowed, scores, masked)
            prob = jnp.exp(scores)
            grad_prob = nt(values[at, :], grads) - spread(delta)
            total_v[at, :] += nn(prob.astype(bf16), grads)
            total_k[at, :] += nn((prob * grad_prob).astype(bf16), queries)

    over_pieces(q_parts, rows, own, visit)
    if not last:
        return
    low = lane_ids(chunk) < half
    for c in range(chunks):
        one = slice(2 * c * chunk, (2 * c + 1) * chunk)
        two = slice((2 * c + 1) * chunk, (2 * c + 2) * chunk)
        key_one, key_two = total_k[one, :], total_k[two, :]
        value_one, value_two = total_v[one, :], total_v[two, :]
        grad_kv[c * chunk : (c + 1) * chunk, :] = jnp.where(
            low, key_one + swap(key_two), swap(value_one) + value_two
        ).astype(bf16)


def store_stack_other(ref, kv, part):
    rows = kv.shape[0]
    low = lane_ids(rows) < half
    other = swap(kv.astype(f32)).astype(bf16)
    zero = jnp.zeros_like(kv)
    one, two = jnp.where(low, (kv, other)[part], zero), jnp.where(low, zero, (other, kv)[part])
    for c in range(rows // chunk):
        ref[2 * c * chunk : (2 * c + 1) * chunk, :] = one[c * chunk : (c + 1) * chunk]
        ref[(2 * c + 1) * chunk : (2 * c + 2) * chunk, :] = two[c * chunk : (c + 1) * chunk]


def middle_kernel(
    spread_out,
    tok, cot, heads, gates, picks, lse, normed, wout, wup, bup, wdown, bdown, gain, shift,
    layer_out, keep, send, grad_mid, dom, delta_out, dlog, grad_route,
    grad_bup, grad_small,
    second_n, second_t, total_y, total_n, mid_keep, mixed_keep,
):
    rows = tok.shape[0]
    width = tok.shape[1]
    lane = lane_ids(rows)
    low = lane < half
    first = picks[0]
    second = picks[1]
    gated = gates[...] * heads[...]
    turned = swap(gated)
    pairs = width // lanes
    mixed = spread_slots(
        jnp.where(low, gated, turned), jnp.where(low, turned, gated), first, second, pairs
    ).astype(bf16)
    mixed_keep[...] = mixed
    middle = tok[...].astype(f32) + nn(mixed, wout[...])
    mid_keep[...] = middle
    unit, _ = normalized(middle)
    n_two = (unit * gain[...] + shift[...]).astype(bf16)
    second_n[...] = n_two
    second_t[...] = n_two.T
    total_y[...] = jnp.zeros(total_y.shape, f32)
    total_n[...] = jnp.zeros(total_n.shape, f32)
    step = 512
    hidden = wup.shape[1]
    root = 0.7978845608028654
    cubic = 0.044715
    core = place(spread_out)[0]
    down_rows = hidden // parts_of
    up_rows = width // parts_of
    piece = gradient_rows(width, hidden)

    def put(index, at_row, at_lane, even, odd):
        count, across = even.shape
        target = (pl.ds(index * piece + at_row, count), slice(at_lane, at_lane + across))
        keep[target] = jnp.where(core == 0, even, odd)
        send[target] = jnp.where(core == 0, odd, even)

    @pl.loop(0, hidden // step)
    def _(f):
        for sub in range(0, step, 256):
            at = pl.ds(pl.multiple_of(f * step + sub, 256), 256)
            up = wup[:, at]
            down = wdown[at, :]
            dy = cot[...]
            pre = nn(second_n[...], up) + bup[:, at]
            square = pre * pre
            bent = jnp.tanh(root * (pre + cubic * (square * pre)))
            act = (0.5 * pre * (1.0 + bent)).astype(bf16)
            slope = 0.5 * (1.0 + bent) + (0.5 * root) * pre * (1.0 - bent * bent) * (
                1.0 + (3.0 * cubic) * square
            )
            total_y[...] += nn(act, down)
            grad_down = tn(act, dy).astype(bf16)
            grad_pre = (nt(dy, down) * slope).astype(bf16)
            grad_bup[:, at] = jnp.sum(grad_pre.astype(f32), axis=0, keepdims=True)
            grad_up = nn(second_t[...], grad_pre).astype(bf16)
            total_n[...] += nt(grad_pre, up)
            for i in range(256 // (2 * down_rows)):
                pair = grad_down[2 * i * down_rows : 2 * (i + 1) * down_rows]
                index = f * (step // (2 * down_rows)) + sub // (2 * down_rows) + i
                put(index, 0, 0, pair[:down_rows], pair[down_rows:])
            for i in range(parts_of // 2):
                pair = grad_up[2 * i * up_rows : 2 * (i + 1) * up_rows]
                put(i, down_rows + f * up_rows, sub, pair[:up_rows], pair[up_rows:])

    middle = mid_keep[...]
    layer_out[...] = (middle + total_y[...] + bdown[...]).astype(bf16)
    unit, inverse = normalized(middle)
    back, grad_gain, grad_shift = normalized_back(total_n[...], unit, inverse, gain[...])
    dy = cot[...].astype(f32)
    grad_middle = dy + back
    grad_mid[...] = grad_middle
    grad_small[0:1, :] = jnp.sum(dy, axis=0, keepdims=True)
    grad_small[1:2, :] = grad_gain
    grad_small[2:3, :] = grad_shift
    grad_small[3:8, :] = jnp.zeros((5, width), f32)
    grad_low = grad_middle.astype(bf16)
    grad_out = tn(mixed_keep[...], grad_low).astype(bf16)
    for i in range(parts_of // 2):
        pair = grad_out[2 * i * up_rows : 2 * (i + 1) * up_rows]
        put(i, piece - up_rows, 0, pair[:up_rows], pair[up_rows:])
    grad_mixed = nt(grad_low, wout[...])
    one = jnp.zeros((rows, lanes), f32)
    two = jnp.zeros((rows, lanes), f32)
    for g in range(pairs):
        part = grad_mixed[:, g * lanes : (g + 1) * lanes]
        one = jnp.where(first // 2 == g, part, one)
        two = jnp.where(second // 2 == g, part, two)
    one = jnp.where(first % 2 == 0, one, swap(one))
    two = jnp.where(second % 2 == 1, two, swap(two))
    slots = jnp.where(low, one, two)
    head_values = heads[...]
    gate = gates[...]
    grad_heads = (gate * slots).astype(bf16)
    dom[0:rows, :] = grad_heads
    gated_grad = slots * head_values
    gate_one = jnp.sum(jnp.where(low, gated_grad, 0.0), axis=1, keepdims=True)
    gate_two = jnp.sum(jnp.where(low, 0.0, gated_grad), axis=1, keepdims=True)
    grad_gate = jnp.where(low, gate_one, gate_two)
    weighted = gate * grad_gate
    mean_grad = weighted + swap(weighted)
    grad_logit = gate * (grad_gate - mean_grad)
    logit_other = swap(grad_logit)
    logit_one = jnp.where(low, grad_logit, logit_other)
    logit_two = jnp.where(low, logit_other, grad_logit)
    grad_logits = jnp.where(
        lane == first, logit_one, jnp.where(lane == second, logit_two, 0.0)
    ).astype(bf16)
    experts = dlog.shape[1]
    dlog[...] = grad_logits[:, :experts]
    grad_route[...] = tn(grad_logits, normed[...])[:experts, :]
    carried = grad_heads.astype(f32) * head_values
    deltas = (
        jnp.sum(jnp.where(low, carried, 0.0), axis=1, keepdims=True),
        jnp.sum(jnp.where(low, 0.0, carried), axis=1, keepdims=True),
    )
    terms = []
    for j in range(2):
        wide_delta = jnp.broadcast_to(deltas[j], (rows, lanes))
        parts = []
        for c in range(rows // chunk):
            at = slice((2 * c + j) * chunk, (2 * c + j + 1) * chunk)
            delta_out[at, :] = wide_delta[c * chunk : (c + 1) * chunk]
            parts.append(lse[at, :])
        terms.append((split(row_of(jnp.concatenate(parts, axis=0)), 3), split(row_of(wide_delta), 2)))
    blocks = terms[0][0] + terms[1][0] + terms[0][1] + terms[1][1]
    dom[rows : rows + stat_rows, :] = jnp.concatenate(
        [to_rows(b) for b in blocks], axis=0
    ).astype(bf16)


def row_of(replicated):
    return jnp.transpose(replicated, (1, 0))[0:1, :]


def split(row, terms):
    out = []
    for _ in range(terms):
        part = row.astype(bf16).astype(f32)
        out.append(part)
        row = row - part
    return out


def final_kernel(
    spread_out, tok, normed, grad_n, grad_kv, grad_mid, wkv, gain, grad_route, grad_bup, small_two,
    grad_tokens, keep, send, whole,
):
    width = tok.shape[1]
    low = grad_kv[...]
    whole[0:width, :] = tn(normed[...], low).astype(bf16)
    upstream = grad_n[...] + nt(low, wkv[...])
    unit, inverse = normalized(tok[...].astype(f32))
    back, grad_gain, grad_shift = normalized_back(upstream, unit, inverse, gain[...])
    grad_tokens[...] = grad_mid[...] + back
    rows = [grad_gain, grad_shift] + [small_two[i : i + 1, :] for i in range(3)]
    rows += [grad_bup[:, i : i + width] for i in range(0, grad_bup.shape[1], width)]
    rows += [grad_route[i : i + 1, :] for i in range(grad_route.shape[0])]
    small = jnp.concatenate([row[:, i : i + lanes] for row in rows for i in range(0, width, lanes)], axis=0)
    last = whole.shape[0] - width
    small = jnp.concatenate([small, jnp.zeros((last - small.shape[0], lanes), f32)], axis=0)
    whole[width:, :] = small.astype(bf16)
    core = place(spread_out)[0]
    piece = keep.shape[0]
    keep[...] = whole[block(core, piece), :]
    send[...] = whole[block(1 - core, piece), :]


parts_of = 32


def place(spread_out):
    if not spread_out:
        return 0, 0, 0, 0
    row, seq = lax.axis_index("row"), lax.axis_index("seq")
    return lax.rem(row, 2), row // 2, lax.rem(seq, 2), seq // 2


def gradient_rows(width, hidden):
    return hidden // parts_of + (hidden // width + 1) * (width // parts_of)


def block(index, count):
    return pl.ds(pl.multiple_of(index * count, 16), count)


def plus(*refs):
    def get(at):
        total = refs[0][at].astype(f32)
        for ref in refs[1:]:
            total = total + ref[at].astype(f32)
        return total.astype(bf16)

    return get


def after_core_kernel(keep, received, one_keep, one_send, two_keep, two_send):
    _, x, y, _ = place(True)
    piece = keep.shape[0] // 16
    middle = keep.shape[1] // 2
    left, right = slice(0, middle), slice(middle, 2 * middle)
    total = plus(keep, received)
    for zy in range(8):
        here = slice(zy * piece, (zy + 1) * piece)
        one_keep[here, :] = total((block(zy * 2 + x, piece), left))
        one_send[here, :] = total((block(zy * 2 + 1 - x, piece), left))
    for z in range(4):
        for at_x in range(2):
            here = slice((z * 2 + at_x) * piece, (z * 2 + at_x + 1) * piece)
            two_keep[here, :] = total((block((z * 2 + y) * 2 + at_x, piece), right))
            two_send[here, :] = total((block((z * 2 + 1 - y) * 2 + at_x, piece), right))


def split_x_kernel(keep, received, kept, sent):
    x = place(True)[1]
    piece = keep.shape[0] // 16
    total = plus(keep, received)
    for zy in range(8):
        here = slice(zy * piece, (zy + 1) * piece)
        kept[here, :] = total((block(zy * 2 + x, piece), slice(None)))
        sent[here, :] = total((block(zy * 2 + 1 - x, piece), slice(None)))


def after_first_kernel(one, one_in, two, two_in, extra, extra_in, one_keep, one_send, two_keep, two_send):
    _, x, y, _ = place(True)
    for total, mine, kept, sent, piece, offset in (
        (plus(one, one_in), y, one_keep, one_send, one.shape[0] // 8, 0),
        (plus(extra, extra_in), y, one_keep, one_send, extra.shape[0] // 8, one.shape[0] // 8),
        (plus(two, two_in), x, two_keep, two_send, two.shape[0] // 8, 0),
    ):
        stride = kept.shape[0] // 4
        for z in range(4):
            here = slice(z * stride + offset, z * stride + offset + piece)
            kept[here, :] = total((block(z * 2 + mine, piece), slice(None)))
            sent[here, :] = total((block(z * 2 + 1 - mine, piece), slice(None)))


def after_second_kernel(one, one_in, two, two_in, *outs):
    z = place(True)[3]
    middle = one.shape[1]
    piece = two.shape[0] // 4
    stride = one.shape[0] // 4
    more = (stride - piece) // 2
    left, right = plus(one, one_in), plus(two, two_in)
    for i, out in enumerate(outs):
        base = (z ^ i) * stride

        def part(offset, count):
            return left((pl.ds(pl.multiple_of(base + offset, 16), count), slice(None)))

        out[:piece, :middle] = part(0, piece)
        out[:piece, middle:] = right((block(z ^ i, piece), slice(None)))
        out[piece:, :middle] = part(piece, more)
        out[piece:, middle:] = part(piece + more, more)


def sum_kernel(*refs):
    refs[-1][...] = plus(*refs[:-1])(Ellipsis)


def join_halves_kernel(*refs):
    z = place(True)[3]
    one, two = refs[4:]
    piece, wide_piece = refs[0].shape
    middle = wide_piece // 2
    for i in range(4):
        one[block(z ^ i, piece), :] = refs[i][:, :middle]
        two[block(z ^ i, piece), :] = refs[i][:, middle:]


def unpack_kernel(spread_out, *refs):
    core, x, y, _ = place(spread_out)
    grad_up, grad_down, grad_out, grad_wq = refs[8:]
    piece, middle = refs[0].shape[0] // 8, refs[0].shape[1]
    width, hidden = grad_up.shape
    down_rows, up_rows = hidden // parts_of, width // parts_of
    for turn in range(2):
        for outer in range(2):
            for side in range(2):
                ref = refs[turn * 4 + side * 2 + outer]
                for inner in range(2):
                    at_x, at_y = (x ^ outer, y ^ inner) if side == 0 else (x ^ inner, y ^ outer)
                    for z in range(4):
                        device = ((z * 2 + at_y) * 2 + at_x) * 2 + (core ^ turn)
                        base = (inner * 4 + z) * piece
                        lane = slice(side * middle, (side + 1) * middle)
                        grad_down[block(device, down_rows), lane] = ref[base : base + down_rows, :].astype(f32)
                        at = base + down_rows
                        target = block(device, up_rows)
                        for c in range(hidden // width):
                            lane_up = slice(c * width + side * middle, c * width + (side + 1) * middle)
                            grad_up[target, lane_up] = ref[at : at + up_rows, :].astype(f32)
                            at += up_rows
                        grad_out[target, lane] = ref[at : at + up_rows, :].astype(f32)
                        grad_wq[target, lane] = ref[at + up_rows : at + 2 * up_rows, :].astype(f32)


def flip_row(x, mask):
    return lax.ppermute(x, "row", [(i, i ^ mask) for i in range(4)])


def flip_seq(x, mask):
    return lax.ppermute(x, "seq", [(i, i ^ mask) for i in range(8)])


def simple(kernel, outs, *operands):
    return call(kernel, outs, [], 48 * mib, 0, *operands)


def add(a, b):
    return (a.astype(f32) + b.astype(f32)).astype(bf16)


def finish_sums(large, small):
    mine, arrived = large
    keep, send = small
    count, width = mine.shape
    total = add(keep, flip_row(send, 1))
    total = add(total, flip_row(total, 2))
    arrived[0] = after(arrived[0], total)
    part = shape((4 * count, width // 2), bf16)
    one, two = simple(join_halves_kernel, (part,) * 2, mine, *arrived)
    one_in, two_in = flip_seq(one, 1), flip_row(two, 2)
    total = add(total, after(flip_seq(total, 1), one))
    one_in = after(one_in, total)
    one, two = jnp.concatenate([one, one_in]), jnp.concatenate([two, two_in])
    one_in, two_in = flip_row(one, 2), flip_seq(two, 1)
    total = add(total, after(flip_seq(total, 2), one))
    total = add(total, flip_seq(total, 4))
    other = flip_row(total, 1)
    one_other, two_other = flip_row(one, 1), flip_row(two, 1)
    one_in = after(one_in, other, one_other, two_other)
    return (
        (one, one_in, two, two_in, one_other, flip_row(one_in, 1), two_other, flip_row(two_in, 1)),
        (total, other),
    )


def unpack_small_kernel(spread_out, mine, other, grad_wkv, grad_route, grad_bup, grad_small, whole):
    core = place(spread_out)[0]
    piece = mine.shape[0]
    whole[block(core, piece), :] = mine[...].astype(f32)
    whole[block(1 - core, piece), :] = other[...].astype(f32)
    width = grad_wkv.shape[0]
    across = width // lanes
    grad_wkv[...] = whole[0:width, :]
    at = width
    for i in range(5):
        for g in range(across):
            grad_small[i : i + 1, g * lanes : (g + 1) * lanes] = whole[at : at + 1, :]
            at += 1
    for g in range(grad_bup.shape[1] // lanes):
        grad_bup[:, g * lanes : (g + 1) * lanes] = whole[at : at + 1, :]
        at += 1
    for i in range(grad_route.shape[0]):
        for g in range(across):
            grad_route[i : i + 1, g * lanes : (g + 1) * lanes] = whole[at : at + 1, :]
            at += 1


def call(kernel, out_shape, scratch, limit, flops, *operands):
    moved = sum(x.size * x.dtype.itemsize for x in operands)
    whole = pl.BlockSpec(memory_space=pltpu.VMEM)
    return pl.pallas_call(
        kernel,
        out_shape=out_shape,
        in_specs=[whole] * len(operands),
        out_specs=jax.tree.map(lambda _: whole, out_shape),
        scratch_shapes=scratch,
        compiler_params=pltpu.CompilerParams(vmem_limit_bytes=limit),
        cost_estimate=pl.CostEstimate(flops=flops, bytes_accessed=moved, transcendentals=0),
    )(*operands)


def shape(dims, dtype):
    return jax.ShapeDtypeStruct(tuple(dims), dtype)


def after(value, *earlier):
    return lax.optimization_barrier((value,) + earlier)[0]


def gather_keys(kvm, size):
    if size != 8:
        return [[kvm[None]], [lax.all_gather(kvm, "seq", axis=0, tiled=False)]]
    near_y, near_z, far_z = flip_seq(kvm, 1), flip_seq(kvm, 2), flip_seq(kvm, 4)
    others = [flip_seq(near_z, 1), flip_seq(far_z, 1), flip_seq(far_z, 2), flip_seq(kvm, 7)]
    return [[m[None] for m in (kvm, near_y, near_z, far_z)], [m[None] for m in others]]


def local(
    tokens, cotangent, w_query, w_kv, w_route, w_out, w_up, bias_up, w_down, bias_down,
    gain_one, shift_one, gain_two, shift_two, choices, segment_ids,
):
    size = lax.axis_size("seq")
    tok, cot = tokens[0], cotangent[0]
    rows, width = tok.shape
    hidden = w_up.shape[1]
    route = w_route.T
    experts = route.shape[0]
    row = lambda v: v.reshape(1, -1)
    message = shape((rows + pad_rows, lanes), bf16)
    kvm, qm, normed, gates, picks = call(
        project_kernel,
        (message, message, shape((rows, width), bf16), shape((rows, lanes), f32), shape((2, rows, lanes), jnp.int32)),
        [], 32 * mib, 2 * rows * width * (width + lanes),
        tok, w_query, w_kv, route, row(gain_one), row(shift_one), choices[0].T, segment_ids,
    )
    spread_out = size == 8 and lax.axis_size("row") == 4
    stacked = (2 * rows, lanes)
    near, others = gather_keys(kvm, size)
    all_kv = near + others
    if size != 8:
        near, others, all_kv = others, [], others
    attention_flops = 2 * 2 * rows * rows * size * lanes
    state = (shape(stacked, f32),) * 2
    kept = [pltpu.VMEM(stacked, bf16), pltpu.VMEM((rows, lanes), f32)]
    finished = (shape((rows, lanes), f32), shape(stacked, f32)) + state
    if others:
        so_far = call(
            functools.partial(forward_kernel, len(near), True, False), state, kept, 40 * mib, attention_flops, qm, kvm, *near
        )
        heads, lse, _, _ = call(
            functools.partial(forward_kernel, len(others), False, True), finished, kept, 40 * mib, attention_flops,
            qm, kvm, *others, *so_far,
        )
    else:
        heads, lse, _, _ = call(
            functools.partial(forward_kernel, len(near), True, True), finished, kept, 40 * mib, attention_flops, qm, kvm, *near
        )
    if size == 8:
        q_two = after(jnp.stack([qm, flip_seq(qm, 1)]), so_far[0])
        q_far = [flip_seq(q_two, 2), flip_seq(q_two, 4)]
        heads = after(heads, q_two)
    piece = gradient_rows(width, hidden)
    gradients = shape((piece * parts_of // 2, width), bf16)
    (
        layer_out, keep, send, grad_mid, dom, delta, dlog, grad_route, grad_bup, small_two,
    ) = call(
        functools.partial(middle_kernel, spread_out),
        (
            shape((rows, width), bf16), gradients, gradients, shape((rows, width), f32), shape((rows + stat_rows, lanes), bf16),
            shape(stacked, f32), shape((rows, experts), bf16), shape((experts, width), f32),
            shape((1, hidden), f32), shape((8, width), f32),
        ),
        [
            pltpu.VMEM((rows, width), bf16), pltpu.VMEM((width, rows), bf16), pltpu.VMEM((rows, width), f32),
            pltpu.VMEM((rows, width), f32), pltpu.VMEM((rows, width), f32), pltpu.VMEM((rows, width), bf16),
        ],
        56 * mib, 12 * rows * width * hidden,
        tok, cot, heads, gates, picks, lse, normed, w_out, w_up, row(bias_up), w_down, row(bias_down),
        row(gain_two), row(shift_two),
    )
    query_flops, key_flops = 3 * attention_flops // 2, 4 * attention_flops // 2
    results = {}
    extra_part = shape((width, width // 2), bf16)

    def query_back(parts, first, last, *earlier):
        finish = (normed, picks, w_query, dlog, route) if last else ()
        outs = (extra_part, extra_part, shape((rows, width), f32)) if last else ()
        results["query"] = call(
            functools.partial(query_back_kernel, spread_out, len(parts), first, last),
            outs + (shape(stacked, f32),),
            [pltpu.VMEM(stacked, bf16), pltpu.VMEM(stacked, bf16), pltpu.VMEM((rows, lanes), f32)],
            40 * mib, query_flops,
            after(qm, *earlier), dom, lse, delta, kvm, *parts, *(() if first else results["query"]), *finish,
        )
        return results["query"][-1]

    def key_back(q_parts, do_parts, first, last, *earlier):
        results["key"] = call(
            functools.partial(key_back_kernel, len(q_parts), first, last),
            ((shape((rows, lanes), bf16),) if last else ()) + state,
            [pltpu.VMEM(stacked, bf16), pltpu.VMEM(stacked, bf16), pltpu.VMEM((rows, lanes), f32)],
            56 * mib, key_flops * len(q_parts) * q_parts[0].shape[0] // size,
            after(kvm, *earlier), *q_parts, *do_parts, *(() if first else results["key"]),
        )
        return results["key"][-1]

    extra = 5 + hidden // width + experts
    small_rows = extra * (width // lanes) + width
    small_rows = -(-small_rows // 32) * 32

    def finish(*earlier):
        part = shape((small_rows // 2, lanes), bf16)
        return call(
            functools.partial(final_kernel, spread_out),
            (shape((rows, width), f32), part, part),
            [pltpu.VMEM((small_rows, lanes), bf16)], 48 * mib, 4 * rows * width * lanes,
            tok, normed, results["query"][2], after(results["key"][0], *earlier), grad_mid, w_kv, row(gain_one),
            grad_route, grad_bup, small_two,
        )

    if spread_out:
        send, q_near, q_other = lax.optimization_barrier((send, *q_far))
        q_last = flip_seq(q_other, 2)
        received = flip_row(send, 1)
        d_two = jnp.stack([dom, flip_seq(dom, 1)])
        received = after(received, query_back(near, True, False))
        part = shape((keep.shape[0] // 2, width // 2), bf16)
        one, one_send, two, two_send = simple(after_core_kernel, (part,) * 4, keep, received)
        one_in, two_in = flip_row(one_send, 2), flip_seq(two_send, 1)
        d_near, d_other = flip_seq(d_two, 2), flip_seq(d_two, 4)
        query_back(others, False, True, one)
        extra_keep, extra_send = results["query"][:2]
        part = shape((width // 2, width // 2), bf16)
        extra_keep, extra_send = simple(split_x_kernel, (part,) * 2, extra_keep, flip_row(extra_send, 1))
        extra_in = flip_row(extra_send, 2)
        done = key_back([q_two], [d_two], True, False, extra_keep)
        wider = shape((keep.shape[0] // 4 + width // 4, width // 2), bf16)
        part = shape((keep.shape[0] // 4, width // 2), bf16)
        one, one_send, two, two_send = simple(
            after_first_kernel, (wider, wider, part, part), one, after(one_in, done), two, two_in, extra_keep, extra_in
        )
        one_in, two_in = flip_seq(one_send, 1), flip_row(two_send, 2)
        d_last = flip_seq(d_other, 2)
        done = key_back([q_near, q_other], [d_near, d_other], False, False, one)
        piece += width // parts_of
        part = shape((piece, width), bf16)
        sent = simple(after_second_kernel, (part,) * 4, one, after(one_in, done), two, two_in)
        planes = [flip_seq(sent[i], 2 * i) for i in (1, 2, 3)]
        done = key_back([q_last], [d_last], False, True, sent[0])
        mine = simple(sum_kernel, part, after(sent[0], done), *planes)
        arrived = [flip_seq(mine, 2 * i) for i in (1, 2, 3)]
        grad_tokens, *small = finish(mine)
        large, small = finish_sums((mine, arrived), small)
    else:
        query_back(all_kv, True, True)
        gathered = [lax.all_gather(m, "seq", axis=0, tiled=False) for m in (qm, dom)]
        key_back(gathered[:1], gathered[1:], True, True)
        grad_tokens, *small = finish()
        small = lax.psum(small, ("seq", "row"))
        sums = lax.psum((keep, send, *results["query"][:2]), ("seq", "row"))
        large = ()
        for total, more in zip(sums[:2], sums[2:]):
            more = more.reshape(16, 2, -1, width // 2).transpose(0, 2, 1, 3).reshape(16, -1, width)
            cube = jnp.concatenate([total.reshape(16, piece, width), more], axis=1)
            cube = cube.reshape((4, 2, 2) + cube.shape[1:])
            for x in (0, 1):
                large += (cube[:, :, x, :, : width // 2].transpose(1, 0, 2, 3).reshape(-1, width // 2),)
            for y in (0, 1):
                large += (cube[:, y, :, :, width // 2 :].transpose(1, 0, 2, 3).reshape(-1, width // 2),)
    grad_wkv, grad_route, grad_bup, grad_small = call(
        functools.partial(unpack_small_kernel, spread_out),
        (
            shape((width, lanes), f32), shape((experts, width), f32), shape((1, hidden), f32), shape((8, width), f32),
        ),
        [pltpu.VMEM((small_rows, lanes), f32)], 48 * mib, 0, *small,
    )
    grad_up, grad_down, grad_out, grad_wq = call(
        functools.partial(unpack_kernel, spread_out),
        (shape((width, hidden), f32), shape((hidden, width), f32)) + (shape((width, width), f32),) * 2,
        [], 48 * mib, 0, *large,
    )
    return (
        layer_out[None],
        grad_tokens[None],
        grad_wq,
        grad_wkv,
        grad_route.T,
        grad_out,
        grad_up,
        grad_bup.reshape(-1),
        grad_down,
        grad_small[2],
        grad_small[0],
        grad_small[1],
        grad_small[3],
        grad_small[4],
    )


def solution(mesh):
    split_tokens = P("row", "seq", None)
    placed = (split_tokens, split_tokens) + (P(),) * 12 + (split_tokens, P("row", "seq"))
    return jax.shard_map(
        local,
        mesh=mesh,
        in_specs=placed,
        out_specs=(split_tokens, split_tokens) + (P(),) * 12,
        check_vma=False,
    )
```

```python
import functools

import jax
import jax.numpy as jnp
from jax import lax
from jax.experimental import pallas as pl
from jax.experimental.pallas import tpu as pltpu
from jax.sharding import PartitionSpec as P

f32 = jnp.float32
bf16 = jnp.bfloat16
epsilon = 1e-05
lanes = 128
half = 64
chunk = 160
pad_rows = 16
stat_rows = 80
masked = -2e30
lowest = -1e30
feed_step = 256
mib = 1 << 20


def nn(a, b):
    return lax.dot_general(a, b, (((1,), (0,)), ((), ())), preferred_element_type=f32)


def nt(a, b):
    return lax.dot_general(a, b, (((1,), (1,)), ((), ())), preferred_element_type=f32)


def tn(a, b):
    return lax.dot_general(a, b, (((0,), (0,)), ((), ())), preferred_element_type=f32)


def lane_ids(rows):
    return lax.broadcasted_iota(jnp.int32, (rows, lanes), 1)


def swap(values):
    return pltpu.roll(values, half, 1)


def column(row):
    return jnp.transpose(jnp.broadcast_to(row, (lanes, row.shape[1])), (1, 0))


def to_rows(row):
    count = row.shape[1] // lanes
    pieces = [row[:, i * lanes : (i + 1) * lanes] for i in range(count)]
    return jnp.concatenate(pieces + [jnp.zeros((8 - count, lanes), f32)], axis=0)


def from_rows(block, count):
    return jnp.concatenate([block[i : i + 1] for i in range(count)], axis=1)


def wide(values, count):
    return jnp.concatenate([values] * count, axis=1)


def normalized(x):
    centred = x - jnp.mean(x, axis=-1, keepdims=True)
    inverse = lax.rsqrt(jnp.mean(centred * centred, axis=-1, keepdims=True) + epsilon)
    return centred * inverse, inverse


def normalized_back(upstream, unit, inverse, gain):
    scaled = upstream * gain
    inner = (
        scaled
        - jnp.mean(scaled, axis=-1, keepdims=True)
        - unit * jnp.mean(scaled * unit, axis=-1, keepdims=True)
    )
    grad_gain = jnp.sum(upstream * unit, axis=0, keepdims=True)
    return inverse * inner, grad_gain, jnp.sum(upstream, axis=0, keepdims=True)


def row_blocks(rows):
    return [slice(r, r + lanes) for r in range(0, rows, lanes)]


def keys_kernel(tok_in, wkv_in, gain_in, shift_in, seg_in, kvm, n_out, seg_out, tok, wkv, gain, shift, seg, sems):
    moves = [
        pltpu.make_async_copy(source, target, sems.at[i])
        for i, (source, target) in enumerate(
            ((tok_in, tok), (wkv_in, wkv), (gain_in, gain), (shift_in, shift), (seg_in, seg))
        )
    ]
    for move in moves:
        move.start()
    for move in moves:
        move.wait()
    rows = tok.shape[0]
    for at in row_blocks(rows):
        unit, _ = normalized(tok[at, :].astype(f32))
        normed = (unit * gain[...] + shift[...]).astype(bf16)
        n_out[at, :] = normed
        kvm[at, :] = nn(normed, wkv[...]).astype(bf16)
        seg_out[at, :] = column(seg[:, at].astype(f32))
    seg_row = seg[...].astype(f32)
    ids = to_rows(seg_row)
    line = lax.broadcasted_iota(jnp.int32, (8, lanes), 0)
    ids = jnp.where(line == rows // lanes, seg_row[:, 0:1], ids)
    ids = jnp.where(line == rows // lanes + 1, seg_row[:, rows - 1 : rows], ids)
    ids = jnp.concatenate([ids, jnp.zeros((pad_rows - 8, lanes), f32)], axis=0).astype(bf16)
    kvm[rows : rows + pad_rows, :] = ids


def queries_kernel(normed_in, kvm, wq, wroute, choice, qm, q_stack, k_stack, v_stack, gates, picks):
    rows = normed_in.shape[0]
    experts = wroute.shape[0]
    low = lane_ids(lanes) < half
    slot = lax.broadcasted_iota(jnp.int32, (lanes, experts), 1)
    zero = jnp.zeros((lanes, lanes), f32)
    scale = half ** (-0.5)
    for at in row_blocks(rows):
        second_at = slice(rows + at.start, rows + at.stop)
        normed = normed_in[at, :]
        first = column(choice[0:1, at].astype(f32)).astype(jnp.int32)
        second = column(choice[1:2, at].astype(f32)).astype(jnp.int32)
        picks[0, at, :] = first
        picks[1, at, :] = second
        query_all = nn(normed, wq[...])
        one, two = pick_slots(query_all, first, second)
        one = one.astype(bf16).astype(f32) * scale
        two = two.astype(bf16).astype(f32) * scale
        qm[at, :] = jnp.where(low, one, two).astype(bf16)
        q_stack[at, :] = jnp.where(low, one, zero).astype(bf16)
        q_stack[second_at, :] = jnp.where(low, swap(two), zero).astype(bf16)
        kv = kvm[at, :].astype(f32)
        other = swap(kv)
        k_stack[at, :] = jnp.where(low, kv, zero).astype(bf16)
        k_stack[second_at, :] = jnp.where(low, zero, other).astype(bf16)
        v_stack[at, :] = jnp.where(low, other, zero).astype(bf16)
        v_stack[second_at, :] = jnp.where(low, zero, kv).astype(bf16)
        logits = nt(normed, wroute[...])
        picked_one = jnp.sum(jnp.where(slot == first[:, :experts], logits, 0.0), axis=1, keepdims=True)
        picked_two = jnp.sum(jnp.where(slot == second[:, :experts], logits, 0.0), axis=1, keepdims=True)
        top = jnp.maximum(picked_one, picked_two)
        exp_one = jnp.exp(picked_one - top)
        exp_two = jnp.exp(picked_two - top)
        gates[at, :] = jnp.where(low, exp_one, exp_two) / (exp_one + exp_two)
    qm[rows : rows + pad_rows, :] = kvm[rows : rows + pad_rows, :]


def pick_slots(values, first, second):
    one = jnp.zeros(first.shape, f32)
    two = jnp.zeros(first.shape, f32)
    first_pair, second_pair = first // 2, second // 2
    for g in range(values.shape[1] // lanes):
        part = values[:, g * lanes : (g + 1) * lanes]
        one = jnp.where(first_pair == g, part, one)
        two = jnp.where(second_pair == g, part, two)
    one = jnp.where(first % 2 == 0, one, swap(one))
    two = jnp.where(second % 2 == 1, two, swap(two))
    return one, two


def id_range(message, rows):
    block = message[rows : rows + pad_rows, :][0:8].astype(f32)
    count = rows // lanes
    return block[count : count + 1], block[count + 1 : count + 2]


def id_row(message, rows):
    block = message[rows : rows + pad_rows, :][0:8].astype(f32)
    return from_rows(block, rows // lanes)


def over_pieces(parts, rows, own, visit):
    own_low, own_high = id_range(own, rows)

    def kind(message):
        low, high = id_range(message, rows)
        meets = jnp.where((low <= own_high) & (high >= own_low), 1.0, 0.0)
        return meets * jnp.where((low == high) & (own_low == own_high), 2.0, 1.0)

    def one(index, i, message, code):
        @pl.when(code == 2)
        def _():
            visit(index, i, message, True)

        @pl.when(code == 1)
        def _():
            visit(index, i, message, False)

    few = [(index, i, part.at[i]) for index, part in enumerate(parts) for i in range(part.shape[0]) if part.shape[0] <= 8]
    if few:
        codes = sum(kind(message) * 4.0**n for n, (_, _, message) in enumerate(few))
        codes = jnp.max(codes).astype(jnp.int32)
    for n, (index, i, message) in enumerate(few):
        one(index, i, message, lax.rem(codes // 4**n, 4))
    for index, part in enumerate(parts):
        if part.shape[0] > 8:

            @pl.loop(0, part.shape[0])
            def _(i, index=index, part=part):
                message = part.at[i]
                one(index, i, message, jnp.max(kind(message)).astype(jnp.int32))


def places(ref, c):
    rows = ref.shape[0] // 2
    return slice(c * chunk, (c + 1) * chunk), slice(rows + c * chunk, rows + (c + 1) * chunk)


def both(ref, c):
    one, two = places(ref, c)
    return jnp.concatenate([ref[one, :], ref[two, :]], axis=0)


def put_both(ref, c, values):
    one, two = places(ref, c)
    ref[one, :] = values[:chunk]
    ref[two, :] = values[chunk:]


def same(seg, c, ids):
    mine = seg[c * chunk : (c + 1) * chunk, :]
    return wide(jnp.concatenate([mine, mine], axis=0), ids.shape[1] // lanes) == ids


def staged(chunks, products, weigh, collect):
    current, ready = products(0), None
    for c in range(chunks):
        following = products(c + 1) if c + 1 < chunks else None
        if ready is not None:
            collect(c - 1, *ready)
        ready = weigh(c, current)
        current = following
    collect(chunks - 1, *ready)


def forward_kernel(piece_count, first, last, stack, seg, own, *rest):
    parts = rest[:piece_count]
    rest = rest[piece_count:]
    if not first:
        total_in, peak_in = rest[:2]
        rest = rest[2:]
    if last:
        heads, lse, total, peak = rest
    else:
        total, peak = rest
    rows = seg.shape[0]
    across = rows // lanes
    if first:
        peak[...] = jnp.full(peak.shape, lowest, f32)
        total[...] = jnp.zeros(total.shape, f32)
    else:
        peak[...] = peak_in[...]
        total[...] = total_in[...]

    def visit(index, i, message, uniform):
        kv = message[0:rows, :]
        low = lane_ids(rows) < half
        values = jnp.where(low, jnp.ones_like(kv), kv)
        if not uniform:
            key_ids = id_row(message, rows)

        def products(c):
            scores = nt(both(stack, c), kv)
            if not uniform:
                scores = jnp.where(same(seg, c, key_ids), scores, masked)
            return scores

        def weigh(c, scores):
            before = both(peak, c)
            now = jnp.maximum(before, jnp.max(scores, axis=1, keepdims=True))
            put_both(peak, c, now)
            return jnp.exp(scores - wide(now, across)).astype(bf16), jnp.exp(before - now)

        def collect(c, weights, factor):
            put_both(total, c, both(total, c) * factor + nn(weights, values))

        staged(rows // chunk, products, weigh, collect)

    over_pieces(parts, rows, own, visit)
    if not last:
        return
    low = lane_ids(lanes) < half
    for at in row_blocks(rows):
        second_at = slice(rows + at.start, rows + at.stop)
        one, two = total[at, :], total[second_at, :]
        one_other, two_other = swap(one), swap(two)
        heads[at, :] = jnp.where(low, one_other, two) / jnp.where(low, one, two_other)
        lse[at, :] = peak[at, :] + jnp.log(jnp.where(low, one, one_other))
        lse[second_at, :] = peak[second_at, :] + jnp.log(jnp.where(low, two, two_other))


def query_back_kernel(spread_out, piece_count, first, last, stack, stack_do, lse, delta, seg, own, *rest):
    parts = rest[:piece_count]
    rest = rest[piece_count:]
    if not first:
        total_in = rest[0]
        rest = rest[1:]
    if last:
        normed, picks, wq, dlog, wroute, keep, send, grad_n, total, spread_keep = rest
    else:
        total = rest[0]
    rows = seg.shape[0]
    across = rows // lanes
    total[...] = jnp.zeros(total.shape, f32) if first else total_in[...]

    def visit(index, i, message, uniform):
        kv = message[0:rows, :]
        if not uniform:
            key_ids = id_row(message, rows)

        def products(c):
            scores = nt(both(stack, c), kv)
            if not uniform:
                scores = jnp.where(same(seg, c, key_ids), scores, masked)
            return scores, nt(both(stack_do, c), kv)

        def weigh(c, pair):
            scores, grad_prob = pair
            prob = jnp.exp(scores - wide(both(lse, c), across))
            return ((prob * (grad_prob - wide(both(delta, c), across))).astype(bf16),)

        def collect(c, grad_scores):
            put_both(total, c, both(total, c) + nn(grad_scores, kv))

        staged(rows // chunk, products, weigh, collect)

    over_pieces(parts, rows, own, visit)
    if not last:
        return
    low = lane_ids(lanes) < half
    scale = half ** (-0.5)
    for at in row_blocks(rows):
        one = total[at, :] * scale
        two = total[slice(rows + at.start, rows + at.stop), :] * scale
        one = jnp.where(low, one, swap(one))
        two = jnp.where(low, two, swap(two))
        spread = spread_slots(one, two, picks[0, at, :], picks[1, at, :], normed.shape[1] // lanes).astype(bf16)
        spread_keep[at, :] = spread
        grad_n[at, :] = nt(spread, wq[...]) + nn(dlog[at, :], wroute[...])
    whole = tn(normed[...], spread_keep[...]).astype(bf16)
    core = place(spread_out)[0]
    count = whole.shape[0] // parts_of
    for i in range(parts_of // 2):
        at = slice(i * count, (i + 1) * count)
        even = whole[2 * i * count : (2 * i + 1) * count]
        odd = whole[(2 * i + 1) * count : (2 * i + 2) * count]
        keep[at, :] = jnp.where(core == 0, even, odd)
        send[at, :] = jnp.where(core == 0, odd, even)


def spread_slots(one, two, first, second, pairs):
    upper = (lane_ids(one.shape[0]) >= half).astype(jnp.int32)
    out = []
    for g in range(pairs):
        expert = 2 * g + upper
        out.append(jnp.where(first == expert, one, jnp.where(second == expert, two, 0.0)))
    return jnp.concatenate(out, axis=1)


def key_back_kernel(piece_count, first, last, keys, values, seg, own, *rest):
    q_parts = rest[:piece_count]
    do_parts = rest[piece_count : 2 * piece_count]
    rest = rest[2 * piece_count :]
    if not first:
        k_in, v_in = rest[:2]
        rest = rest[2:]
    if last:
        grad_kv = rest[0]
        rest = rest[1:]
    total_k, total_v = rest
    rows = seg.shape[0]
    across = rows // lanes
    if first:
        total_k[...] = jnp.zeros(total_k.shape, f32)
        total_v[...] = jnp.zeros(total_v.shape, f32)
    else:
        total_k[...] = k_in[...]
        total_v[...] = v_in[...]

    def visit(index, i, message, uniform):
        queries = message[0:rows, :]
        sent = do_parts[index].at[i]
        grads = sent[0:rows, :]
        stats = sent[rows : rows + stat_rows, :].astype(f32)

        def stat(first, terms):
            block = stats[first * 8 : first * 8 + 8]
            for t in range(1, terms):
                block = block + stats[(first + t) * 8 : (first + t) * 8 + 8]
            return from_rows(block, across)

        lse = (stat(0, 3), stat(3, 3))
        delta = (stat(6, 2), stat(8, 2))
        if not uniform:
            query_ids = id_row(message, rows)

        def spread(pair):
            return jnp.concatenate(
                [jnp.broadcast_to(pair[0], (chunk, rows)), jnp.broadcast_to(pair[1], (chunk, rows))],
                axis=0,
            )

        def products(c):
            scores = nt(both(keys, c), queries)
            if not uniform:
                scores = jnp.where(same(seg, c, query_ids), scores, masked)
            return scores, nt(both(values, c), grads)

        def weigh(c, pair):
            scores, grad_prob = pair
            prob = jnp.exp(scores - spread(lse))
            return prob.astype(bf16), (prob * (grad_prob - spread(delta))).astype(bf16)

        def collect(c, prob, grad_scores):
            put_both(total_v, c, both(total_v, c) + nn(prob, grads))
            put_both(total_k, c, both(total_k, c) + nn(grad_scores, queries))

        staged(rows // chunk, products, weigh, collect)

    over_pieces(q_parts, rows, own, visit)
    if not last:
        return
    low = lane_ids(lanes) < half
    for at in row_blocks(rows):
        second_at = slice(rows + at.start, rows + at.stop)
        key_grad = total_k[at, :] + swap(total_k[second_at, :])
        value_grad = swap(total_v[at, :]) + total_v[second_at, :]
        grad_kv[at, :] = jnp.where(low, key_grad, value_grad).astype(bf16)


def middle_kernel(
    spread_out,
    tok, cot, heads, gates, picks, lse, normed, wout, wup, bup, wdown, bdown, gain, shift,
    layer_out, keep, send, grad_mid, dom, do_stack, delta_out, dlog, grad_route, grad_bup, grad_small,
    second_n, second_t, total_y, total_n, mid_keep, mixed_keep, unit_keep, inverse_keep, low_keep, logit_keep,
):
    rows, width = tok.shape
    hidden = wup.shape[1]
    lane = lane_ids(lanes)
    low = lane < half
    pairs = width // lanes
    for at in row_blocks(rows):
        gated = gates[at, :] * heads[at, :]
        turned = swap(gated)
        mixed = spread_slots(
            jnp.where(low, gated, turned), jnp.where(low, turned, gated), picks[0, at, :], picks[1, at, :], pairs
        ).astype(bf16)
        mixed_keep[at, :] = mixed
        middle = tok[at, :].astype(f32) + nn(mixed, wout[...])
        mid_keep[at, :] = middle
        unit, inverse = normalized(middle)
        unit_keep[at, :] = unit
        inverse_keep[at, :] = jnp.broadcast_to(inverse, (lanes, lanes))
        n_two = (unit * gain[...] + shift[...]).astype(bf16)
        second_n[at, :] = n_two
        second_t[:, at] = n_two.T
    total_y[...] = jnp.zeros(total_y.shape, f32)
    total_n[...] = jnp.zeros(total_n.shape, f32)
    step = feed_step
    root = 0.7978845608028654
    cubic = 0.044715
    core = place(spread_out)[0]
    down_rows = hidden // parts_of
    up_rows = width // parts_of
    piece = gradient_rows(width, hidden)

    def put(index, at_row, at_lane, even, odd):
        count, across = even.shape
        start = index * piece + at_row
        target = (slice(start, start + count), slice(at_lane, at_lane + across))
        keep[target] = jnp.where(core == 0, even, odd)
        send[target] = jnp.where(core == 0, odd, even)

    def products(f):
        at = slice(f * step, (f + 1) * step)
        return nn(second_n[...], wup[:, at]) + bup[:, at], nt(cot[...], wdown[at, :])

    def bend(f, pair):
        pre, grad_act = pair
        square = pre * pre
        bent = jnp.tanh(pre * (root + (root * cubic) * square))
        rise = 0.5 + 0.5 * bent
        act = (pre * rise).astype(bf16)
        slope = rise + (pre * (rise * (1.0 - bent))) * (root + (3.0 * root * cubic) * square)
        grad_pre = (grad_act * slope).astype(bf16)
        grad_bup[:, f * step : (f + 1) * step] = jnp.sum(grad_pre.astype(f32), axis=0, keepdims=True)
        return act, grad_pre

    def collect(f, act, grad_pre):
        at = slice(f * step, (f + 1) * step)
        total_y[...] += nn(act, wdown[at, :])
        total_n[...] += nt(grad_pre, wup[:, at])
        grad_down = tn(act, cot[...]).astype(bf16)
        for i in range(step // (2 * down_rows)):
            pair = grad_down[2 * i * down_rows : 2 * (i + 1) * down_rows]
            put(f * (step // (2 * down_rows)) + i, 0, 0, pair[:down_rows], pair[down_rows:])
        grad_up = nn(second_t[...], grad_pre).astype(bf16)
        block_of, at_lane = divmod(f * step, width)
        for i in range(parts_of // 2):
            pair = grad_up[2 * i * up_rows : 2 * (i + 1) * up_rows]
            put(i, down_rows + block_of * up_rows, at_lane, pair[:up_rows], pair[up_rows:])

    staged(hidden // step, products, bend, collect)

    sums = [jnp.zeros((1, width), f32)] * 3
    experts = dlog.shape[1]
    stats = [[], [], [], []]
    zero = jnp.zeros((lanes, lanes), f32)
    for at in row_blocks(rows):
        second_at = slice(rows + at.start, rows + at.stop)
        first, second = picks[0, at, :], picks[1, at, :]
        layer_out[at, :] = (mid_keep[at, :] + total_y[at, :] + bdown[...]).astype(bf16)
        unit = unit_keep[at, :]
        back, grad_gain, grad_shift = normalized_back(total_n[at, :], unit, wide(inverse_keep[at, :], pairs), gain[...])
        dy = cot[at, :].astype(f32)
        grad_middle = dy + back
        grad_mid[at, :] = grad_middle
        sums = [a + b for a, b in zip(sums, (jnp.sum(dy, axis=0, keepdims=True), grad_gain, grad_shift))]
        grad_low = grad_middle.astype(bf16)
        low_keep[at, :] = grad_low
        one, two = pick_slots(nt(grad_low, wout[...]), first, second)
        slots = jnp.where(low, one, two)
        head_values = heads[at, :]
        gate = gates[at, :]
        grad_heads = (gate * slots).astype(bf16)
        dom[at, :] = grad_heads
        carried = grad_heads.astype(f32)
        turned = swap(carried)
        do_stack[at, :] = jnp.where(low, zero, turned).astype(bf16)
        do_stack[second_at, :] = jnp.where(low, zero, carried).astype(bf16)
        gated_grad = slots * head_values
        gate_one = jnp.sum(jnp.where(low, gated_grad, 0.0), axis=1, keepdims=True)
        gate_two = jnp.sum(jnp.where(low, 0.0, gated_grad), axis=1, keepdims=True)
        grad_gate = jnp.where(low, gate_one, gate_two)
        weighted = gate * grad_gate
        grad_logit = gate * (grad_gate - (weighted + swap(weighted)))
        logit_other = swap(grad_logit)
        logit_one = jnp.where(low, grad_logit, logit_other)
        logit_two = jnp.where(low, logit_other, grad_logit)
        grad_logits = jnp.where(lane == first, logit_one, jnp.where(lane == second, logit_two, 0.0)).astype(bf16)
        logit_keep[at, :] = grad_logits
        dlog[at, :] = grad_logits[:, :experts]
        carried = carried * head_values
        delta_one = jnp.broadcast_to(jnp.sum(jnp.where(low, carried, 0.0), axis=1, keepdims=True), (lanes, lanes))
        delta_two = jnp.broadcast_to(jnp.sum(jnp.where(low, 0.0, carried), axis=1, keepdims=True), (lanes, lanes))
        delta_out[at, :] = delta_one
        delta_out[second_at, :] = delta_two
        for store, values in zip(stats, (lse[at, :], lse[second_at, :], delta_one, delta_two)):
            store.append(jnp.transpose(values, (1, 0))[0:1, :])
    blocks = []
    for store, terms in zip(stats, (3, 3, 2, 2)):
        rest = jnp.concatenate(store + [jnp.zeros((8 - len(store), lanes), f32)], axis=0)
        for _ in range(terms):
            part = rest.astype(bf16).astype(f32)
            blocks.append(part)
            rest = rest - part
    dom[rows : rows + stat_rows, :] = jnp.concatenate(blocks, axis=0).astype(bf16)
    grad_small[...] = jnp.concatenate(sums + [jnp.zeros((5, width), f32)], axis=0)
    grad_route[...] = tn(logit_keep[...], normed[...])[:experts, :]
    grad_out = tn(mixed_keep[...], low_keep[...]).astype(bf16)
    for i in range(parts_of // 2):
        pair = grad_out[2 * i * up_rows : 2 * (i + 1) * up_rows]
        put(i, piece - up_rows, 0, pair[:up_rows], pair[up_rows:])


def final_kernel(
    spread_out, tok, normed, grad_n, grad_kv, grad_mid, wkv, gain, grad_route, grad_bup, small_two,
    grad_tokens, keep, send, whole,
):
    width = tok.shape[1]
    whole[0:width, :] = tn(normed[...], grad_kv[...]).astype(bf16)
    grad_gain = grad_shift = jnp.zeros((1, width), f32)
    for at in row_blocks(tok.shape[0]):
        upstream = grad_n[at, :] + nt(grad_kv[at, :], wkv[...])
        unit, inverse = normalized(tok[at, :].astype(f32))
        back, more_gain, more_shift = normalized_back(upstream, unit, inverse, gain[...])
        grad_tokens[at, :] = grad_mid[at, :] + back
        grad_gain, grad_shift = grad_gain + more_gain, grad_shift + more_shift
    rows = [grad_gain, grad_shift] + [small_two[i : i + 1, :] for i in range(3)]
    rows += [grad_bup[:, i : i + width] for i in range(0, grad_bup.shape[1], width)]
    rows += [grad_route[i : i + 1, :] for i in range(grad_route.shape[0])]
    small = jnp.concatenate([row[:, i : i + lanes] for row in rows for i in range(0, width, lanes)], axis=0)
    last = whole.shape[0] - width
    small = jnp.concatenate([small, jnp.zeros((last - small.shape[0], lanes), f32)], axis=0)
    whole[width:, :] = small.astype(bf16)
    core = place(spread_out)[0]
    piece = keep.shape[0]
    keep[...] = whole[block(core, piece), :]
    send[...] = whole[block(1 - core, piece), :]


parts_of = 32


def place(spread_out):
    if not spread_out:
        return 0, 0, 0, 0
    row, seq = lax.axis_index("row"), lax.axis_index("seq")
    return lax.rem(row, 2), row // 2, lax.rem(seq, 2), seq // 2


def gradient_rows(width, hidden):
    return hidden // parts_of + (hidden // width + 1) * (width // parts_of)


def block(index, count):
    return pl.ds(pl.multiple_of(index * count, 16), count)


def plus(*refs):
    def get(at):
        total = refs[0][at].astype(f32)
        for ref in refs[1:]:
            total = total + ref[at].astype(f32)
        return total.astype(bf16)

    return get


def after_core_kernel(keep, received, one_keep, one_send, two_keep, two_send):
    _, x, y, _ = place(True)
    piece, upper, lower = keep.shape[0] // 16, one_keep.shape[0] // 8, two_keep.shape[0] // 8
    total = plus(keep, received)

    def part(index, offset, count):
        return total((pl.ds(pl.multiple_of(index * piece + offset, 16), count), slice(None)))

    for zy in range(8):
        here = slice(zy * upper, (zy + 1) * upper)
        one_keep[here, :] = part(zy * 2 + x, 0, upper)
        one_send[here, :] = part(zy * 2 + 1 - x, 0, upper)
    for z in range(4):
        for at_x in range(2):
            here = slice((z * 2 + at_x) * lower, (z * 2 + at_x + 1) * lower)
            two_keep[here, :] = part((z * 2 + y) * 2 + at_x, upper, lower)
            two_send[here, :] = part((z * 2 + 1 - y) * 2 + at_x, upper, lower)


def split_kernel(keep, received, kept, sent):
    x = place(True)[1]
    piece = kept.shape[0] // 8
    total = plus(keep, received)
    for i in range(8):
        here = slice(i * piece, (i + 1) * piece)
        kept[here, :] = total((block(i * 2 + x, piece), slice(None)))
        sent[here, :] = total((block(i * 2 + 1 - x, piece), slice(None)))


def after_first_kernel(one, one_in, extra, extra_in, two, two_in, one_keep, one_send, two_keep, two_send):
    _, x, y, _ = place(True)
    upper = one.shape[0] // 8
    for total, mine, kept, sent, piece, offset in (
        (plus(one, one_in), y, one_keep, one_send, upper, 0),
        (plus(extra, extra_in), y, one_keep, one_send, extra.shape[0] // 8, upper),
        (plus(two, two_in), x, two_keep, two_send, two.shape[0] // 8, 0),
    ):
        stride = kept.shape[0] // 4
        for z in range(4):
            here = slice(z * stride + offset, z * stride + offset + piece)
            kept[here, :] = total((block(z * 2 + mine, piece), slice(None)))
            sent[here, :] = total((block(z * 2 + 1 - mine, piece), slice(None)))


def after_second_kernel(one, one_in, two, two_in, *outs):
    z = place(True)[3]
    at = 0
    for total, count in ((plus(one, one_in), one.shape[0] // 4), (plus(two, two_in), two.shape[0] // 4)):
        for i, out in enumerate(outs):
            out[at : at + count, :] = total((block(z ^ i, count), slice(None)))
        at += count


def sum_kernel(*refs):
    refs[-1][...] = plus(*refs[:-1])(Ellipsis)


def join_halves_kernel(*refs):
    z = place(True)[3]
    one, two = refs[4:]
    upper, lower = one.shape[0] // 4, two.shape[0] // 4
    for i in range(4):
        one[block(z ^ i, upper), :] = refs[i][:upper, :]
        two[block(z ^ i, lower), :] = refs[i][upper:, :]


def unpack_kernel(spread_out, turns, outer, fresh, *refs):
    core, x, y, _ = place(spread_out)
    count = 2 * len(turns)
    parts, refs = refs[:count], refs[count if fresh else count + 4 :]
    outs, stages, sems = refs[:4], refs[4:8], refs[8]
    grad_up, grad_down, grad_out, grad_wq = outs
    width, hidden = grad_up.shape
    down_rows, up_rows = hidden // parts_of, width // parts_of
    moves = []

    def send(stage, start, rows, out, device):
        target = out.at[block(device, rows), :]
        moves.append(pltpu.make_async_copy(stage.at[start : start + rows, :], target, sems.at[len(moves)]))
        moves[-1].start()

    at = 0
    for n, turn in enumerate(turns):
        one, two = parts[2 * n : 2 * n + 2]
        for inner in range(2):
            for z in range(4):
                row, low, high = inner * 4 + z, at * down_rows, at * up_rows
                at += 1
                device = ((z * 2 + (y ^ inner)) * 2 + (x ^ outer)) * 2 + (core ^ turn)
                base = row * (down_rows + up_rows)
                stages[1][low : low + down_rows, :] = one[base : base + down_rows, :].astype(f32)
                send(stages[1], low, down_rows, grad_down, device)
                base += down_rows
                stages[3][high : high + up_rows, :] = one[base : base + up_rows, :].astype(f32)
                send(stages[3], high, up_rows, grad_wq, device)
                device = ((z * 2 + (y ^ outer)) * 2 + (x ^ inner)) * 2 + (core ^ turn)
                across = hidden // width
                base = row * (across + 1) * up_rows
                for c in range(across):
                    value = two[base + c * up_rows : base + (c + 1) * up_rows, :]
                    stages[0][high : high + up_rows, c * width : (c + 1) * width] = value.astype(f32)
                send(stages[0], high, up_rows, grad_up, device)
                base += across * up_rows
                stages[2][high : high + up_rows, :] = two[base : base + up_rows, :].astype(f32)
                send(stages[2], high, up_rows, grad_out, device)
    for move in moves:
        move.wait()


def unpack(spread_out, turns, outer, parts, so_far, width, hidden):
    outs = (shape((width, hidden), f32), shape((hidden, width), f32)) + (shape((width, width), f32),) * 2
    share = 4 // len(turns)
    hbm = pl.BlockSpec(memory_space=pltpu.HBM)
    whole = pl.BlockSpec(memory_space=pltpu.VMEM)
    return pl.pallas_call(
        functools.partial(unpack_kernel, spread_out, turns, outer, not so_far),
        out_shape=outs,
        in_specs=[whole] * len(parts) + [hbm] * len(so_far),
        out_specs=(hbm,) * 4,
        scratch_shapes=[pltpu.VMEM((out.shape[0] // share, out.shape[1]), f32) for out in outs]
        + [pltpu.SemaphoreType.DMA((32 * len(turns),))],
        input_output_aliases={len(parts) + i: i for i in range(len(so_far))},
        compiler_params=pltpu.CompilerParams(vmem_limit_bytes=16 * mib),
        cost_estimate=pl.CostEstimate(flops=2 * busy, bytes_accessed=0, transcendentals=0),
    )(*parts, *so_far)


def flip_row(x, mask):
    return lax.ppermute(x, "row", [(i, i ^ mask) for i in range(4)])


def flip_seq(x, mask):
    return lax.ppermute(x, "seq", [(i, i ^ mask) for i in range(8)])


def simple(kernel, outs, *operands):
    return call(kernel, outs, [], 20 * mib, 0.5, *operands)


def add(a, b):
    return (a.astype(f32) + b.astype(f32)).astype(bf16)


def finish_sums(large, small, hidden):
    mine, arrived = large
    keep, send = small
    count, width = mine.shape
    part = shape((2 * count, width), bf16)
    one, two = simple(join_halves_kernel, (part,) * 2, mine, *arrived)
    total = add(keep, after(flip_row(send, 1), one))
    one_in, two_in = flip_seq(one, 1), flip_row(two, 2)
    one, two = jnp.concatenate([one, one_in]), jnp.concatenate([two, two_in])
    one_in, two_in = flip_row(one, 2), flip_seq(two, 1)
    total = add(total, after(flip_row(total, 2), one, two))
    total = add(total, flip_seq(total, 1))
    one_other, two_other = flip_row(one, 1), flip_row(two, 1)
    total = add(total, flip_seq(total, 2))
    done = unpack(True, (0, 1), 0, (one, two, one_other, two_other), (), width, hidden)
    total = add(total, after(flip_seq(total, 4), done[3]))
    other = flip_row(total, 1)
    one_in = after(one_in, other)
    one_other, two_other = flip_row(one_in, 1), flip_row(two_in, 1)
    done = unpack(True, (0,), 1, (one_in, two_in), done, width, hidden)
    done = unpack(True, (1,), 1, (one_other, two_other), done, width, hidden)
    return done, (total, other)


def unpack_small_kernel(spread_out, mine, other, grad_wkv, grad_route, grad_bup, grad_small, whole):
    core = place(spread_out)[0]
    piece = mine.shape[0]
    whole[block(core, piece), :] = mine[...].astype(f32)
    whole[block(1 - core, piece), :] = other[...].astype(f32)
    width = grad_wkv.shape[0]
    across = width // lanes
    grad_wkv[...] = whole[0:width, :]
    at = width
    for i in range(5):
        for g in range(across):
            grad_small[i : i + 1, g * lanes : (g + 1) * lanes] = whole[at : at + 1, :]
            at += 1
    for g in range(grad_bup.shape[1] // lanes):
        grad_bup[:, g * lanes : (g + 1) * lanes] = whole[at : at + 1, :]
        at += 1
    for i in range(grad_route.shape[0]):
        for g in range(across):
            grad_route[i : i + 1, g * lanes : (g + 1) * lanes] = whole[at : at + 1, :]
            at += 1


busy = 400_000_000


def call(kernel, out_shape, scratch, limit, time, *operands):
    whole = pl.BlockSpec(memory_space=pltpu.VMEM)
    return pl.pallas_call(
        kernel,
        out_shape=out_shape,
        in_specs=[whole] * len(operands),
        out_specs=jax.tree.map(lambda _: whole, out_shape),
        scratch_shapes=scratch,
        compiler_params=pltpu.CompilerParams(vmem_limit_bytes=limit),
        cost_estimate=pl.CostEstimate(flops=int(time * busy), bytes_accessed=0, transcendentals=0),
    )(*operands)


def shape(dims, dtype):
    return jax.ShapeDtypeStruct(tuple(dims), dtype)


def after(value, *earlier):
    return lax.optimization_barrier((value,) + earlier)[0]


def local(
    tokens, cotangent, w_query, w_kv, w_route, w_out, w_up, bias_up, w_down, bias_down,
    gain_one, shift_one, gain_two, shift_two, choices, segment_ids,
):
    size = lax.axis_size("seq")
    tok, cot = tokens[0], cotangent[0]
    rows, width = tok.shape
    hidden = w_up.shape[1]
    route = w_route.T
    experts = route.shape[0]
    row = lambda v: v.reshape(1, -1)
    message = shape((rows + pad_rows, lanes), bf16)
    stacked = (2 * rows, lanes)
    stack = shape(stacked, bf16)
    hbm = pl.BlockSpec(memory_space=pltpu.HBM)
    whole = pl.BlockSpec(memory_space=pltpu.VMEM)
    kvm, normed, seg = pl.pallas_call(
        keys_kernel,
        out_shape=(message, shape((rows, width), bf16), shape((rows, lanes), f32)),
        in_specs=[hbm] * 5,
        out_specs=(whole,) * 3,
        scratch_shapes=[
            pltpu.VMEM((rows, width), bf16), pltpu.VMEM((width, lanes), bf16), pltpu.VMEM((1, width), f32),
            pltpu.VMEM((1, width), f32), pltpu.VMEM((1, rows), jnp.int32), pltpu.SemaphoreType.DMA((5,)),
        ],
        compiler_params=pltpu.CompilerParams(vmem_limit_bytes=8 * mib),
        cost_estimate=pl.CostEstimate(flops=busy, bytes_accessed=0, transcendentals=0),
    )(tok, w_kv, row(gain_one), row(shift_one), segment_ids)
    spread_out = size == 8 and lax.axis_size("row") == 4
    qm, q_stack, k_stack, v_stack, gates, picks = call(
        queries_kernel,
        (message, stack, stack, stack, shape((rows, lanes), f32), shape((2, rows, lanes), jnp.int32)),
        [], 12 * mib, 1.6,
        normed, kvm, w_query, route, choices[0].T,
    )
    state = (shape(stacked, f32),) * 2
    finished = (shape((rows, lanes), f32), shape(stacked, f32)) + state

    def forward(parts, first, last, *so_far):
        return call(
            functools.partial(forward_kernel, len(parts), first, last), finished if last else state, [], 16 * mib,
            1.4 * len(parts) * parts[0].shape[0], q_stack, seg, kvm, *parts, *so_far,
        )

    if size == 8:
        far_z, near_z, near_y = flip_seq(kvm, 4), flip_seq(kvm, 2), flip_seq(kvm, 1)
        near_y, near_z, far_z, q_stack, kvm = lax.optimization_barrier((near_y, near_z, far_z, q_stack, kvm))
        near = [m[None] for m in (kvm, near_y, near_z, far_z)]
        others = [flip_seq(near_z, 1), flip_seq(far_z, 1), flip_seq(far_z, 2), flip_seq(kvm, 7)]
        others = [m[None] for m in others]
        so_far = forward(near, True, False)
        heads, lse, _, _ = forward(others, False, True, *so_far)
        q_two = after(jnp.stack([qm, flip_seq(qm, 1)]), so_far[0])
        q_far = [flip_seq(q_two, 2), flip_seq(q_two, 4)]
        heads = after(heads, q_two)
    else:
        all_kv = [lax.all_gather(kvm, "seq", axis=0, tiled=False)]
        heads, lse, _, _ = forward(all_kv, True, True)
    piece = gradient_rows(width, hidden)
    gradients = shape((piece * parts_of // 2, width), bf16)
    (
        layer_out, keep, send, grad_mid, dom, do_stack, delta, dlog, grad_route, grad_bup, small_two,
    ) = call(
        functools.partial(middle_kernel, spread_out),
        (
            shape((rows, width), bf16), gradients, gradients, shape((rows, width), f32), shape((rows + stat_rows, lanes), bf16),
            stack, shape(stacked, f32), shape((rows, experts), bf16), shape((experts, width), f32),
            shape((1, hidden), f32), shape((8, width), f32),
        ),
        [
            pltpu.VMEM((rows, width), bf16), pltpu.VMEM((width, rows), bf16), pltpu.VMEM((rows, width), f32),
            pltpu.VMEM((rows, width), f32), pltpu.VMEM((rows, width), f32), pltpu.VMEM((rows, width), bf16),
            pltpu.VMEM((rows, width), f32), pltpu.VMEM((rows, lanes), f32), pltpu.VMEM((rows, width), bf16),
            pltpu.VMEM((rows, lanes), bf16),
        ],
        40 * mib, 15,
        tok, cot, heads, gates, picks, lse, normed, w_out, w_up, row(bias_up), w_down, row(bias_down),
        row(gain_two), row(shift_two),
    )
    results = {}
    extra_part = shape((width // 2, width), bf16)

    def query_back(parts, first, last, *earlier):
        finish = (normed, picks, w_query, dlog, route) if last else ()
        outs = (extra_part, extra_part, shape((rows, width), f32)) if last else ()
        results["query"] = call(
            functools.partial(query_back_kernel, spread_out, len(parts), first, last),
            outs + (shape(stacked, f32),),
            [pltpu.VMEM((rows, width), bf16)] if last else [],
            20 * mib, 1.6 * len(parts) * parts[0].shape[0],
            after(q_stack, *earlier), do_stack, lse, delta, seg, kvm, *parts, *(() if first else results["query"]), *finish,
        )
        return results["query"][-1]

    def key_back(q_parts, do_parts, first, last, *earlier):
        results["key"] = call(
            functools.partial(key_back_kernel, len(q_parts), first, last),
            ((shape((rows, lanes), bf16),) if last else ()) + state,
            [], 20 * mib, 2.1 * len(q_parts) * q_parts[0].shape[0],
            after(k_stack, *earlier), v_stack, seg, kvm, *q_parts, *do_parts, *(() if first else results["key"]),
        )
        return results["key"][-1]

    extra = 5 + hidden // width + experts
    small_rows = extra * (width // lanes) + width
    small_rows = -(-small_rows // 32) * 32

    def finish(*earlier):
        part = shape((small_rows // 2, lanes), bf16)
        return call(
            functools.partial(final_kernel, spread_out),
            (shape((rows, width), f32), part, part),
            [pltpu.VMEM((small_rows, lanes), bf16)], 16 * mib, 2.4,
            tok, normed, results["query"][2], after(results["key"][0], *earlier), grad_mid, w_kv, row(gain_one),
            grad_route, grad_bup, small_two,
        )

    if spread_out:
        send, q_near, q_other = lax.optimization_barrier((send, *q_far))
        q_last = flip_seq(q_other, 2)
        received = flip_row(send, 1)
        d_two = jnp.stack([dom, flip_seq(dom, 1)])
        received = after(received, query_back(near, True, False), q_last)
        upper, lower = hidden // parts_of, piece - hidden // parts_of
        more = width // parts_of
        part = lambda count, rows: shape((count * rows, width), bf16)
        one, one_send, two, two_send = simple(
            after_core_kernel, (part(8, upper),) * 2 + (part(8, lower),) * 2, keep, received
        )
        one_in, two_in = flip_row(one_send, 2), flip_seq(two_send, 1)
        d_other, d_near = flip_seq(d_two, 4), flip_seq(d_two, 2)
        query_back(others, False, True, one, d_two)
        extra, extra_send, _, done = results["query"]
        extra, extra_send = simple(split_kernel, (part(8, more),) * 2, extra, flip_row(extra_send, 1))
        extra_in = flip_row(extra_send, 2)
        done = key_back([q_two], [d_two], True, False, extra, d_near)
        one, one_send, two, two_send = simple(
            after_first_kernel, (part(4, upper + more),) * 2 + (part(4, lower),) * 2,
            one, after(one_in, done), extra, extra_in, two, two_in,
        )
        one_in, two_in = flip_seq(one_send, 1), flip_row(two_send, 2)
        done = key_back([q_near], [d_near], False, False, one)
        sent = simple(after_second_kernel, (part(1, piece + more),) * 4, one, after(one_in, done), two, two_in)
        planes = [flip_seq(sent[i], 2 * i) for i in (1, 2, 3)]
        d_last = flip_seq(after(d_other, sent[0]), 2)
        key_back([q_other], [d_other], False, False, sent[0])
        done = key_back([q_last], [d_last], False, True)
        grad_tokens, *small = finish(done)
        mine = simple(sum_kernel, part(1, piece + more), after(sent[0], small[0]), *planes)
        mine, *small = lax.optimization_barrier((mine, *small))
        arrived = [flip_seq(mine, 2 * i) for i in (1, 2, 3)]
        large, small = finish_sums((mine, arrived), small, hidden)
    else:
        query_back(all_kv, True, True)
        gathered = [lax.all_gather(m, "seq", axis=0, tiled=False) for m in (qm, dom)]
        key_back(gathered[:1], gathered[1:], True, True)
        grad_tokens, *small = finish()
        small = lax.psum(small, ("seq", "row"))
        sums = lax.psum((keep, send, *results["query"][:2]), ("seq", "row"))
        large = []
        upper = hidden // parts_of
        for total, more in zip(sums[:2], sums[2:]):
            cube = total.reshape(4, 2, 2, piece, width)
            more = more.reshape(4, 2, 2, -1, width)
            one = jnp.concatenate([cube[:, :, :, :upper], more], axis=3)
            two = cube[:, :, :, upper:]
            for i in range(2):
                large.append(one[:, :, i].transpose(1, 0, 2, 3).reshape(-1, width))
                large.append(two[:, i].transpose(1, 0, 2, 3).reshape(-1, width))
        done = unpack(False, (0, 1), 0, (large[0], large[1], large[4], large[5]), (), width, hidden)
        done = unpack(False, (0,), 1, large[2:4], done, width, hidden)
        large = unpack(False, (1,), 1, large[6:8], done, width, hidden)
    grad_wkv, grad_route, grad_bup, grad_small = call(
        functools.partial(unpack_small_kernel, spread_out),
        (
            shape((width, lanes), f32), shape((experts, width), f32), shape((1, hidden), f32), shape((8, width), f32),
        ),
        [pltpu.VMEM((small_rows, lanes), f32)], 8 * mib, 0.8, *small,
    )
    grad_up, grad_down, grad_out, grad_wq = large
    return (
        layer_out[None],
        grad_tokens[None],
        grad_wq,
        grad_wkv,
        grad_route.T,
        grad_out,
        grad_up,
        grad_bup.reshape(-1),
        grad_down,
        grad_small[2],
        grad_small[0],
        grad_small[1],
        grad_small[3],
        grad_small[4],
    )


def solution(mesh):
    split_tokens = P("row", "seq", None)
    placed = (split_tokens, split_tokens) + (P(),) * 12 + (split_tokens, P("row", "seq"))
    return jax.shard_map(
        local,
        mesh=mesh,
        in_specs=placed,
        out_specs=(split_tokens, split_tokens) + (P(),) * 12,
        check_vma=False,
    )
```

```python
import functools

import jax
import jax.numpy as jnp
from jax import lax
from jax.experimental import pallas as pl
from jax.experimental.pallas import tpu as pltpu
from jax.sharding import PartitionSpec as P

f32 = jnp.float32
bf16 = jnp.bfloat16
epsilon = 1e-05
lanes = 128
half = 64
chunk = 160
pad_rows = 16
stat_rows = 80
masked = -2e30
lowest = -1e30
feed_step = 256
mib = 1 << 20


def nn(a, b):
    return lax.dot_general(a, b, (((1,), (0,)), ((), ())), preferred_element_type=f32)


def nt(a, b):
    return lax.dot_general(a, b, (((1,), (1,)), ((), ())), preferred_element_type=f32)


def tn(a, b):
    return lax.dot_general(a, b, (((0,), (0,)), ((), ())), preferred_element_type=f32)


def lane_ids(rows):
    return lax.broadcasted_iota(jnp.int32, (rows, lanes), 1)


def swap(values):
    return pltpu.roll(values, half, 1)


def column(row):
    return jnp.transpose(jnp.broadcast_to(row, (lanes, row.shape[1])), (1, 0))


def to_rows(row):
    count = row.shape[1] // lanes
    pieces = [row[:, i * lanes : (i + 1) * lanes] for i in range(count)]
    return jnp.concatenate(pieces + [jnp.zeros((8 - count, lanes), f32)], axis=0)


def from_rows(block, count):
    return jnp.concatenate([block[i : i + 1] for i in range(count)], axis=1)


def wide(values, count):
    return jnp.concatenate([values] * count, axis=1)


def normalized(x):
    centred = x - jnp.mean(x, axis=-1, keepdims=True)
    inverse = lax.rsqrt(jnp.mean(centred * centred, axis=-1, keepdims=True) + epsilon)
    return centred * inverse, inverse


def normalized_back(upstream, unit, inverse, gain):
    scaled = upstream * gain
    inner = (
        scaled
        - jnp.mean(scaled, axis=-1, keepdims=True)
        - unit * jnp.mean(scaled * unit, axis=-1, keepdims=True)
    )
    grad_gain = jnp.sum(upstream * unit, axis=0, keepdims=True)
    return inverse * inner, grad_gain, jnp.sum(upstream, axis=0, keepdims=True)


def row_blocks(rows):
    return [slice(r, r + lanes) for r in range(0, rows, lanes)]


def keys_kernel(tok_in, wkv_in, gain_in, shift_in, seg_in, kvm, n_out, tok, wkv, gain, shift, seg, sems):
    moves = [
        pltpu.make_async_copy(source, target, sems.at[i])
        for i, (source, target) in enumerate(
            ((tok_in, tok), (wkv_in, wkv), (gain_in, gain), (shift_in, shift), (seg_in, seg))
        )
    ]
    for move in moves:
        move.start()
    for move in moves:
        move.wait()
    rows = tok.shape[0]
    for at in row_blocks(rows):
        unit, _ = normalized(tok[at, :].astype(f32))
        normed = (unit * gain[...] + shift[...]).astype(bf16)
        n_out[at, :] = normed
        kvm[at, :] = nn(normed, wkv[...]).astype(bf16)
    seg_row = seg[...].astype(f32)
    ids = to_rows(seg_row)
    line = lax.broadcasted_iota(jnp.int32, (8, lanes), 0)
    ids = jnp.where(line == rows // lanes, seg_row[:, 0:1], ids)
    ids = jnp.where(line == rows // lanes + 1, seg_row[:, rows - 1 : rows], ids)
    ids = jnp.concatenate([ids, jnp.zeros((pad_rows - 8, lanes), f32)], axis=0).astype(bf16)
    kvm[rows : rows + pad_rows, :] = ids


def queries_kernel(
    normed_in, kvm, seg, wq, wroute, choice, qm, q_stack, k_stack, v_stack, gates, picks, seg_out, kvm_out
):
    rows = normed_in.shape[0]
    experts = wroute.shape[0]
    low = lane_ids(lanes) < half
    slot = lax.broadcasted_iota(jnp.int32, (lanes, experts), 1)
    zero = jnp.zeros((lanes, lanes), f32)
    scale = half ** (-0.5)
    for at in row_blocks(rows):
        second_at = slice(rows + at.start, rows + at.stop)
        normed = normed_in[at, :]
        first = column(choice[0:1, at].astype(f32)).astype(jnp.int32)
        second = column(choice[1:2, at].astype(f32)).astype(jnp.int32)
        picks[0, at, :] = first
        picks[1, at, :] = second
        query_all = nn(normed, wq[...])
        one, two = pick_slots(query_all, first, second)
        one = one.astype(bf16).astype(f32) * scale
        two = two.astype(bf16).astype(f32) * scale
        qm[at, :] = jnp.where(low, one, two).astype(bf16)
        q_stack[at, :] = jnp.where(low, one, zero).astype(bf16)
        q_stack[second_at, :] = jnp.where(low, swap(two), zero).astype(bf16)
        seg_out[at, :] = column(seg[:, at].astype(f32))
        kvm_out[at, :] = kvm[at, :]
        kv = kvm[at, :].astype(f32)
        other = swap(kv)
        k_stack[at, :] = jnp.where(low, kv, zero).astype(bf16)
        k_stack[second_at, :] = jnp.where(low, zero, other).astype(bf16)
        v_stack[at, :] = jnp.where(low, other, zero).astype(bf16)
        v_stack[second_at, :] = jnp.where(low, zero, kv).astype(bf16)
        logits = nt(normed, wroute[...])
        picked_one = jnp.sum(jnp.where(slot == first[:, :experts], logits, 0.0), axis=1, keepdims=True)
        picked_two = jnp.sum(jnp.where(slot == second[:, :experts], logits, 0.0), axis=1, keepdims=True)
        top = jnp.maximum(picked_one, picked_two)
        exp_one = jnp.exp(picked_one - top)
        exp_two = jnp.exp(picked_two - top)
        gates[at, :] = jnp.where(low, exp_one, exp_two) / (exp_one + exp_two)
    qm[rows : rows + pad_rows, :] = kvm[rows : rows + pad_rows, :]
    kvm_out[rows : rows + pad_rows, :] = kvm[rows : rows + pad_rows, :]


def pick_slots(values, first, second):
    one = jnp.zeros(first.shape, f32)
    two = jnp.zeros(first.shape, f32)
    first_pair, second_pair = first // 2, second // 2
    for g in range(values.shape[1] // lanes):
        part = values[:, g * lanes : (g + 1) * lanes]
        one = jnp.where(first_pair == g, part, one)
        two = jnp.where(second_pair == g, part, two)
    one = jnp.where(first % 2 == 0, one, swap(one))
    two = jnp.where(second % 2 == 1, two, swap(two))
    return one, two


def id_range(message, rows):
    block = message[rows : rows + pad_rows, :][0:8].astype(f32)
    count = rows // lanes
    return block[count : count + 1], block[count + 1 : count + 2]


def id_row(message, rows):
    block = message[rows : rows + pad_rows, :][0:8].astype(f32)
    return from_rows(block, rows // lanes)


def over_pieces(parts, rows, own, visit):
    own_low, own_high = id_range(own, rows)

    def kind(message):
        low, high = id_range(message, rows)
        meets = jnp.where((low <= own_high) & (high >= own_low), 1.0, 0.0)
        return meets * jnp.where((low == high) & (own_low == own_high), 2.0, 1.0)

    def one(index, i, message, code):
        @pl.when(code == 2)
        def _():
            visit(index, i, message, True)

        @pl.when(code == 1)
        def _():
            visit(index, i, message, False)

    few = [(index, i, part.at[i]) for index, part in enumerate(parts) for i in range(part.shape[0]) if part.shape[0] <= 8]
    if few:
        codes = sum(kind(message) * 4.0**n for n, (_, _, message) in enumerate(few))
        codes = jnp.max(codes).astype(jnp.int32)
    for n, (index, i, message) in enumerate(few):
        one(index, i, message, lax.rem(codes // 4**n, 4))
    for index, part in enumerate(parts):
        if part.shape[0] > 8:

            @pl.loop(0, part.shape[0])
            def _(i, index=index, part=part):
                message = part.at[i]
                one(index, i, message, jnp.max(kind(message)).astype(jnp.int32))


def places(ref, c):
    rows = ref.shape[0] // 2
    return slice(c * chunk, (c + 1) * chunk), slice(rows + c * chunk, rows + (c + 1) * chunk)


def both(ref, c):
    one, two = places(ref, c)
    return jnp.concatenate([ref[one, :], ref[two, :]], axis=0)


def put_both(ref, c, values):
    one, two = places(ref, c)
    ref[one, :] = values[:chunk]
    ref[two, :] = values[chunk:]


def same(seg, c, ids):
    mine = seg[c * chunk : (c + 1) * chunk, :]
    return wide(jnp.concatenate([mine, mine], axis=0), ids.shape[1] // lanes) == ids


def staged(chunks, products, weigh, collect):
    current, ready = products(0), None
    for c in range(chunks):
        following = products(c + 1) if c + 1 < chunks else None
        if ready is not None:
            collect(c - 1, *ready)
        ready = weigh(c, current)
        current = following
    collect(chunks - 1, *ready)


def forward_kernel(piece_count, first, last, stack, seg, own, *rest):
    parts = rest[:piece_count]
    rest = rest[piece_count:]
    if not first:
        total_in, peak_in = rest[:2]
        rest = rest[2:]
    if last:
        heads, lse, total, peak = rest
    else:
        total, peak = rest
    rows = seg.shape[0]
    across = rows // lanes
    if first:
        peak[...] = jnp.full(peak.shape, lowest, f32)
        total[...] = jnp.zeros(total.shape, f32)
    else:
        peak[...] = peak_in[...]
        total[...] = total_in[...]

    def visit(index, i, message, uniform):
        kv = message[0:rows, :]
        low = lane_ids(rows) < half
        values = jnp.where(low, jnp.ones_like(kv), kv)
        if not uniform:
            key_ids = id_row(message, rows)

        def products(c):
            scores = nt(both(stack, c), kv)
            if not uniform:
                scores = jnp.where(same(seg, c, key_ids), scores, masked)
            return scores

        def weigh(c, scores):
            before = both(peak, c)
            now = jnp.maximum(before, jnp.max(scores, axis=1, keepdims=True))
            put_both(peak, c, now)
            return jnp.exp(scores - wide(now, across)).astype(bf16), jnp.exp(before - now)

        def collect(c, weights, factor):
            put_both(total, c, both(total, c) * factor + nn(weights, values))

        staged(rows // chunk, products, weigh, collect)

    over_pieces(parts, rows, own, visit)
    if not last:
        return
    low = lane_ids(lanes) < half
    for at in row_blocks(rows):
        second_at = slice(rows + at.start, rows + at.stop)
        one, two = total[at, :], total[second_at, :]
        one_other, two_other = swap(one), swap(two)
        heads[at, :] = jnp.where(low, one_other, two) / jnp.where(low, one, two_other)
        lse[at, :] = peak[at, :] + jnp.log(jnp.where(low, one, one_other))
        lse[second_at, :] = peak[second_at, :] + jnp.log(jnp.where(low, two, two_other))


def query_back_kernel(spread_out, piece_count, first, last, stack, stack_do, lse, delta, seg, own, *rest):
    parts = rest[:piece_count]
    rest = rest[piece_count:]
    if not first:
        total_in = rest[0]
        rest = rest[1:]
    if last:
        normed, picks, wq, dlog, wroute, keep, send, grad_n, total, spread_keep = rest
    else:
        total = rest[0]
    rows = seg.shape[0]
    across = rows // lanes
    total[...] = jnp.zeros(total.shape, f32) if first else total_in[...]

    def visit(index, i, message, uniform):
        kv = message[0:rows, :]
        if not uniform:
            key_ids = id_row(message, rows)

        def products(c):
            scores = nt(both(stack, c), kv)
            if not uniform:
                scores = jnp.where(same(seg, c, key_ids), scores, masked)
            return scores, nt(both(stack_do, c), kv)

        def weigh(c, pair):
            scores, grad_prob = pair
            prob = jnp.exp(scores - wide(both(lse, c), across))
            return ((prob * (grad_prob - wide(both(delta, c), across))).astype(bf16),)

        def collect(c, grad_scores):
            put_both(total, c, both(total, c) + nn(grad_scores, kv))

        staged(rows // chunk, products, weigh, collect)

    over_pieces(parts, rows, own, visit)
    if not last:
        return
    low = lane_ids(lanes) < half
    scale = half ** (-0.5)
    for at in row_blocks(rows):
        one = total[at, :] * scale
        two = total[slice(rows + at.start, rows + at.stop), :] * scale
        one = jnp.where(low, one, swap(one))
        two = jnp.where(low, two, swap(two))
        spread = spread_slots(one, two, picks[0, at, :], picks[1, at, :], normed.shape[1] // lanes).astype(bf16)
        spread_keep[at, :] = spread
        grad_n[at, :] = nt(spread, wq[...]) + nn(dlog[at, :], wroute[...])
    whole = tn(normed[...], spread_keep[...]).astype(bf16)
    core = place(spread_out)[0]
    count = whole.shape[0] // parts_of
    for i in range(parts_of // 2):
        at = slice(i * count, (i + 1) * count)
        even = whole[2 * i * count : (2 * i + 1) * count]
        odd = whole[(2 * i + 1) * count : (2 * i + 2) * count]
        keep[at, :] = jnp.where(core == 0, even, odd)
        send[at, :] = jnp.where(core == 0, odd, even)


def spread_slots(one, two, first, second, pairs):
    upper = (lane_ids(one.shape[0]) >= half).astype(jnp.int32)
    out = []
    for g in range(pairs):
        expert = 2 * g + upper
        out.append(jnp.where(first == expert, one, jnp.where(second == expert, two, 0.0)))
    return jnp.concatenate(out, axis=1)


def key_back_kernel(piece_count, first, last, keys, values, seg, own, *rest):
    q_parts = rest[:piece_count]
    do_parts = rest[piece_count : 2 * piece_count]
    rest = rest[2 * piece_count :]
    if not first:
        k_in, v_in = rest[:2]
        rest = rest[2:]
    if last:
        grad_kv = rest[0]
        rest = rest[1:]
    total_k, total_v = rest
    rows = seg.shape[0]
    across = rows // lanes
    if first:
        total_k[...] = jnp.zeros(total_k.shape, f32)
        total_v[...] = jnp.zeros(total_v.shape, f32)
    else:
        total_k[...] = k_in[...]
        total_v[...] = v_in[...]

    def visit(index, i, message, uniform):
        queries = message[0:rows, :]
        sent = do_parts[index].at[i]
        grads = sent[0:rows, :]
        stats = sent[rows : rows + stat_rows, :].astype(f32)

        def stat(first, terms):
            block = stats[first * 8 : first * 8 + 8]
            for t in range(1, terms):
                block = block + stats[(first + t) * 8 : (first + t) * 8 + 8]
            return from_rows(block, across)

        lse = (stat(0, 3), stat(3, 3))
        delta = (stat(6, 2), stat(8, 2))
        if not uniform:
            query_ids = id_row(message, rows)

        def spread(pair):
            return jnp.concatenate(
                [jnp.broadcast_to(pair[0], (chunk, rows)), jnp.broadcast_to(pair[1], (chunk, rows))],
                axis=0,
            )

        def products(c):
            scores = nt(both(keys, c), queries)
            if not uniform:
                scores = jnp.where(same(seg, c, query_ids), scores, masked)
            return scores, nt(both(values, c), grads)

        def weigh(c, pair):
            scores, grad_prob = pair
            prob = jnp.exp(scores - spread(lse))
            return prob.astype(bf16), (prob * (grad_prob - spread(delta))).astype(bf16)

        def collect(c, prob, grad_scores):
            put_both(total_v, c, both(total_v, c) + nn(prob, grads))
            put_both(total_k, c, both(total_k, c) + nn(grad_scores, queries))

        staged(rows // chunk, products, weigh, collect)

    over_pieces(q_parts, rows, own, visit)
    if not last:
        return
    low = lane_ids(lanes) < half
    for at in row_blocks(rows):
        second_at = slice(rows + at.start, rows + at.stop)
        key_grad = total_k[at, :] + swap(total_k[second_at, :])
        value_grad = swap(total_v[at, :]) + total_v[second_at, :]
        grad_kv[at, :] = jnp.where(low, key_grad, value_grad).astype(bf16)


def middle_kernel(
    spread_out,
    tok, cot, heads, gates, picks, lse, normed, wout, wup, bup, wdown, bdown, gain, shift,
    layer_out, keep, send, grad_mid, dom, do_stack, delta_out, dlog, grad_route, grad_bup, grad_small,
    second_n, second_t, total_y, total_n, mid_keep, mixed_keep, unit_keep, inverse_keep, low_keep, logit_keep,
):
    rows, width = tok.shape
    hidden = wup.shape[1]
    lane = lane_ids(lanes)
    low = lane < half
    pairs = width // lanes
    for at in row_blocks(rows):
        gated = gates[at, :] * heads[at, :]
        turned = swap(gated)
        mixed = spread_slots(
            jnp.where(low, gated, turned), jnp.where(low, turned, gated), picks[0, at, :], picks[1, at, :], pairs
        ).astype(bf16)
        mixed_keep[at, :] = mixed
        middle = tok[at, :].astype(f32) + nn(mixed, wout[...])
        mid_keep[at, :] = middle
        unit, inverse = normalized(middle)
        unit_keep[at, :] = unit
        inverse_keep[at, :] = jnp.broadcast_to(inverse, (lanes, lanes))
        n_two = (unit * gain[...] + shift[...]).astype(bf16)
        second_n[at, :] = n_two
        second_t[:, at] = n_two.T
    total_y[...] = jnp.zeros(total_y.shape, f32)
    total_n[...] = jnp.zeros(total_n.shape, f32)
    step = feed_step
    root = 0.7978845608028654
    cubic = 0.044715
    core = place(spread_out)[0]
    down_rows = hidden // parts_of
    up_rows = width // parts_of
    piece = gradient_rows(width, hidden)

    def put(index, at_row, at_lane, even, odd):
        count, across = even.shape
        start = index * piece + at_row
        target = (slice(start, start + count), slice(at_lane, at_lane + across))
        keep[target] = jnp.where(core == 0, even, odd)
        send[target] = jnp.where(core == 0, odd, even)

    def products(f):
        at = slice(f * step, (f + 1) * step)
        return nn(second_n[...], wup[:, at]) + bup[:, at], nt(cot[...], wdown[at, :])

    def bend(f, pair):
        pre, grad_act = pair
        square = pre * pre
        bent = jnp.tanh(pre * (root + (root * cubic) * square))
        rise = 0.5 + 0.5 * bent
        act = (pre * rise).astype(bf16)
        slope = rise + (pre * (rise * (1.0 - bent))) * (root + (3.0 * root * cubic) * square)
        grad_pre = (grad_act * slope).astype(bf16)
        grad_bup[:, f * step : (f + 1) * step] = jnp.sum(grad_pre.astype(f32), axis=0, keepdims=True)
        return act, grad_pre

    def collect(f, act, grad_pre):
        at = slice(f * step, (f + 1) * step)
        total_y[...] += nn(act, wdown[at, :])
        total_n[...] += nt(grad_pre, wup[:, at])
        grad_down = tn(act, cot[...]).astype(bf16)
        for i in range(step // (2 * down_rows)):
            pair = grad_down[2 * i * down_rows : 2 * (i + 1) * down_rows]
            put(f * (step // (2 * down_rows)) + i, 0, 0, pair[:down_rows], pair[down_rows:])
        grad_up = nn(second_t[...], grad_pre).astype(bf16)
        block_of, at_lane = divmod(f * step, width)
        for i in range(parts_of // 2):
            pair = grad_up[2 * i * up_rows : 2 * (i + 1) * up_rows]
            put(i, down_rows + block_of * up_rows, at_lane, pair[:up_rows], pair[up_rows:])

    staged(hidden // step, products, bend, collect)

    sums = [jnp.zeros((1, width), f32)] * 3
    experts = dlog.shape[1]
    stats = [[], [], [], []]
    zero = jnp.zeros((lanes, lanes), f32)
    for at in row_blocks(rows):
        second_at = slice(rows + at.start, rows + at.stop)
        first, second = picks[0, at, :], picks[1, at, :]
        layer_out[at, :] = (mid_keep[at, :] + total_y[at, :] + bdown[...]).astype(bf16)
        unit = unit_keep[at, :]
        back, grad_gain, grad_shift = normalized_back(total_n[at, :], unit, wide(inverse_keep[at, :], pairs), gain[...])
        dy = cot[at, :].astype(f32)
        grad_middle = dy + back
        grad_mid[at, :] = grad_middle
        sums = [a + b for a, b in zip(sums, (jnp.sum(dy, axis=0, keepdims=True), grad_gain, grad_shift))]
        grad_low = grad_middle.astype(bf16)
        low_keep[at, :] = grad_low
        one, two = pick_slots(nt(grad_low, wout[...]), first, second)
        slots = jnp.where(low, one, two)
        head_values = heads[at, :]
        gate = gates[at, :]
        grad_heads = (gate * slots).astype(bf16)
        dom[at, :] = grad_heads
        carried = grad_heads.astype(f32)
        turned = swap(carried)
        do_stack[at, :] = jnp.where(low, zero, turned).astype(bf16)
        do_stack[second_at, :] = jnp.where(low, zero, carried).astype(bf16)
        gated_grad = slots * head_values
        gate_one = jnp.sum(jnp.where(low, gated_grad, 0.0), axis=1, keepdims=True)
        gate_two = jnp.sum(jnp.where(low, 0.0, gated_grad), axis=1, keepdims=True)
        grad_gate = jnp.where(low, gate_one, gate_two)
        weighted = gate * grad_gate
        grad_logit = gate * (grad_gate - (weighted + swap(weighted)))
        logit_other = swap(grad_logit)
        logit_one = jnp.where(low, grad_logit, logit_other)
        logit_two = jnp.where(low, logit_other, grad_logit)
        grad_logits = jnp.where(lane == first, logit_one, jnp.where(lane == second, logit_two, 0.0)).astype(bf16)
        logit_keep[at, :] = grad_logits
        dlog[at, :] = grad_logits[:, :experts]
        carried = carried * head_values
        delta_one = jnp.broadcast_to(jnp.sum(jnp.where(low, carried, 0.0), axis=1, keepdims=True), (lanes, lanes))
        delta_two = jnp.broadcast_to(jnp.sum(jnp.where(low, 0.0, carried), axis=1, keepdims=True), (lanes, lanes))
        delta_out[at, :] = delta_one
        delta_out[second_at, :] = delta_two
        for store, values in zip(stats, (lse[at, :], lse[second_at, :], delta_one, delta_two)):
            store.append(jnp.transpose(values, (1, 0))[0:1, :])
    blocks = []
    for store, terms in zip(stats, (3, 3, 2, 2)):
        rest = jnp.concatenate(store + [jnp.zeros((8 - len(store), lanes), f32)], axis=0)
        for _ in range(terms):
            part = rest.astype(bf16).astype(f32)
            blocks.append(part)
            rest = rest - part
    dom[rows : rows + stat_rows, :] = jnp.concatenate(blocks, axis=0).astype(bf16)
    grad_small[...] = jnp.concatenate(sums + [jnp.zeros((5, width), f32)], axis=0)
    grad_route[...] = tn(logit_keep[...], normed[...])[:experts, :]
    grad_out = tn(mixed_keep[...], low_keep[...]).astype(bf16)
    for i in range(parts_of // 2):
        pair = grad_out[2 * i * up_rows : 2 * (i + 1) * up_rows]
        put(i, piece - up_rows, 0, pair[:up_rows], pair[up_rows:])


def final_kernel(
    spread_out, tok, normed, grad_n, grad_kv, grad_mid, wkv, gain, grad_route, grad_bup, small_two,
    grad_tokens, keep, send, whole,
):
    width = tok.shape[1]
    whole[0:width, :] = tn(normed[...], grad_kv[...]).astype(bf16)
    grad_gain = grad_shift = jnp.zeros((1, width), f32)
    for at in row_blocks(tok.shape[0]):
        upstream = grad_n[at, :] + nt(grad_kv[at, :], wkv[...])
        unit, inverse = normalized(tok[at, :].astype(f32))
        back, more_gain, more_shift = normalized_back(upstream, unit, inverse, gain[...])
        grad_tokens[at, :] = grad_mid[at, :] + back
        grad_gain, grad_shift = grad_gain + more_gain, grad_shift + more_shift
    rows = [grad_gain, grad_shift] + [small_two[i : i + 1, :] for i in range(3)]
    rows += [grad_bup[:, i : i + width] for i in range(0, grad_bup.shape[1], width)]
    rows += [grad_route[i : i + 1, :] for i in range(grad_route.shape[0])]
    small = jnp.concatenate([row[:, i : i + lanes] for row in rows for i in range(0, width, lanes)], axis=0)
    last = whole.shape[0] - width
    small = jnp.concatenate([small, jnp.zeros((last - small.shape[0], lanes), f32)], axis=0)
    whole[width:, :] = small.astype(bf16)
    core = place(spread_out)[0]
    piece = keep.shape[0]
    keep[...] = whole[block(core, piece), :]
    send[...] = whole[block(1 - core, piece), :]


parts_of = 32


def place(spread_out):
    if not spread_out:
        return 0, 0, 0, 0
    row, seq = lax.axis_index("row"), lax.axis_index("seq")
    return lax.rem(row, 2), row // 2, lax.rem(seq, 2), seq // 2


def gradient_rows(width, hidden):
    return hidden // parts_of + (hidden // width + 1) * (width // parts_of)


def block(index, count):
    return pl.ds(pl.multiple_of(index * count, 16), count)


def plus(*refs):
    def get(at):
        total = refs[0][at].astype(f32)
        for ref in refs[1:]:
            total = total + ref[at].astype(f32)
        return total.astype(bf16)

    return get


def after_core_kernel(keep, received, one_keep, one_send, two_keep, two_send):
    _, x, y, _ = place(True)
    piece, upper, lower = keep.shape[0] // 16, one_keep.shape[0] // 8, two_keep.shape[0] // 8
    total = plus(keep, received)

    def part(index, offset, count):
        return total((pl.ds(pl.multiple_of(index * piece + offset, 16), count), slice(None)))

    for zy in range(8):
        here = slice(zy * upper, (zy + 1) * upper)
        one_keep[here, :] = part(zy * 2 + x, 0, upper)
        one_send[here, :] = part(zy * 2 + 1 - x, 0, upper)
    for z in range(4):
        for at_x in range(2):
            here = slice((z * 2 + at_x) * lower, (z * 2 + at_x + 1) * lower)
            two_keep[here, :] = part((z * 2 + y) * 2 + at_x, upper, lower)
            two_send[here, :] = part((z * 2 + 1 - y) * 2 + at_x, upper, lower)


def split_kernel(keep, received, kept, sent):
    x = place(True)[1]
    piece = kept.shape[0] // 8
    total = plus(keep, received)
    for i in range(8):
        here = slice(i * piece, (i + 1) * piece)
        kept[here, :] = total((block(i * 2 + x, piece), slice(None)))
        sent[here, :] = total((block(i * 2 + 1 - x, piece), slice(None)))


def after_first_kernel(one, one_in, extra, extra_in, two, two_in, one_keep, one_send, two_keep, two_send):
    _, x, y, _ = place(True)
    upper = one.shape[0] // 8
    for total, mine, kept, sent, piece, offset in (
        (plus(one, one_in), y, one_keep, one_send, upper, 0),
        (plus(extra, extra_in), y, one_keep, one_send, extra.shape[0] // 8, upper),
        (plus(two, two_in), x, two_keep, two_send, two.shape[0] // 8, 0),
    ):
        stride = kept.shape[0] // 4
        for z in range(4):
            here = slice(z * stride + offset, z * stride + offset + piece)
            kept[here, :] = total((block(z * 2 + mine, piece), slice(None)))
            sent[here, :] = total((block(z * 2 + 1 - mine, piece), slice(None)))


def after_second_kernel(one, one_in, two, two_in, *outs):
    z = place(True)[3]
    at = 0
    for total, count in ((plus(one, one_in), one.shape[0] // 4), (plus(two, two_in), two.shape[0] // 4)):
        for i, out in enumerate(outs):
            out[at : at + count, :] = total((block(z ^ i, count), slice(None)))
        at += count


def sum_kernel(*refs):
    refs[-1][...] = plus(*refs[:-1])(Ellipsis)


def join_halves_kernel(*refs):
    z = place(True)[3]
    one, two = refs[4:]
    upper, lower = one.shape[0] // 4, two.shape[0] // 4
    for i in range(4):
        one[block(z ^ i, upper), :] = refs[i][:upper, :]
        two[block(z ^ i, lower), :] = refs[i][upper:, :]


def unpack_kernel(spread_out, turns, outer, fresh, *refs):
    core, x, y, _ = place(spread_out)
    count = 2 * len(turns)
    parts, refs = refs[:count], refs[count if fresh else count + 4 :]
    outs, stages, sems = refs[:4], refs[4:8], refs[8]
    grad_up, grad_down, grad_out, grad_wq = outs
    width, hidden = grad_up.shape
    down_rows, up_rows = hidden // parts_of, width // parts_of
    moves = []

    def send(stage, start, rows, out, device):
        target = out.at[block(device, rows), :]
        moves.append(pltpu.make_async_copy(stage.at[start : start + rows, :], target, sems.at[len(moves)]))
        moves[-1].start()

    at = 0
    for n, turn in enumerate(turns):
        one, two = parts[2 * n : 2 * n + 2]
        for inner in range(2):
            for z in range(4):
                row, low, high = inner * 4 + z, at * down_rows, at * up_rows
                at += 1
                device = ((z * 2 + (y ^ inner)) * 2 + (x ^ outer)) * 2 + (core ^ turn)
                base = row * (down_rows + up_rows)
                stages[1][low : low + down_rows, :] = one[base : base + down_rows, :].astype(f32)
                send(stages[1], low, down_rows, grad_down, device)
                base += down_rows
                stages[3][high : high + up_rows, :] = one[base : base + up_rows, :].astype(f32)
                send(stages[3], high, up_rows, grad_wq, device)
                device = ((z * 2 + (y ^ outer)) * 2 + (x ^ inner)) * 2 + (core ^ turn)
                across = hidden // width
                base = row * (across + 1) * up_rows
                for c in range(across):
                    value = two[base + c * up_rows : base + (c + 1) * up_rows, :]
                    stages[0][high : high + up_rows, c * width : (c + 1) * width] = value.astype(f32)
                send(stages[0], high, up_rows, grad_up, device)
                base += across * up_rows
                stages[2][high : high + up_rows, :] = two[base : base + up_rows, :].astype(f32)
                send(stages[2], high, up_rows, grad_out, device)
    for move in moves:
        move.wait()


def unpack(spread_out, turns, outer, parts, so_far, width, hidden):
    outs = (shape((width, hidden), f32), shape((hidden, width), f32)) + (shape((width, width), f32),) * 2
    share = 4 // len(turns)
    hbm = pl.BlockSpec(memory_space=pltpu.HBM)
    whole = pl.BlockSpec(memory_space=pltpu.VMEM)
    return pl.pallas_call(
        functools.partial(unpack_kernel, spread_out, turns, outer, not so_far),
        out_shape=outs,
        in_specs=[whole] * len(parts) + [hbm] * len(so_far),
        out_specs=(hbm,) * 4,
        scratch_shapes=[pltpu.VMEM((out.shape[0] // share, out.shape[1]), f32) for out in outs]
        + [pltpu.SemaphoreType.DMA((32 * len(turns),))],
        input_output_aliases={len(parts) + i: i for i in range(len(so_far))},
        compiler_params=pltpu.CompilerParams(vmem_limit_bytes=16 * mib),
        cost_estimate=pl.CostEstimate(flops=2 * busy, bytes_accessed=0, transcendentals=0),
    )(*parts, *so_far)


def flip_row(x, mask):
    return lax.ppermute(x, "row", [(i, i ^ mask) for i in range(4)])


def flip_seq(x, mask):
    return lax.ppermute(x, "seq", [(i, i ^ mask) for i in range(8)])


def simple(kernel, outs, *operands):
    return call(kernel, outs, [], 20 * mib, 0.5, *operands)


def add(a, b):
    return (a.astype(f32) + b.astype(f32)).astype(bf16)


def finish_sums(large, small, hidden):
    mine, arrived = large
    keep, send = small
    count, width = mine.shape
    total = add(keep, after(flip_row(send, 1), mine))
    part = shape((2 * count, width), bf16)
    one, two = simple(join_halves_kernel, (part,) * 2, mine, *arrived)
    one_in, two_in = flip_seq(one, 1), flip_row(two, 2)
    total = add(total, after(flip_row(total, 2), one))
    one, two = jnp.concatenate([one, one_in]), jnp.concatenate([two, two_in])
    one_in, two_in = flip_row(one, 2), flip_seq(two, 1)
    one_other, two_other = flip_row(one, 1), flip_row(two, 1)
    total = add(total, after(flip_seq(total, 1), one, two))
    done = unpack(True, (0, 1), 0, (one, two, one_other, two_other), (), width, hidden)
    total = add(total, flip_seq(total, 2))
    total = add(total, after(flip_seq(total, 4), done[3]))
    one_in = after(one_in, total)
    other = flip_row(total, 1)
    one_other, two_other = flip_row(one_in, 1), flip_row(two_in, 1)
    done = unpack(True, (0,), 1, (one_in, two_in), done, width, hidden)
    done = unpack(True, (1,), 1, (one_other, two_other), done, width, hidden)
    return done, (total, other)


def unpack_small_kernel(spread_out, mine, other, grad_wkv, grad_route, grad_bup, grad_small, whole):
    core = place(spread_out)[0]
    piece = mine.shape[0]
    whole[block(core, piece), :] = mine[...].astype(f32)
    whole[block(1 - core, piece), :] = other[...].astype(f32)
    width = grad_wkv.shape[0]
    across = width // lanes
    grad_wkv[...] = whole[0:width, :]
    at = width
    for i in range(5):
        for g in range(across):
            grad_small[i : i + 1, g * lanes : (g + 1) * lanes] = whole[at : at + 1, :]
            at += 1
    for g in range(grad_bup.shape[1] // lanes):
        grad_bup[:, g * lanes : (g + 1) * lanes] = whole[at : at + 1, :]
        at += 1
    for i in range(grad_route.shape[0]):
        for g in range(across):
            grad_route[i : i + 1, g * lanes : (g + 1) * lanes] = whole[at : at + 1, :]
            at += 1


busy = 400_000_000


def call(kernel, out_shape, scratch, limit, time, *operands):
    whole = pl.BlockSpec(memory_space=pltpu.VMEM)
    return pl.pallas_call(
        kernel,
        out_shape=out_shape,
        in_specs=[whole] * len(operands),
        out_specs=jax.tree.map(lambda _: whole, out_shape),
        scratch_shapes=scratch,
        compiler_params=pltpu.CompilerParams(vmem_limit_bytes=limit),
        cost_estimate=pl.CostEstimate(flops=int(time * busy), bytes_accessed=0, transcendentals=0),
    )(*operands)


def shape(dims, dtype):
    return jax.ShapeDtypeStruct(tuple(dims), dtype)


def after(value, *earlier):
    return lax.optimization_barrier((value,) + earlier)[0]


def local(
    tokens, cotangent, w_query, w_kv, w_route, w_out, w_up, bias_up, w_down, bias_down,
    gain_one, shift_one, gain_two, shift_two, choices, segment_ids,
):
    size = lax.axis_size("seq")
    tok, cot = tokens[0], cotangent[0]
    rows, width = tok.shape
    hidden = w_up.shape[1]
    route = w_route.T
    experts = route.shape[0]
    row = lambda v: v.reshape(1, -1)
    message = shape((rows + pad_rows, lanes), bf16)
    stacked = (2 * rows, lanes)
    stack = shape(stacked, bf16)
    hbm = pl.BlockSpec(memory_space=pltpu.HBM)
    whole = pl.BlockSpec(memory_space=pltpu.VMEM)
    sent_keys, normed = pl.pallas_call(
        keys_kernel,
        out_shape=(message, shape((rows, width), bf16)),
        in_specs=[hbm] * 5,
        out_specs=(whole,) * 2,
        scratch_shapes=[
            pltpu.VMEM((rows, width), bf16), pltpu.VMEM((width, lanes), bf16), pltpu.VMEM((1, width), f32),
            pltpu.VMEM((1, width), f32), pltpu.VMEM((1, rows), jnp.int32), pltpu.SemaphoreType.DMA((5,)),
        ],
        compiler_params=pltpu.CompilerParams(vmem_limit_bytes=60 * mib),
        cost_estimate=pl.CostEstimate(flops=busy, bytes_accessed=0, transcendentals=0),
    )(tok, w_kv, row(gain_one), row(shift_one), segment_ids)
    spread_out = size == 8 and lax.axis_size("row") == 4
    qm, q_stack, k_stack, v_stack, gates, picks, seg, kvm = call(
        queries_kernel,
        (
            message, stack, stack, stack, shape((rows, lanes), f32), shape((2, rows, lanes), jnp.int32),
            shape((rows, lanes), f32), message,
        ),
        [], 12 * mib, 1.6,
        normed, sent_keys, segment_ids, w_query, route, choices[0].T,
    )
    state = (shape(stacked, f32),) * 2
    finished = (shape((rows, lanes), f32), shape(stacked, f32)) + state

    def forward(parts, first, last, *so_far):
        return call(
            functools.partial(forward_kernel, len(parts), first, last), finished if last else state, [], 16 * mib,
            1.4 * len(parts) * parts[0].shape[0], q_stack, seg, kvm, *parts, *so_far,
        )

    if size == 8:
        far_z, near_z, near_y = flip_seq(sent_keys, 4), flip_seq(sent_keys, 2), flip_seq(sent_keys, 1)
        near_y, near_z, far_z, q_stack, kvm = lax.optimization_barrier((near_y, near_z, far_z, q_stack, kvm))
        near = [m[None] for m in (kvm, near_y, near_z, far_z)]
        others = [flip_seq(near_z, 1), flip_seq(far_z, 1), flip_seq(far_z, 2), flip_seq(after(sent_keys, far_z), 7)]
        others = [m[None] for m in others]
        so_far = forward(near, True, False)
        heads, lse, _, _ = forward(others, False, True, *so_far)
        q_two = jnp.stack([qm, after(flip_seq(qm, 1), so_far[0])])
        q_far = [flip_seq(q_two, 2), flip_seq(q_two, 4)]
        heads = after(heads, q_two)
    else:
        all_kv = [lax.all_gather(kvm, "seq", axis=0, tiled=False)]
        heads, lse, _, _ = forward(all_kv, True, True)
    piece = gradient_rows(width, hidden)
    gradients = shape((piece * parts_of // 2, width), bf16)
    (
        layer_out, keep, send, grad_mid, dom, do_stack, delta, dlog, grad_route, grad_bup, small_two,
    ) = call(
        functools.partial(middle_kernel, spread_out),
        (
            shape((rows, width), bf16), gradients, gradients, shape((rows, width), f32), shape((rows + stat_rows, lanes), bf16),
            stack, shape(stacked, f32), shape((rows, experts), bf16), shape((experts, width), f32),
            shape((1, hidden), f32), shape((8, width), f32),
        ),
        [
            pltpu.VMEM((rows, width), bf16), pltpu.VMEM((width, rows), bf16), pltpu.VMEM((rows, width), f32),
            pltpu.VMEM((rows, width), f32), pltpu.VMEM((rows, width), f32), pltpu.VMEM((rows, width), bf16),
            pltpu.VMEM((rows, width), f32), pltpu.VMEM((rows, lanes), f32), pltpu.VMEM((rows, width), bf16),
            pltpu.VMEM((rows, lanes), bf16),
        ],
        40 * mib, 15,
        tok, cot, heads, gates, picks, lse, normed, w_out, w_up, row(bias_up), w_down, row(bias_down),
        row(gain_two), row(shift_two),
    )
    results = {}
    extra_part = shape((width // 2, width), bf16)

    def query_back(parts, first, last, *earlier):
        finish = (normed, picks, w_query, dlog, route) if last else ()
        outs = (extra_part, extra_part, shape((rows, width), f32)) if last else ()
        results["query"] = call(
            functools.partial(query_back_kernel, spread_out, len(parts), first, last),
            outs + (shape(stacked, f32),),
            [pltpu.VMEM((rows, width), bf16)] if last else [],
            20 * mib, 1.6 * len(parts) * parts[0].shape[0],
            after(q_stack, *earlier), do_stack, lse, delta, seg, kvm, *parts, *(() if first else results["query"]), *finish,
        )
        return results["query"][-1]

    def key_back(q_parts, do_parts, first, last, *earlier):
        results["key"] = call(
            functools.partial(key_back_kernel, len(q_parts), first, last),
            ((shape((rows, lanes), bf16),) if last else ()) + state,
            [], 20 * mib, 2.1 * len(q_parts) * q_parts[0].shape[0],
            after(k_stack, *earlier), v_stack, seg, kvm, *q_parts, *do_parts, *(() if first else results["key"]),
        )
        return results["key"][-1]

    extra = 5 + hidden // width + experts
    small_rows = extra * (width // lanes) + width
    small_rows = -(-small_rows // 32) * 32

    def finish(*earlier):
        part = shape((small_rows // 2, lanes), bf16)
        return call(
            functools.partial(final_kernel, spread_out),
            (shape((rows, width), f32), part, part),
            [pltpu.VMEM((small_rows, lanes), bf16)], 16 * mib, 2.4,
            tok, normed, results["query"][2], after(results["key"][0], *earlier), grad_mid, w_kv, row(gain_one),
            grad_route, grad_bup, small_two,
        )

    if spread_out:
        send, q_near, q_other = lax.optimization_barrier((send, *q_far))
        q_last = flip_seq(q_other, 2)
        received = flip_row(send, 1)
        d_two = jnp.stack([dom, flip_seq(dom, 1)])
        received = after(received, query_back(near, True, False))
        upper, lower = hidden // parts_of, piece - hidden // parts_of
        more = width // parts_of
        part = lambda count, rows: shape((count * rows, width), bf16)
        one, one_send, two, two_send = simple(
            after_core_kernel, (part(8, upper),) * 2 + (part(8, lower),) * 2, keep, received
        )
        one_in, two_in = flip_row(one_send, 2), flip_seq(two_send, 1)
        d_other, d_near = flip_seq(d_two, 4), flip_seq(d_two, 2)
        query_back(others, False, True, one, d_two, q_last)
        extra, extra_send, _, done = results["query"]
        extra, extra_send = simple(split_kernel, (part(8, more),) * 2, extra, flip_row(extra_send, 1))
        extra_in = flip_row(extra_send, 2)
        done = key_back([q_two], [d_two], True, False, extra, d_near)
        one, one_send, two, two_send = simple(
            after_first_kernel, (part(4, upper + more),) * 2 + (part(4, lower),) * 2,
            one, after(one_in, done), extra, extra_in, two, two_in,
        )
        one_in, two_in = flip_seq(one_send, 1), flip_row(two_send, 2)
        done = key_back([q_near], [d_near], False, False, one)
        d_last = flip_seq(after(d_other, done), 2)
        sent = simple(after_second_kernel, (part(1, piece + more),) * 4, one, after(one_in, done), two, two_in)
        planes = [flip_seq(sent[i], 2 * i) for i in (1, 2, 3)]
        key_back([q_other], [d_other], False, False, sent[0])
        done = key_back([q_last], [d_last], False, True)
        grad_tokens, *small = finish(done)
        mine = simple(sum_kernel, part(1, piece + more), after(sent[0], small[0]), *planes)
        arrived = [flip_seq(mine, 2 * i) for i in (1, 2, 3)]
        large, small = finish_sums((mine, arrived), small, hidden)
    else:
        query_back(all_kv, True, True)
        gathered = [lax.all_gather(m, "seq", axis=0, tiled=False) for m in (qm, dom)]
        key_back(gathered[:1], gathered[1:], True, True)
        grad_tokens, *small = finish()
        small = lax.psum(small, ("seq", "row"))
        sums = lax.psum((keep, send, *results["query"][:2]), ("seq", "row"))
        large = []
        upper = hidden // parts_of
        for total, more in zip(sums[:2], sums[2:]):
            cube = total.reshape(4, 2, 2, piece, width)
            more = more.reshape(4, 2, 2, -1, width)
            one = jnp.concatenate([cube[:, :, :, :upper], more], axis=3)
            two = cube[:, :, :, upper:]
            for i in range(2):
                large.append(one[:, :, i].transpose(1, 0, 2, 3).reshape(-1, width))
                large.append(two[:, i].transpose(1, 0, 2, 3).reshape(-1, width))
        done = unpack(False, (0, 1), 0, (large[0], large[1], large[4], large[5]), (), width, hidden)
        done = unpack(False, (0,), 1, large[2:4], done, width, hidden)
        large = unpack(False, (1,), 1, large[6:8], done, width, hidden)
    grad_wkv, grad_route, grad_bup, grad_small = call(
        functools.partial(unpack_small_kernel, spread_out),
        (
            shape((width, lanes), f32), shape((experts, width), f32), shape((1, hidden), f32), shape((8, width), f32),
        ),
        [pltpu.VMEM((small_rows, lanes), f32)], 8 * mib, 0.8, *small,
    )
    grad_up, grad_down, grad_out, grad_wq = large
    return (
        layer_out[None],
        grad_tokens[None],
        grad_wq,
        grad_wkv,
        grad_route.T,
        grad_out,
        grad_up,
        grad_bup.reshape(-1),
        grad_down,
        grad_small[2],
        grad_small[0],
        grad_small[1],
        grad_small[3],
        grad_small[4],
    )


def solution(mesh):
    split_tokens = P("row", "seq", None)
    placed = (split_tokens, split_tokens) + (P(),) * 12 + (split_tokens, P("row", "seq"))
    return jax.shard_map(
        local,
        mesh=mesh,
        in_specs=placed,
        out_specs=(split_tokens, split_tokens) + (P(),) * 12,
        check_vma=False,
    )
```

```python
import functools

import jax
import jax.numpy as jnp
from jax import lax
from jax.experimental import pallas as pl
from jax.experimental.pallas import tpu as pltpu
from jax.sharding import PartitionSpec as P

f32 = jnp.float32
bf16 = jnp.bfloat16
epsilon = 1e-05
lanes = 128
half = 64
chunk = 160
pad_rows = 16
stat_rows = 80
masked = -2e30
lowest = -1e30
feed_step = 256
mib = 1 << 20


def nn(a, b):
    return lax.dot_general(a, b, (((1,), (0,)), ((), ())), preferred_element_type=f32)


def nt(a, b):
    return lax.dot_general(a, b, (((1,), (1,)), ((), ())), preferred_element_type=f32)


def tn(a, b):
    return lax.dot_general(a, b, (((0,), (0,)), ((), ())), preferred_element_type=f32)


def lane_ids(rows):
    return lax.broadcasted_iota(jnp.int32, (rows, lanes), 1)


def swap(values):
    return pltpu.roll(values, half, 1)


def column(row):
    return jnp.transpose(jnp.broadcast_to(row, (lanes, row.shape[1])), (1, 0))


def to_rows(row):
    count = row.shape[1] // lanes
    pieces = [row[:, i * lanes : (i + 1) * lanes] for i in range(count)]
    return jnp.concatenate(pieces + [jnp.zeros((8 - count, lanes), f32)], axis=0)


def from_rows(block, count):
    return jnp.concatenate([block[i : i + 1] for i in range(count)], axis=1)


def wide(values, count):
    return jnp.concatenate([values] * count, axis=1)


def normalized(x):
    centred = x - jnp.mean(x, axis=-1, keepdims=True)
    inverse = lax.rsqrt(jnp.mean(centred * centred, axis=-1, keepdims=True) + epsilon)
    return centred * inverse, inverse


def normalized_back(upstream, unit, inverse, gain):
    scaled = upstream * gain
    inner = (
        scaled
        - jnp.mean(scaled, axis=-1, keepdims=True)
        - unit * jnp.mean(scaled * unit, axis=-1, keepdims=True)
    )
    grad_gain = jnp.sum(upstream * unit, axis=0, keepdims=True)
    return inverse * inner, grad_gain, jnp.sum(upstream, axis=0, keepdims=True)


def row_blocks(rows):
    return [slice(r, r + lanes) for r in range(0, rows, lanes)]


def keys_kernel(tok_in, wkv_in, gain_in, shift_in, seg_in, kvm, n_out, tok, wkv, gain, shift, seg, sems):
    moves = [
        pltpu.make_async_copy(source, target, sems.at[i])
        for i, (source, target) in enumerate(
            ((tok_in, tok), (wkv_in, wkv), (gain_in, gain), (shift_in, shift), (seg_in, seg))
        )
    ]
    for move in moves:
        move.start()
    for move in moves:
        move.wait()
    rows = tok.shape[0]
    for at in row_blocks(rows):
        unit, _ = normalized(tok[at, :].astype(f32))
        normed = (unit * gain[...] + shift[...]).astype(bf16)
        n_out[at, :] = normed
        kvm[at, :] = nn(normed, wkv[...]).astype(bf16)
    seg_row = seg[...].astype(f32)
    ids = to_rows(seg_row)
    line = lax.broadcasted_iota(jnp.int32, (8, lanes), 0)
    ids = jnp.where(line == rows // lanes, seg_row[:, 0:1], ids)
    ids = jnp.where(line == rows // lanes + 1, seg_row[:, rows - 1 : rows], ids)
    ids = jnp.concatenate([ids, jnp.zeros((pad_rows - 8, lanes), f32)], axis=0).astype(bf16)
    kvm[rows : rows + pad_rows, :] = ids


def queries_kernel(
    normed_in, kvm, seg, wq, wroute, choice, qm, q_stack, k_stack, v_stack, gates, picks, seg_out, kvm_out
):
    rows = normed_in.shape[0]
    experts = wroute.shape[0]
    low = lane_ids(lanes) < half
    slot = lax.broadcasted_iota(jnp.int32, (lanes, experts), 1)
    zero = jnp.zeros((lanes, lanes), f32)
    scale = half ** (-0.5)
    for at in row_blocks(rows):
        second_at = slice(rows + at.start, rows + at.stop)
        normed = normed_in[at, :]
        first = column(choice[0:1, at].astype(f32)).astype(jnp.int32)
        second = column(choice[1:2, at].astype(f32)).astype(jnp.int32)
        picks[0, at, :] = first
        picks[1, at, :] = second
        query_all = nn(normed, wq[...])
        one, two = pick_slots(query_all, first, second)
        one = one.astype(bf16).astype(f32) * scale
        two = two.astype(bf16).astype(f32) * scale
        qm[at, :] = jnp.where(low, one, two).astype(bf16)
        q_stack[at, :] = jnp.where(low, one, zero).astype(bf16)
        q_stack[second_at, :] = jnp.where(low, swap(two), zero).astype(bf16)
        seg_out[at, :] = column(seg[:, at].astype(f32))
        kvm_out[at, :] = kvm[at, :]
        kv = kvm[at, :].astype(f32)
        other = swap(kv)
        k_stack[at, :] = jnp.where(low, kv, zero).astype(bf16)
        k_stack[second_at, :] = jnp.where(low, zero, other).astype(bf16)
        v_stack[at, :] = jnp.where(low, other, zero).astype(bf16)
        v_stack[second_at, :] = jnp.where(low, zero, kv).astype(bf16)
        logits = nt(normed, wroute[...])
        picked_one = jnp.sum(jnp.where(slot == first[:, :experts], logits, 0.0), axis=1, keepdims=True)
        picked_two = jnp.sum(jnp.where(slot == second[:, :experts], logits, 0.0), axis=1, keepdims=True)
        top = jnp.maximum(picked_one, picked_two)
        exp_one = jnp.exp(picked_one - top)
        exp_two = jnp.exp(picked_two - top)
        gates[at, :] = jnp.where(low, exp_one, exp_two) / (exp_one + exp_two)
    qm[rows : rows + pad_rows, :] = kvm[rows : rows + pad_rows, :]
    kvm_out[rows : rows + pad_rows, :] = kvm[rows : rows + pad_rows, :]


def pick_slots(values, first, second):
    one = jnp.zeros(first.shape, f32)
    two = jnp.zeros(first.shape, f32)
    first_pair, second_pair = first // 2, second // 2
    for g in range(values.shape[1] // lanes):
        part = values[:, g * lanes : (g + 1) * lanes]
        one = jnp.where(first_pair == g, part, one)
        two = jnp.where(second_pair == g, part, two)
    one = jnp.where(first % 2 == 0, one, swap(one))
    two = jnp.where(second % 2 == 1, two, swap(two))
    return one, two


def id_range(message, rows):
    block = message[rows : rows + pad_rows, :][0:8].astype(f32)
    count = rows // lanes
    return block[count : count + 1], block[count + 1 : count + 2]


def id_row(message, rows):
    block = message[rows : rows + pad_rows, :][0:8].astype(f32)
    return from_rows(block, rows // lanes)


def over_pieces(parts, rows, own, visit):
    own_low, own_high = id_range(own, rows)

    def kind(message):
        low, high = id_range(message, rows)
        meets = jnp.where((low <= own_high) & (high >= own_low), 1.0, 0.0)
        return meets * jnp.where((low == high) & (own_low == own_high), 2.0, 1.0)

    def one(index, i, message, code):
        @pl.when(code == 2)
        def _():
            visit(index, i, message, True)

        @pl.when(code == 1)
        def _():
            visit(index, i, message, False)

    few = [(index, i, part.at[i]) for index, part in enumerate(parts) for i in range(part.shape[0]) if part.shape[0] <= 8]
    if few:
        codes = sum(kind(message) * 4.0**n for n, (_, _, message) in enumerate(few))
        codes = jnp.max(codes).astype(jnp.int32)
    for n, (index, i, message) in enumerate(few):
        one(index, i, message, lax.rem(codes // 4**n, 4))
    for index, part in enumerate(parts):
        if part.shape[0] > 8:

            @pl.loop(0, part.shape[0])
            def _(i, index=index, part=part):
                message = part.at[i]
                one(index, i, message, jnp.max(kind(message)).astype(jnp.int32))


def places(ref, c):
    rows = ref.shape[0] // 2
    return slice(c * chunk, (c + 1) * chunk), slice(rows + c * chunk, rows + (c + 1) * chunk)


def both(ref, c):
    one, two = places(ref, c)
    return jnp.concatenate([ref[one, :], ref[two, :]], axis=0)


def put_both(ref, c, values):
    one, two = places(ref, c)
    ref[one, :] = values[:chunk]
    ref[two, :] = values[chunk:]


def same(seg, c, ids):
    mine = seg[c * chunk : (c + 1) * chunk, :]
    return wide(jnp.concatenate([mine, mine], axis=0), ids.shape[1] // lanes) == ids


def staged(chunks, products, weigh, collect):
    current, ready = products(0), None
    for c in range(chunks):
        following = products(c + 1) if c + 1 < chunks else None
        if ready is not None:
            collect(c - 1, *ready)
        ready = weigh(c, current)
        current = following
    collect(chunks - 1, *ready)


def forward_kernel(piece_count, first, last, stack, seg, own, *rest):
    parts = rest[:piece_count]
    rest = rest[piece_count:]
    if not first:
        total_in, peak_in = rest[:2]
        rest = rest[2:]
    if last:
        heads, lse, total, peak = rest
    else:
        total, peak = rest
    rows = seg.shape[0]
    across = rows // lanes
    if first:
        peak[...] = jnp.full(peak.shape, lowest, f32)
        total[...] = jnp.zeros(total.shape, f32)
    else:
        peak[...] = peak_in[...]
        total[...] = total_in[...]

    def visit(index, i, message, uniform):
        kv = message[0:rows, :]
        low = lane_ids(rows) < half
        values = jnp.where(low, jnp.ones_like(kv), kv)
        if not uniform:
            key_ids = id_row(message, rows)

        def products(c):
            scores = nt(both(stack, c), kv)
            if not uniform:
                scores = jnp.where(same(seg, c, key_ids), scores, masked)
            return scores

        def weigh(c, scores):
            before = both(peak, c)
            now = jnp.maximum(before, jnp.max(scores, axis=1, keepdims=True))
            put_both(peak, c, now)
            return jnp.exp(scores - wide(now, across)).astype(bf16), jnp.exp(before - now)

        def collect(c, weights, factor):
            put_both(total, c, both(total, c) * factor + nn(weights, values))

        staged(rows // chunk, products, weigh, collect)

    over_pieces(parts, rows, own, visit)
    if not last:
        return
    low = lane_ids(lanes) < half
    for at in row_blocks(rows):
        second_at = slice(rows + at.start, rows + at.stop)
        one, two = total[at, :], total[second_at, :]
        one_other, two_other = swap(one), swap(two)
        heads[at, :] = jnp.where(low, one_other, two) / jnp.where(low, one, two_other)
        lse[at, :] = peak[at, :] + jnp.log(jnp.where(low, one, one_other))
        lse[second_at, :] = peak[second_at, :] + jnp.log(jnp.where(low, two, two_other))


def query_back_kernel(spread_out, piece_count, first, last, stack, stack_do, lse, delta, seg, own, *rest):
    parts = rest[:piece_count]
    rest = rest[piece_count:]
    if not first:
        total_in = rest[0]
        rest = rest[1:]
    if last:
        normed, picks, wq, dlog, wroute, keep, send, grad_n, total, spread_keep = rest
    else:
        total = rest[0]
    rows = seg.shape[0]
    across = rows // lanes
    total[...] = jnp.zeros(total.shape, f32) if first else total_in[...]

    def visit(index, i, message, uniform):
        kv = message[0:rows, :]
        if not uniform:
            key_ids = id_row(message, rows)

        def products(c):
            scores = nt(both(stack, c), kv)
            if not uniform:
                scores = jnp.where(same(seg, c, key_ids), scores, masked)
            return scores, nt(both(stack_do, c), kv)

        def weigh(c, pair):
            scores, grad_prob = pair
            prob = jnp.exp(scores - wide(both(lse, c), across))
            return ((prob * (grad_prob - wide(both(delta, c), across))).astype(bf16),)

        def collect(c, grad_scores):
            put_both(total, c, both(total, c) + nn(grad_scores, kv))

        staged(rows // chunk, products, weigh, collect)

    over_pieces(parts, rows, own, visit)
    if not last:
        return
    low = lane_ids(lanes) < half
    scale = half ** (-0.5)
    for at in row_blocks(rows):
        one = total[at, :] * scale
        two = total[slice(rows + at.start, rows + at.stop), :] * scale
        one = jnp.where(low, one, swap(one))
        two = jnp.where(low, two, swap(two))
        spread = spread_slots(one, two, picks[0, at, :], picks[1, at, :], normed.shape[1] // lanes).astype(bf16)
        spread_keep[at, :] = spread
        grad_n[at, :] = nt(spread, wq[...]) + nn(dlog[at, :], wroute[...])
    whole = tn(normed[...], spread_keep[...]).astype(bf16)
    core = place(spread_out)[0]
    count = whole.shape[0] // parts_of
    for i in range(parts_of // 2):
        at = slice(i * count, (i + 1) * count)
        even = whole[2 * i * count : (2 * i + 1) * count]
        odd = whole[(2 * i + 1) * count : (2 * i + 2) * count]
        keep[at, :] = jnp.where(core == 0, even, odd)
        send[at, :] = jnp.where(core == 0, odd, even)


def spread_slots(one, two, first, second, pairs):
    upper = (lane_ids(one.shape[0]) >= half).astype(jnp.int32)
    out = []
    for g in range(pairs):
        expert = 2 * g + upper
        out.append(jnp.where(first == expert, one, jnp.where(second == expert, two, 0.0)))
    return jnp.concatenate(out, axis=1)


def key_back_kernel(spread_out, piece_count, first, last, keys, values, seg, own, *rest):
    q_parts = rest[:piece_count]
    do_parts = rest[piece_count : 2 * piece_count]
    rest = rest[2 * piece_count :]
    if not first:
        k_in, v_in = rest[:2]
        rest = rest[2:]
    if last:
        final_in, final_out = rest[:9] + (place(spread_out)[0],), rest[9:12]
        total_k, total_v, grad_kv, whole = rest[12:]
    else:
        total_k, total_v = rest
    rows = seg.shape[0]
    across = rows // lanes
    if first:
        total_k[...] = jnp.zeros(total_k.shape, f32)
        total_v[...] = jnp.zeros(total_v.shape, f32)
    else:
        total_k[...] = k_in[...]
        total_v[...] = v_in[...]

    def visit(index, i, message, uniform):
        queries = message[0:rows, :]
        sent = do_parts[index].at[i]
        grads = sent[0:rows, :]
        stats = sent[rows : rows + stat_rows, :].astype(f32)

        def stat(first, terms):
            block = stats[first * 8 : first * 8 + 8]
            for t in range(1, terms):
                block = block + stats[(first + t) * 8 : (first + t) * 8 + 8]
            return from_rows(block, across)

        lse = (stat(0, 3), stat(3, 3))
        delta = (stat(6, 2), stat(8, 2))
        if not uniform:
            query_ids = id_row(message, rows)

        def spread(pair):
            return jnp.concatenate(
                [jnp.broadcast_to(pair[0], (chunk, rows)), jnp.broadcast_to(pair[1], (chunk, rows))],
                axis=0,
            )

        def products(c):
            scores = nt(both(keys, c), queries)
            if not uniform:
                scores = jnp.where(same(seg, c, query_ids), scores, masked)
            return scores, nt(both(values, c), grads)

        def weigh(c, pair):
            scores, grad_prob = pair
            prob = jnp.exp(scores - spread(lse))
            return prob.astype(bf16), (prob * (grad_prob - spread(delta))).astype(bf16)

        def collect(c, prob, grad_scores):
            put_both(total_v, c, both(total_v, c) + nn(prob, grads))
            put_both(total_k, c, both(total_k, c) + nn(grad_scores, queries))

        staged(rows // chunk, products, weigh, collect)

    over_pieces(q_parts, rows, own, visit)
    if not last:
        return
    low = lane_ids(lanes) < half
    for at in row_blocks(rows):
        second_at = slice(rows + at.start, rows + at.stop)
        key_grad = total_k[at, :] + swap(total_k[second_at, :])
        value_grad = swap(total_v[at, :]) + total_v[second_at, :]
        grad_kv[at, :] = jnp.where(low, key_grad, value_grad).astype(bf16)
    final_step(*final_in, grad_kv, *final_out, whole)


def middle_kernel(
    spread_out,
    tok, cot, heads, gates, picks, lse, normed, wout, wup, bup, wdown, bdown, gain, shift,
    layer_out, keep, send, grad_mid, dom, do_stack, delta_out, dlog, grad_route, grad_bup, grad_small,
    second_n, second_t, total_y, total_n, mid_keep, mixed_keep, unit_keep, inverse_keep, low_keep, logit_keep,
):
    rows, width = tok.shape
    hidden = wup.shape[1]
    lane = lane_ids(lanes)
    low = lane < half
    pairs = width // lanes
    for at in row_blocks(rows):
        gated = gates[at, :] * heads[at, :]
        turned = swap(gated)
        mixed = spread_slots(
            jnp.where(low, gated, turned), jnp.where(low, turned, gated), picks[0, at, :], picks[1, at, :], pairs
        ).astype(bf16)
        mixed_keep[at, :] = mixed
        middle = tok[at, :].astype(f32) + nn(mixed, wout[...])
        mid_keep[at, :] = middle
        unit, inverse = normalized(middle)
        unit_keep[at, :] = unit
        inverse_keep[at, :] = jnp.broadcast_to(inverse, (lanes, lanes))
        n_two = (unit * gain[...] + shift[...]).astype(bf16)
        second_n[at, :] = n_two
        second_t[:, at] = n_two.T
    total_y[...] = jnp.zeros(total_y.shape, f32)
    total_n[...] = jnp.zeros(total_n.shape, f32)
    step = feed_step
    root = 0.7978845608028654
    cubic = 0.044715
    core = place(spread_out)[0]
    down_rows = hidden // parts_of
    up_rows = width // parts_of
    piece = gradient_rows(width, hidden)

    def put(index, at_row, at_lane, even, odd):
        count, across = even.shape
        start = index * piece + at_row
        target = (slice(start, start + count), slice(at_lane, at_lane + across))
        keep[target] = jnp.where(core == 0, even, odd)
        send[target] = jnp.where(core == 0, odd, even)

    def products(f):
        at = slice(f * step, (f + 1) * step)
        return nn(second_n[...], wup[:, at]) + bup[:, at], nt(cot[...], wdown[at, :])

    def bend(f, pair):
        pre, grad_act = pair
        square = pre * pre
        bent = jnp.tanh(pre * (root + (root * cubic) * square))
        rise = 0.5 + 0.5 * bent
        act = (pre * rise).astype(bf16)
        slope = rise + (pre * (rise * (1.0 - bent))) * (root + (3.0 * root * cubic) * square)
        grad_pre = (grad_act * slope).astype(bf16)
        grad_bup[:, f * step : (f + 1) * step] = jnp.sum(grad_pre.astype(f32), axis=0, keepdims=True)
        return act, grad_pre

    def collect(f, act, grad_pre):
        at = slice(f * step, (f + 1) * step)
        total_y[...] += nn(act, wdown[at, :])
        total_n[...] += nt(grad_pre, wup[:, at])
        grad_down = tn(act, cot[...]).astype(bf16)
        for i in range(step // (2 * down_rows)):
            pair = grad_down[2 * i * down_rows : 2 * (i + 1) * down_rows]
            put(f * (step // (2 * down_rows)) + i, 0, 0, pair[:down_rows], pair[down_rows:])
        grad_up = nn(second_t[...], grad_pre).astype(bf16)
        block_of, at_lane = divmod(f * step, width)
        for i in range(parts_of // 2):
            pair = grad_up[2 * i * up_rows : 2 * (i + 1) * up_rows]
            put(i, down_rows + block_of * up_rows, at_lane, pair[:up_rows], pair[up_rows:])

    staged(hidden // step, products, bend, collect)

    sums = [jnp.zeros((1, width), f32)] * 3
    experts = dlog.shape[1]
    stats = [[], [], [], []]
    zero = jnp.zeros((lanes, lanes), f32)
    for at in row_blocks(rows):
        second_at = slice(rows + at.start, rows + at.stop)
        first, second = picks[0, at, :], picks[1, at, :]
        layer_out[at, :] = (mid_keep[at, :] + total_y[at, :] + bdown[...]).astype(bf16)
        unit = unit_keep[at, :]
        back, grad_gain, grad_shift = normalized_back(total_n[at, :], unit, wide(inverse_keep[at, :], pairs), gain[...])
        dy = cot[at, :].astype(f32)
        grad_middle = dy + back
        grad_mid[at, :] = grad_middle
        sums = [a + b for a, b in zip(sums, (jnp.sum(dy, axis=0, keepdims=True), grad_gain, grad_shift))]
        grad_low = grad_middle.astype(bf16)
        low_keep[at, :] = grad_low
        one, two = pick_slots(nt(grad_low, wout[...]), first, second)
        slots = jnp.where(low, one, two)
        head_values = heads[at, :]
        gate = gates[at, :]
        grad_heads = (gate * slots).astype(bf16)
        dom[at, :] = grad_heads
        carried = grad_heads.astype(f32)
        turned = swap(carried)
        do_stack[at, :] = jnp.where(low, zero, turned).astype(bf16)
        do_stack[second_at, :] = jnp.where(low, zero, carried).astype(bf16)
        gated_grad = slots * head_values
        gate_one = jnp.sum(jnp.where(low, gated_grad, 0.0), axis=1, keepdims=True)
        gate_two = jnp.sum(jnp.where(low, 0.0, gated_grad), axis=1, keepdims=True)
        grad_gate = jnp.where(low, gate_one, gate_two)
        weighted = gate * grad_gate
        grad_logit = gate * (grad_gate - (weighted + swap(weighted)))
        logit_other = swap(grad_logit)
        logit_one = jnp.where(low, grad_logit, logit_other)
        logit_two = jnp.where(low, logit_other, grad_logit)
        grad_logits = jnp.where(lane == first, logit_one, jnp.where(lane == second, logit_two, 0.0)).astype(bf16)
        logit_keep[at, :] = grad_logits
        dlog[at, :] = grad_logits[:, :experts]
        carried = carried * head_values
        delta_one = jnp.broadcast_to(jnp.sum(jnp.where(low, carried, 0.0), axis=1, keepdims=True), (lanes, lanes))
        delta_two = jnp.broadcast_to(jnp.sum(jnp.where(low, 0.0, carried), axis=1, keepdims=True), (lanes, lanes))
        delta_out[at, :] = delta_one
        delta_out[second_at, :] = delta_two
        for store, values in zip(stats, (lse[at, :], lse[second_at, :], delta_one, delta_two)):
            store.append(jnp.transpose(values, (1, 0))[0:1, :])
    blocks = []
    for store, terms in zip(stats, (3, 3, 2, 2)):
        rest = jnp.concatenate(store + [jnp.zeros((8 - len(store), lanes), f32)], axis=0)
        for _ in range(terms):
            part = rest.astype(bf16).astype(f32)
            blocks.append(part)
            rest = rest - part
    dom[rows : rows + stat_rows, :] = jnp.concatenate(blocks, axis=0).astype(bf16)
    grad_small[...] = jnp.concatenate(sums + [jnp.zeros((5, width), f32)], axis=0)
    grad_route[...] = tn(logit_keep[...], normed[...])[:experts, :]
    grad_out = tn(mixed_keep[...], low_keep[...]).astype(bf16)
    for i in range(parts_of // 2):
        pair = grad_out[2 * i * up_rows : 2 * (i + 1) * up_rows]
        put(i, piece - up_rows, 0, pair[:up_rows], pair[up_rows:])


def final_step(
    tok, normed, grad_n, grad_mid, wkv, gain, grad_route, grad_bup, small_two, core_at, grad_kv,
    grad_tokens, keep, send, whole,
):
    width = tok.shape[1]
    whole[0:width, :] = tn(normed[...], grad_kv[...]).astype(bf16)
    grad_gain = grad_shift = jnp.zeros((1, width), f32)
    for at in row_blocks(tok.shape[0]):
        upstream = grad_n[at, :] + nt(grad_kv[at, :], wkv[...])
        unit, inverse = normalized(tok[at, :].astype(f32))
        back, more_gain, more_shift = normalized_back(upstream, unit, inverse, gain[...])
        grad_tokens[at, :] = grad_mid[at, :] + back
        grad_gain, grad_shift = grad_gain + more_gain, grad_shift + more_shift
    rows = [grad_gain, grad_shift] + [small_two[i : i + 1, :] for i in range(3)]
    rows += [grad_bup[:, i : i + width] for i in range(0, grad_bup.shape[1], width)]
    rows += [grad_route[i : i + 1, :] for i in range(grad_route.shape[0])]
    small = jnp.concatenate([row[:, i : i + lanes] for row in rows for i in range(0, width, lanes)], axis=0)
    last = whole.shape[0] - width
    small = jnp.concatenate([small, jnp.zeros((last - small.shape[0], lanes), f32)], axis=0)
    whole[width:, :] = small.astype(bf16)
    core = core_at
    piece = keep.shape[0]
    keep[...] = whole[block(core, piece), :]
    send[...] = whole[block(1 - core, piece), :]


parts_of = 32


def place(spread_out):
    if not spread_out:
        return 0, 0, 0, 0
    row, seq = lax.axis_index("row"), lax.axis_index("seq")
    return lax.rem(row, 2), row // 2, lax.rem(seq, 2), seq // 2


def gradient_rows(width, hidden):
    return hidden // parts_of + (hidden // width + 1) * (width // parts_of)


def block(index, count):
    return pl.ds(pl.multiple_of(index * count, 16), count)


def plus(*refs):
    def get(at):
        total = refs[0][at].astype(f32)
        for ref in refs[1:]:
            total = total + ref[at].astype(f32)
        return total.astype(bf16)

    return get


def after_core_kernel(keep, received, one_keep, one_send, two_keep, two_send):
    _, x, y, _ = place(True)
    piece, upper, lower = keep.shape[0] // 16, one_keep.shape[0] // 8, two_keep.shape[0] // 8
    total = plus(keep, received)

    def part(index, offset, count):
        return total((pl.ds(pl.multiple_of(index * piece + offset, 16), count), slice(None)))

    for zy in range(8):
        here = slice(zy * upper, (zy + 1) * upper)
        one_keep[here, :] = part(zy * 2 + x, 0, upper)
        one_send[here, :] = part(zy * 2 + 1 - x, 0, upper)
    for z in range(4):
        for at_x in range(2):
            here = slice((z * 2 + at_x) * lower, (z * 2 + at_x + 1) * lower)
            two_keep[here, :] = part((z * 2 + y) * 2 + at_x, upper, lower)
            two_send[here, :] = part((z * 2 + 1 - y) * 2 + at_x, upper, lower)


def split_kernel(keep, received, kept, sent):
    x = place(True)[1]
    piece = kept.shape[0] // 8
    total = plus(keep, received)
    for i in range(8):
        here = slice(i * piece, (i + 1) * piece)
        kept[here, :] = total((block(i * 2 + x, piece), slice(None)))
        sent[here, :] = total((block(i * 2 + 1 - x, piece), slice(None)))


def after_first_kernel(one, one_in, extra, extra_in, two, two_in, one_keep, one_send, two_keep, two_send):
    _, x, y, _ = place(True)
    upper = one.shape[0] // 8
    for total, mine, kept, sent, piece, offset in (
        (plus(one, one_in), y, one_keep, one_send, upper, 0),
        (plus(extra, extra_in), y, one_keep, one_send, extra.shape[0] // 8, upper),
        (plus(two, two_in), x, two_keep, two_send, two.shape[0] // 8, 0),
    ):
        stride = kept.shape[0] // 4
        for z in range(4):
            here = slice(z * stride + offset, z * stride + offset + piece)
            kept[here, :] = total((block(z * 2 + mine, piece), slice(None)))
            sent[here, :] = total((block(z * 2 + 1 - mine, piece), slice(None)))


def after_second_kernel(one, one_in, two, two_in, *outs):
    z = place(True)[3]
    at = 0
    for total, count in ((plus(one, one_in), one.shape[0] // 4), (plus(two, two_in), two.shape[0] // 4)):
        for i, out in enumerate(outs):
            out[at : at + count, :] = total((block(z ^ i, count), slice(None)))
        at += count


def sum_kernel(*refs):
    refs[-1][...] = plus(*refs[:-1])(Ellipsis)


def join_halves_kernel(*refs):
    z = place(True)[3]
    one, two = refs[4:]
    upper, lower = one.shape[0] // 4, two.shape[0] // 4
    for i in range(4):
        one[block(z ^ i, upper), :] = refs[i][:upper, :]
        two[block(z ^ i, lower), :] = refs[i][upper:, :]


def unpack_kernel(spread_out, turns, outer, fresh, *refs):
    core, x, y, _ = place(spread_out)
    count = 2 * len(turns)
    parts, refs = refs[:count], refs[count if fresh else count + 4 :]
    outs, stages, sems = refs[:4], refs[4:8], refs[8]
    grad_up, grad_down, grad_out, grad_wq = outs
    width, hidden = grad_up.shape
    down_rows, up_rows = hidden // parts_of, width // parts_of
    moves = []

    def send(stage, start, rows, out, device):
        target = out.at[block(device, rows), :]
        moves.append(pltpu.make_async_copy(stage.at[start : start + rows, :], target, sems.at[len(moves)]))
        moves[-1].start()

    at = 0
    for n, turn in enumerate(turns):
        one, two = parts[2 * n : 2 * n + 2]
        for inner in range(2):
            for z in range(4):
                row, low, high = inner * 4 + z, at * down_rows, at * up_rows
                at += 1
                device = ((z * 2 + (y ^ inner)) * 2 + (x ^ outer)) * 2 + (core ^ turn)
                base = row * (down_rows + up_rows)
                stages[1][low : low + down_rows, :] = one[base : base + down_rows, :].astype(f32)
                send(stages[1], low, down_rows, grad_down, device)
                base += down_rows
                stages[3][high : high + up_rows, :] = one[base : base + up_rows, :].astype(f32)
                send(stages[3], high, up_rows, grad_wq, device)
                device = ((z * 2 + (y ^ outer)) * 2 + (x ^ inner)) * 2 + (core ^ turn)
                across = hidden // width
                base = row * (across + 1) * up_rows
                for c in range(across):
                    value = two[base + c * up_rows : base + (c + 1) * up_rows, :]
                    stages[0][high : high + up_rows, c * width : (c + 1) * width] = value.astype(f32)
                send(stages[0], high, up_rows, grad_up, device)
                base += across * up_rows
                stages[2][high : high + up_rows, :] = two[base : base + up_rows, :].astype(f32)
                send(stages[2], high, up_rows, grad_out, device)
    for move in moves:
        move.wait()


def unpack(spread_out, turns, outer, parts, so_far, width, hidden):
    outs = (shape((width, hidden), f32), shape((hidden, width), f32)) + (shape((width, width), f32),) * 2
    share = 4 // len(turns)
    hbm = pl.BlockSpec(memory_space=pltpu.HBM)
    whole = pl.BlockSpec(memory_space=pltpu.VMEM)
    return pl.pallas_call(
        functools.partial(unpack_kernel, spread_out, turns, outer, not so_far),
        out_shape=outs,
        in_specs=[whole] * len(parts) + [hbm] * len(so_far),
        out_specs=(hbm,) * 4,
        scratch_shapes=[pltpu.VMEM((out.shape[0] // share, out.shape[1]), f32) for out in outs]
        + [pltpu.SemaphoreType.DMA((32 * len(turns),))],
        input_output_aliases={len(parts) + i: i for i in range(len(so_far))},
        compiler_params=pltpu.CompilerParams(vmem_limit_bytes=16 * mib),
        cost_estimate=pl.CostEstimate(flops=int(2 * unpack_weight * busy), bytes_accessed=0, transcendentals=0),
    )(*parts, *so_far)


def flip_row(x, mask):
    return lax.ppermute(x, "row", [(i, i ^ mask) for i in range(4)])


def flip_seq(x, mask):
    return lax.ppermute(x, "seq", [(i, i ^ mask) for i in range(8)])


def simple(kernel, outs, *operands):
    return call(kernel, outs, [], 20 * mib, 0.5 * small_weight, *operands)


def add(a, b):
    return (a.astype(f32) + b.astype(f32)).astype(bf16)


def finish_sums(large, small, hidden):
    mine, arrived = large
    keep, send = small
    count, width = mine.shape
    total = add(keep, after(flip_row(send, 1), mine))
    part = shape((2 * count, width), bf16)
    one, two = simple(join_halves_kernel, (part,) * 2, mine, *arrived)
    one_in, two_in = flip_seq(one, 1), flip_row(two, 2)
    total = add(total, after(flip_row(total, 2), one))
    one, two = jnp.concatenate([one, one_in]), jnp.concatenate([two, two_in])
    one_in, two_in = flip_row(one, 2), flip_seq(two, 1)
    one_other, two_other = flip_row(one, 1), flip_row(two, 1)
    total = add(total, after(flip_seq(total, 1), one, two))
    done = unpack(True, (0, 1), 0, (one, two, one_other, two_other), (), width, hidden)
    total = add(total, flip_seq(total, 2))
    total = add(total, after(flip_seq(total, 4), done[3]))
    one_in = after(one_in, total)
    other = flip_row(total, 1)
    one_other, two_other = flip_row(one_in, 1), flip_row(two_in, 1)
    done = unpack(True, (0,), 1, (one_in, two_in), done, width, hidden)
    done = unpack(True, (1,), 1, (one_other, two_other), done, width, hidden)
    return done, (total, other)


def unpack_small_kernel(spread_out, mine, other, grad_wkv, grad_route, grad_bup, *rest):
    small, whole = rest[:5], rest[5]
    core = place(spread_out)[0]
    piece = mine.shape[0]
    whole[block(core, piece), :] = mine[...].astype(f32)
    whole[block(1 - core, piece), :] = other[...].astype(f32)
    width = grad_wkv.shape[0]
    across = width // lanes
    grad_wkv[...] = whole[0:width, :]
    at = width
    for i in range(5):
        for g in range(across):
            small[i][:, g * lanes : (g + 1) * lanes] = whole[at : at + 1, :]
            at += 1
    for g in range(grad_bup.shape[1] // lanes):
        grad_bup[:, g * lanes : (g + 1) * lanes] = whole[at : at + 1, :]
        at += 1
    for i in range(grad_route.shape[0]):
        for g in range(across):
            grad_route[i : i + 1, g * lanes : (g + 1) * lanes] = whole[at : at + 1, :]
            at += 1


busy = 400_000_000
key_weight, query_weight, forward_weight, final_weight, unpack_weight, small_weight = 1.0, 1.0, 1.0, 1.0, 1.0, 1.0


def call(kernel, out_shape, scratch, limit, time, *operands):
    whole = pl.BlockSpec(memory_space=pltpu.VMEM)
    return pl.pallas_call(
        kernel,
        out_shape=out_shape,
        in_specs=[whole] * len(operands),
        out_specs=jax.tree.map(lambda _: whole, out_shape),
        scratch_shapes=scratch,
        compiler_params=pltpu.CompilerParams(vmem_limit_bytes=limit),
        cost_estimate=pl.CostEstimate(flops=int(time * busy), bytes_accessed=0, transcendentals=0),
    )(*operands)


def shape(dims, dtype):
    return jax.ShapeDtypeStruct(tuple(dims), dtype)


def after(value, *earlier):
    return lax.optimization_barrier((value,) + earlier)[0]


def local(
    tokens, cotangent, w_query, w_kv, w_route, w_out, w_up, bias_up, w_down, bias_down,
    gain_one, shift_one, gain_two, shift_two, choices, segment_ids,
):
    size = lax.axis_size("seq")
    tok, cot = tokens[0], cotangent[0]
    rows, width = tok.shape
    hidden = w_up.shape[1]
    route = w_route.T
    experts = route.shape[0]
    row = lambda v: v.reshape(1, -1)
    message = shape((rows + pad_rows, lanes), bf16)
    stacked = (2 * rows, lanes)
    stack = shape(stacked, bf16)
    hbm = pl.BlockSpec(memory_space=pltpu.HBM)
    whole = pl.BlockSpec(memory_space=pltpu.VMEM)
    sent_keys, normed = pl.pallas_call(
        keys_kernel,
        out_shape=(message, shape((rows, width), bf16)),
        in_specs=[hbm] * 5,
        out_specs=(whole,) * 2,
        scratch_shapes=[
            pltpu.VMEM((rows, width), bf16), pltpu.VMEM((width, lanes), bf16), pltpu.VMEM((1, width), f32),
            pltpu.VMEM((1, width), f32), pltpu.VMEM((1, rows), jnp.int32), pltpu.SemaphoreType.DMA((5,)),
        ],
        compiler_params=pltpu.CompilerParams(vmem_limit_bytes=60 * mib),
        cost_estimate=pl.CostEstimate(flops=busy, bytes_accessed=0, transcendentals=0),
    )(tok, w_kv, row(gain_one), row(shift_one), segment_ids)
    spread_out = size == 8 and lax.axis_size("row") == 4
    qm, q_stack, k_stack, v_stack, gates, picks, seg, kvm = call(
        queries_kernel,
        (
            message, stack, stack, stack, shape((rows, lanes), f32), shape((2, rows, lanes), jnp.int32),
            shape((rows, lanes), f32), message,
        ),
        [], 12 * mib, 1.6,
        normed, sent_keys, segment_ids, w_query, route, choices[0].T,
    )
    state = (shape(stacked, f32),) * 2
    finished = (shape((rows, lanes), f32), shape(stacked, f32)) + state

    def forward(parts, first, last, *so_far):
        return call(
            functools.partial(forward_kernel, len(parts), first, last), finished if last else state, [], 16 * mib,
            1.4 * forward_weight * len(parts) * parts[0].shape[0], q_stack, seg, kvm, *parts, *so_far,
        )

    if size == 8:
        far_z, near_z, near_y = flip_seq(sent_keys, 4), flip_seq(sent_keys, 2), flip_seq(sent_keys, 1)
        near_y, near_z, far_z, q_stack, kvm = lax.optimization_barrier((near_y, near_z, far_z, q_stack, kvm))
        near = [m[None] for m in (kvm, near_y, near_z, far_z)]
        others = [flip_seq(near_z, 1), flip_seq(far_z, 1), flip_seq(far_z, 2), flip_seq(after(sent_keys, far_z), 7)]
        others = [m[None] for m in others]
        so_far = forward(near, True, False)
        heads, lse, _, _ = forward(others, False, True, *so_far)
        q_two = jnp.stack([qm, after(flip_seq(qm, 1), so_far[0])])
        q_far = [flip_seq(q_two, 2), flip_seq(q_two, 4)]
        heads = after(heads, q_two)
    else:
        all_kv = [lax.all_gather(kvm, "seq", axis=0, tiled=False)]
        heads, lse, _, _ = forward(all_kv, True, True)
    piece = gradient_rows(width, hidden)
    gradients = shape((piece * parts_of // 2, width), bf16)
    (
        layer_out, keep, send, grad_mid, dom, do_stack, delta, dlog, grad_route, grad_bup, small_two,
    ) = call(
        functools.partial(middle_kernel, spread_out),
        (
            shape((rows, width), bf16), gradients, gradients, shape((rows, width), f32), shape((rows + stat_rows, lanes), bf16),
            stack, shape(stacked, f32), shape((rows, experts), bf16), shape((experts, width), f32),
            shape((1, hidden), f32), shape((8, width), f32),
        ),
        [
            pltpu.VMEM((rows, width), bf16), pltpu.VMEM((width, rows), bf16), pltpu.VMEM((rows, width), f32),
            pltpu.VMEM((rows, width), f32), pltpu.VMEM((rows, width), f32), pltpu.VMEM((rows, width), bf16),
            pltpu.VMEM((rows, width), f32), pltpu.VMEM((rows, lanes), f32), pltpu.VMEM((rows, width), bf16),
            pltpu.VMEM((rows, lanes), bf16),
        ],
        40 * mib, 15,
        tok, cot, heads, gates, picks, lse, normed, w_out, w_up, row(bias_up), w_down, row(bias_down),
        row(gain_two), row(shift_two),
    )
    results = {}
    extra_part = shape((width // 2, width), bf16)

    def query_back(parts, first, last, *earlier):
        finish = (normed, picks, w_query, dlog, route) if last else ()
        outs = (extra_part, extra_part, shape((rows, width), f32)) if last else ()
        results["query"] = call(
            functools.partial(query_back_kernel, spread_out, len(parts), first, last),
            outs + (shape(stacked, f32),),
            [pltpu.VMEM((rows, width), bf16)] if last else [],
            20 * mib, 1.6 * query_weight * len(parts) * parts[0].shape[0],
            after(q_stack, *earlier), do_stack, lse, delta, seg, kvm, *parts, *(() if first else results["query"]), *finish,
        )
        return results["query"][-1]

    extra = 5 + hidden // width + experts
    small_rows = extra * (width // lanes) + width
    small_rows = -(-small_rows // 32) * 32

    def key_back(q_parts, do_parts, first, last, *earlier):
        part = shape((small_rows // 2, lanes), bf16)
        final = (
            tok, normed, results["query"][2], grad_mid, w_kv, row(gain_one), grad_route, grad_bup, small_two,
        ) if last else ()
        results["key"] = call(
            functools.partial(key_back_kernel, spread_out, len(q_parts), first, last),
            ((shape((rows, width), f32), part, part) if last else ()) + state,
            [pltpu.VMEM((rows, lanes), bf16), pltpu.VMEM((small_rows, lanes), bf16)] if last else [],
            24 * mib, 2.1 * key_weight * len(q_parts) * q_parts[0].shape[0] + 2.4 * last,
            after(k_stack, *earlier), v_stack, seg, kvm, *q_parts, *do_parts, *(() if first else results["key"]), *final,
        )
        return results["key"][-1]

    if spread_out:
        send, q_near, q_other = lax.optimization_barrier((send, *q_far))
        q_last = flip_seq(q_other, 2)
        received = flip_row(send, 1)
        d_two = jnp.stack([dom, flip_seq(dom, 1)])
        received = after(received, query_back(near, True, False))
        upper, lower = hidden // parts_of, piece - hidden // parts_of
        more = width // parts_of
        part = lambda count, rows: shape((count * rows, width), bf16)
        one, one_send, two, two_send = simple(
            after_core_kernel, (part(8, upper),) * 2 + (part(8, lower),) * 2, keep, received
        )
        one_in, two_in = flip_row(one_send, 2), flip_seq(two_send, 1)
        d_other, d_near = flip_seq(d_two, 4), flip_seq(d_two, 2)
        query_back(others, False, True, one, d_two, q_last)
        extra, extra_send, _, done = results["query"]
        extra, extra_send = simple(split_kernel, (part(8, more),) * 2, extra, flip_row(extra_send, 1))
        extra_in = flip_row(extra_send, 2)
        done = key_back([q_two], [d_two], True, False, extra, d_other)
        d_last = flip_seq(after(d_other, done), 2)
        one, one_send, two, two_send = simple(
            after_first_kernel, (part(4, upper + more),) * 2 + (part(4, lower),) * 2,
            one, after(one_in, done), extra, extra_in, two, two_in,
        )
        one_in, two_in = flip_seq(one_send, 1), flip_row(two_send, 2)
        done = key_back([q_other], [d_other], False, False, one)
        sent = simple(after_second_kernel, (part(1, piece + more),) * 4, one, after(one_in, done), two, two_in)
        planes = [flip_seq(sent[i], 2 * i) for i in (1, 2, 3)]
        key_back([q_near], [d_near], False, False, sent[0])
        key_back([q_last], [d_last], False, True)
        grad_tokens, *small = results["key"][:3]
        mine = simple(sum_kernel, part(1, piece + more), after(sent[0], small[0]), *planes)
        arrived = [flip_seq(mine, 2 * i) for i in (1, 2, 3)]
        large, small = finish_sums((mine, arrived), small, hidden)
    else:
        query_back(all_kv, True, True)
        gathered = [lax.all_gather(m, "seq", axis=0, tiled=False) for m in (qm, dom)]
        key_back(gathered[:1], gathered[1:], True, True)
        grad_tokens, *small = results["key"][:3]
        small = lax.psum(small, ("seq", "row"))
        sums = lax.psum((keep, send, *results["query"][:2]), ("seq", "row"))
        large = []
        upper = hidden // parts_of
        for total, more in zip(sums[:2], sums[2:]):
            cube = total.reshape(4, 2, 2, piece, width)
            more = more.reshape(4, 2, 2, -1, width)
            one = jnp.concatenate([cube[:, :, :, :upper], more], axis=3)
            two = cube[:, :, :, upper:]
            for i in range(2):
                large.append(one[:, :, i].transpose(1, 0, 2, 3).reshape(-1, width))
                large.append(two[:, i].transpose(1, 0, 2, 3).reshape(-1, width))
        done = unpack(False, (0, 1), 0, (large[0], large[1], large[4], large[5]), (), width, hidden)
        done = unpack(False, (0,), 1, large[2:4], done, width, hidden)
        large = unpack(False, (1,), 1, large[6:8], done, width, hidden)
    grad_wkv, grad_route, grad_bup, *grad_small = call(
        functools.partial(unpack_small_kernel, spread_out),
        (
            shape((width, lanes), f32), shape((experts, width), f32), shape((1, hidden), f32),
        ) + (shape((1, width), f32),) * 5,
        [pltpu.VMEM((small_rows, lanes), f32)], 8 * mib, 0.8, *small,
    )
    grad_up, grad_down, grad_out, grad_wq = large
    return (
        layer_out[None],
        grad_tokens[None],
        grad_wq,
        grad_wkv,
        grad_route.T,
        grad_out,
        grad_up,
        grad_bup.reshape(-1),
        grad_down,
        grad_small[2].reshape(-1),
        grad_small[0].reshape(-1),
        grad_small[1].reshape(-1),
        grad_small[3].reshape(-1),
        grad_small[4].reshape(-1),
    )


def solution(mesh):
    split_tokens = P("row", "seq", None)
    placed = (split_tokens, split_tokens) + (P(),) * 12 + (split_tokens, P("row", "seq"))
    return jax.shard_map(
        local,
        mesh=mesh,
        in_specs=placed,
        out_specs=(split_tokens, split_tokens) + (P(),) * 12,
        check_vma=False,
    )
```

```python
import functools

import jax
import jax.numpy as jnp
from jax import lax
from jax.experimental import pallas as pl
from jax.experimental.pallas import tpu as pltpu
from jax.sharding import PartitionSpec as P

f32 = jnp.float32
bf16 = jnp.bfloat16
epsilon = 1e-05
lanes = 128
half = 64
chunk = 160
pad_rows = 16
stat_rows = 80
masked = -2e30
lowest = -1e30
feed_step = 256
mib = 1 << 20


def nn(a, b):
    return lax.dot_general(a, b, (((1,), (0,)), ((), ())), preferred_element_type=f32)


def nt(a, b):
    return lax.dot_general(a, b, (((1,), (1,)), ((), ())), preferred_element_type=f32)


def tn(a, b):
    return lax.dot_general(a, b, (((0,), (0,)), ((), ())), preferred_element_type=f32)


def lane_ids(rows):
    return lax.broadcasted_iota(jnp.int32, (rows, lanes), 1)


def swap(values):
    return pltpu.roll(values, half, 1)


def column(row):
    return jnp.transpose(jnp.broadcast_to(row, (lanes, row.shape[1])), (1, 0))


def to_rows(row):
    count = row.shape[1] // lanes
    pieces = [row[:, i * lanes : (i + 1) * lanes] for i in range(count)]
    return jnp.concatenate(pieces + [jnp.zeros((8 - count, lanes), f32)], axis=0)


def from_rows(block, count):
    return jnp.concatenate([block[i : i + 1] for i in range(count)], axis=1)


def wide(values, count):
    return jnp.concatenate([values] * count, axis=1)


def normalized(x):
    centred = x - jnp.mean(x, axis=-1, keepdims=True)
    inverse = lax.rsqrt(jnp.mean(centred * centred, axis=-1, keepdims=True) + epsilon)
    return centred * inverse, inverse


def normalized_back(upstream, unit, inverse, gain):
    scaled = upstream * gain
    inner = (
        scaled
        - jnp.mean(scaled, axis=-1, keepdims=True)
        - unit * jnp.mean(scaled * unit, axis=-1, keepdims=True)
    )
    grad_gain = jnp.sum(upstream * unit, axis=0, keepdims=True)
    return inverse * inner, grad_gain, jnp.sum(upstream, axis=0, keepdims=True)


def row_blocks(rows):
    return [slice(r, r + lanes) for r in range(0, rows, lanes)]


def keys_kernel(tok_in, wkv_in, gain_in, shift_in, seg_in, kvm, n_out, tok, wkv, gain, shift, seg, sems):
    moves = [
        pltpu.make_async_copy(source, target, sems.at[i])
        for i, (source, target) in enumerate(
            ((tok_in, tok), (wkv_in, wkv), (gain_in, gain), (shift_in, shift), (seg_in, seg))
        )
    ]
    for move in moves:
        move.start()
    for move in moves:
        move.wait()
    rows = tok.shape[0]
    for at in row_blocks(rows):
        unit, _ = normalized(tok[at, :].astype(f32))
        normed = (unit * gain[...] + shift[...]).astype(bf16)
        n_out[at, :] = normed
        kvm[at, :] = nn(normed, wkv[...]).astype(bf16)
    seg_row = seg[...].astype(f32)
    ids = to_rows(seg_row)
    line = lax.broadcasted_iota(jnp.int32, (8, lanes), 0)
    ids = jnp.where(line == rows // lanes, seg_row[:, 0:1], ids)
    ids = jnp.where(line == rows // lanes + 1, seg_row[:, rows - 1 : rows], ids)
    ids = jnp.concatenate([ids, jnp.zeros((pad_rows - 8, lanes), f32)], axis=0).astype(bf16)
    kvm[rows : rows + pad_rows, :] = ids


def queries_kernel(
    normed_in, kvm, seg, wq, wroute, choice, qm, q_stack, k_stack, v_stack, gates, picks, seg_out, kvm_out
):
    rows = normed_in.shape[0]
    experts = wroute.shape[0]
    low = lane_ids(lanes) < half
    slot = lax.broadcasted_iota(jnp.int32, (lanes, experts), 1)
    zero = jnp.zeros((lanes, lanes), f32)
    scale = half ** (-0.5)
    for at in row_blocks(rows):
        second_at = slice(rows + at.start, rows + at.stop)
        normed = normed_in[at, :]
        first = column(choice[0:1, at].astype(f32)).astype(jnp.int32)
        second = column(choice[1:2, at].astype(f32)).astype(jnp.int32)
        picks[0, at, :] = first
        picks[1, at, :] = second
        query_all = nn(normed, wq[...])
        one, two = pick_slots(query_all, first, second)
        one = one.astype(bf16).astype(f32) * scale
        two = two.astype(bf16).astype(f32) * scale
        qm[at, :] = jnp.where(low, one, two).astype(bf16)
        q_stack[at, :] = jnp.where(low, one, zero).astype(bf16)
        q_stack[second_at, :] = jnp.where(low, swap(two), zero).astype(bf16)
        seg_out[at, :] = column(seg[:, at].astype(f32))
        kvm_out[at, :] = kvm[at, :]
        kv = kvm[at, :].astype(f32)
        other = swap(kv)
        k_stack[at, :] = jnp.where(low, kv, zero).astype(bf16)
        k_stack[second_at, :] = jnp.where(low, zero, other).astype(bf16)
        v_stack[at, :] = jnp.where(low, other, zero).astype(bf16)
        v_stack[second_at, :] = jnp.where(low, zero, kv).astype(bf16)
        logits = nt(normed, wroute[...])
        picked_one = jnp.sum(jnp.where(slot == first[:, :experts], logits, 0.0), axis=1, keepdims=True)
        picked_two = jnp.sum(jnp.where(slot == second[:, :experts], logits, 0.0), axis=1, keepdims=True)
        top = jnp.maximum(picked_one, picked_two)
        exp_one = jnp.exp(picked_one - top)
        exp_two = jnp.exp(picked_two - top)
        gates[at, :] = jnp.where(low, exp_one, exp_two) / (exp_one + exp_two)
    qm[rows : rows + pad_rows, :] = kvm[rows : rows + pad_rows, :]
    kvm_out[rows : rows + pad_rows, :] = kvm[rows : rows + pad_rows, :]


def pick_slots(values, first, second):
    one = jnp.zeros(first.shape, f32)
    two = jnp.zeros(first.shape, f32)
    first_pair, second_pair = first // 2, second // 2
    for g in range(values.shape[1] // lanes):
        part = values[:, g * lanes : (g + 1) * lanes]
        one = jnp.where(first_pair == g, part, one)
        two = jnp.where(second_pair == g, part, two)
    one = jnp.where(first % 2 == 0, one, swap(one))
    two = jnp.where(second % 2 == 1, two, swap(two))
    return one, two


def id_range(message, rows):
    block = message[rows : rows + pad_rows, :][0:8].astype(f32)
    count = rows // lanes
    return block[count : count + 1], block[count + 1 : count + 2]


def id_row(message, rows):
    block = message[rows : rows + pad_rows, :][0:8].astype(f32)
    return from_rows(block, rows // lanes)


def over_pieces(parts, rows, own, visit):
    own_low, own_high = id_range(own, rows)

    def kind(message):
        low, high = id_range(message, rows)
        meets = jnp.where((low <= own_high) & (high >= own_low), 1.0, 0.0)
        return meets * jnp.where((low == high) & (own_low == own_high), 2.0, 1.0)

    def one(index, i, message, code):
        @pl.when(code == 2)
        def _():
            visit(index, i, message, True)

        @pl.when(code == 1)
        def _():
            visit(index, i, message, False)

    few = [(index, i, part.at[i]) for index, part in enumerate(parts) for i in range(part.shape[0]) if part.shape[0] <= 8]
    if few:
        codes = sum(kind(message) * 4.0**n for n, (_, _, message) in enumerate(few))
        codes = jnp.max(codes).astype(jnp.int32)
    for n, (index, i, message) in enumerate(few):
        one(index, i, message, lax.rem(codes // 4**n, 4))
    for index, part in enumerate(parts):
        if part.shape[0] > 8:

            @pl.loop(0, part.shape[0])
            def _(i, index=index, part=part):
                message = part.at[i]
                one(index, i, message, jnp.max(kind(message)).astype(jnp.int32))


def places(ref, c):
    rows = ref.shape[0] // 2
    return slice(c * chunk, (c + 1) * chunk), slice(rows + c * chunk, rows + (c + 1) * chunk)


def both(ref, c):
    one, two = places(ref, c)
    return jnp.concatenate([ref[one, :], ref[two, :]], axis=0)


def put_both(ref, c, values):
    one, two = places(ref, c)
    ref[one, :] = values[:chunk]
    ref[two, :] = values[chunk:]


def same(seg, c, ids):
    mine = seg[c * chunk : (c + 1) * chunk, :]
    return wide(jnp.concatenate([mine, mine], axis=0), ids.shape[1] // lanes) == ids


def staged(chunks, products, weigh, collect):
    current, ready = products(0), None
    for c in range(chunks):
        following = products(c + 1) if c + 1 < chunks else None
        if ready is not None:
            collect(c - 1, *ready)
        ready = weigh(c, current)
        current = following
    collect(chunks - 1, *ready)


def forward_kernel(piece_count, first, last, stack, seg, own, *rest):
    parts = rest[:piece_count]
    rest = rest[piece_count:]
    if not first:
        total_in, peak_in = rest[:2]
        rest = rest[2:]
    if last:
        heads, lse, total, peak = rest
    else:
        total, peak = rest
    rows = seg.shape[0]
    across = rows // lanes
    if first:
        peak[...] = jnp.full(peak.shape, lowest, f32)
        total[...] = jnp.zeros(total.shape, f32)
    else:
        peak[...] = peak_in[...]
        total[...] = total_in[...]

    def visit(index, i, message, uniform):
        kv = message[0:rows, :]
        low = lane_ids(rows) < half
        values = jnp.where(low, jnp.ones_like(kv), kv)
        if not uniform:
            key_ids = id_row(message, rows)

        def products(c):
            scores = nt(both(stack, c), kv)
            if not uniform:
                scores = jnp.where(same(seg, c, key_ids), scores, masked)
            return scores

        def weigh(c, scores):
            before = both(peak, c)
            now = jnp.maximum(before, jnp.max(scores, axis=1, keepdims=True))
            put_both(peak, c, now)
            return jnp.exp(scores - wide(now, across)).astype(bf16), jnp.exp(before - now)

        def collect(c, weights, factor):
            put_both(total, c, both(total, c) * factor + nn(weights, values))

        staged(rows // chunk, products, weigh, collect)

    over_pieces(parts, rows, own, visit)
    if not last:
        return
    low = lane_ids(lanes) < half
    for at in row_blocks(rows):
        second_at = slice(rows + at.start, rows + at.stop)
        one, two = total[at, :], total[second_at, :]
        one_other, two_other = swap(one), swap(two)
        heads[at, :] = jnp.where(low, one_other, two) / jnp.where(low, one, two_other)
        lse[at, :] = peak[at, :] + jnp.log(jnp.where(low, one, one_other))
        lse[second_at, :] = peak[second_at, :] + jnp.log(jnp.where(low, two, two_other))


def query_back_kernel(spread_out, piece_count, first, last, stack, stack_do, lse, delta, seg, own, *rest):
    parts = rest[:piece_count]
    rest = rest[piece_count:]
    if not first:
        total_in = rest[0]
        rest = rest[1:]
    if last:
        normed, picks, wq, dlog, wroute, keep, send, grad_n, total, spread_keep = rest
    else:
        total = rest[0]
    rows = seg.shape[0]
    across = rows // lanes
    total[...] = jnp.zeros(total.shape, f32) if first else total_in[...]

    def visit(index, i, message, uniform):
        kv = message[0:rows, :]
        if not uniform:
            key_ids = id_row(message, rows)

        def products(c):
            scores = nt(both(stack, c), kv)
            if not uniform:
                scores = jnp.where(same(seg, c, key_ids), scores, masked)
            return scores, nt(both(stack_do, c), kv)

        def weigh(c, pair):
            scores, grad_prob = pair
            prob = jnp.exp(scores - wide(both(lse, c), across))
            return ((prob * (grad_prob - wide(both(delta, c), across))).astype(bf16),)

        def collect(c, grad_scores):
            put_both(total, c, both(total, c) + nn(grad_scores, kv))

        staged(rows // chunk, products, weigh, collect)

    over_pieces(parts, rows, own, visit)
    if not last:
        return
    low = lane_ids(lanes) < half
    scale = half ** (-0.5)
    for at in row_blocks(rows):
        one = total[at, :] * scale
        two = total[slice(rows + at.start, rows + at.stop), :] * scale
        one = jnp.where(low, one, swap(one))
        two = jnp.where(low, two, swap(two))
        spread = spread_slots(one, two, picks[0, at, :], picks[1, at, :], normed.shape[1] // lanes).astype(bf16)
        spread_keep[at, :] = spread
        grad_n[at, :] = nt(spread, wq[...]) + nn(dlog[at, :], wroute[...])
    whole = tn(normed[...], spread_keep[...]).astype(bf16)
    core = place(spread_out)[0]
    count = whole.shape[0] // parts_of
    for i in range(parts_of // 2):
        at = slice(i * count, (i + 1) * count)
        even = whole[2 * i * count : (2 * i + 1) * count]
        odd = whole[(2 * i + 1) * count : (2 * i + 2) * count]
        keep[at, :] = jnp.where(core == 0, even, odd)
        send[at, :] = jnp.where(core == 0, odd, even)


def spread_slots(one, two, first, second, pairs):
    upper = (lane_ids(one.shape[0]) >= half).astype(jnp.int32)
    out = []
    for g in range(pairs):
        expert = 2 * g + upper
        out.append(jnp.where(first == expert, one, jnp.where(second == expert, two, 0.0)))
    return jnp.concatenate(out, axis=1)


def key_back_kernel(spread_out, piece_count, first, last, keys, values, seg, own, *rest):
    q_parts = rest[:piece_count]
    do_parts = rest[piece_count : 2 * piece_count]
    rest = rest[2 * piece_count :]
    if not first:
        k_in, v_in = rest[:2]
        rest = rest[2:]
    if last:
        final_in, final_out = rest[:9] + (place(spread_out)[0],), rest[9:12]
        total_k, total_v, grad_kv, whole = rest[12:]
    else:
        total_k, total_v = rest
    rows = seg.shape[0]
    across = rows // lanes
    if first:
        total_k[...] = jnp.zeros(total_k.shape, f32)
        total_v[...] = jnp.zeros(total_v.shape, f32)
    else:
        total_k[...] = k_in[...]
        total_v[...] = v_in[...]

    def visit(index, i, message, uniform):
        queries = message[0:rows, :]
        sent = do_parts[index].at[i]
        grads = sent[0:rows, :]
        stats = sent[rows : rows + stat_rows, :].astype(f32)

        def stat(first, terms):
            block = stats[first * 8 : first * 8 + 8]
            for t in range(1, terms):
                block = block + stats[(first + t) * 8 : (first + t) * 8 + 8]
            return from_rows(block, across)

        lse = (stat(0, 3), stat(3, 3))
        delta = (stat(6, 2), stat(8, 2))
        if not uniform:
            query_ids = id_row(message, rows)

        def spread(pair):
            return jnp.concatenate(
                [jnp.broadcast_to(pair[0], (chunk, rows)), jnp.broadcast_to(pair[1], (chunk, rows))],
                axis=0,
            )

        def products(c):
            scores = nt(both(keys, c), queries)
            if not uniform:
                scores = jnp.where(same(seg, c, query_ids), scores, masked)
            return scores, nt(both(values, c), grads)

        def weigh(c, pair):
            scores, grad_prob = pair
            prob = jnp.exp(scores - spread(lse))
            return prob.astype(bf16), (prob * (grad_prob - spread(delta))).astype(bf16)

        def collect(c, prob, grad_scores):
            put_both(total_v, c, both(total_v, c) + nn(prob, grads))
            put_both(total_k, c, both(total_k, c) + nn(grad_scores, queries))

        staged(rows // chunk, products, weigh, collect)

    over_pieces(q_parts, rows, own, visit)
    if not last:
        return
    low = lane_ids(lanes) < half
    for at in row_blocks(rows):
        second_at = slice(rows + at.start, rows + at.stop)
        key_grad = total_k[at, :] + swap(total_k[second_at, :])
        value_grad = swap(total_v[at, :]) + total_v[second_at, :]
        grad_kv[at, :] = jnp.where(low, key_grad, value_grad).astype(bf16)
    final_step(*final_in, grad_kv, *final_out, whole)


def middle_kernel(
    spread_out,
    tok, cot, heads, gates, picks, lse, normed, wout, wup, bup, wdown, bdown, gain, shift,
    layer_out, keep, send, grad_mid, dom, do_stack, delta_out, dlog, grad_route, grad_bup, grad_small,
    second_n, second_t, total_y, total_n, mid_keep, mixed_keep, unit_keep, inverse_keep, low_keep, logit_keep,
):
    rows, width = tok.shape
    hidden = wup.shape[1]
    lane = lane_ids(lanes)
    low = lane < half
    pairs = width // lanes
    for at in row_blocks(rows):
        gated = gates[at, :] * heads[at, :]
        turned = swap(gated)
        mixed = spread_slots(
            jnp.where(low, gated, turned), jnp.where(low, turned, gated), picks[0, at, :], picks[1, at, :], pairs
        ).astype(bf16)
        mixed_keep[at, :] = mixed
        middle = tok[at, :].astype(f32) + nn(mixed, wout[...])
        mid_keep[at, :] = middle
        unit, inverse = normalized(middle)
        unit_keep[at, :] = unit
        inverse_keep[at, :] = jnp.broadcast_to(inverse, (lanes, lanes))
        n_two = (unit * gain[...] + shift[...]).astype(bf16)
        second_n[at, :] = n_two
        second_t[:, at] = n_two.T
    total_y[...] = jnp.zeros(total_y.shape, f32)
    total_n[...] = jnp.zeros(total_n.shape, f32)
    step = feed_step
    root = 0.7978845608028654
    cubic = 0.044715
    core = place(spread_out)[0]
    down_rows = hidden // parts_of
    up_rows = width // parts_of
    piece = gradient_rows(width, hidden)

    def put(index, at_row, at_lane, even, odd):
        count, across = even.shape
        start = index * piece + at_row
        target = (slice(start, start + count), slice(at_lane, at_lane + across))
        keep[target] = jnp.where(core == 0, even, odd)
        send[target] = jnp.where(core == 0, odd, even)

    def products(f):
        at = slice(f * step, (f + 1) * step)
        return nn(second_n[...], wup[:, at]) + bup[:, at], nt(cot[...], wdown[at, :])

    def bend(f, pair):
        pre, grad_act = pair
        square = pre * pre
        bent = jnp.tanh(pre * (root + (root * cubic) * square))
        rise = 0.5 + 0.5 * bent
        act = (pre * rise).astype(bf16)
        slope = rise + (pre * (rise * (1.0 - bent))) * (root + (3.0 * root * cubic) * square)
        grad_pre = (grad_act * slope).astype(bf16)
        grad_bup[:, f * step : (f + 1) * step] = jnp.sum(grad_pre.astype(f32), axis=0, keepdims=True)
        return act, grad_pre

    def collect(f, act, grad_pre):
        at = slice(f * step, (f + 1) * step)
        total_y[...] += nn(act, wdown[at, :])
        total_n[...] += nt(grad_pre, wup[:, at])
        grad_down = tn(act, cot[...]).astype(bf16)
        for i in range(step // (2 * down_rows)):
            pair = grad_down[2 * i * down_rows : 2 * (i + 1) * down_rows]
            put(f * (step // (2 * down_rows)) + i, 0, 0, pair[:down_rows], pair[down_rows:])
        grad_up = nn(second_t[...], grad_pre).astype(bf16)
        block_of, at_lane = divmod(f * step, width)
        for i in range(parts_of // 2):
            pair = grad_up[2 * i * up_rows : 2 * (i + 1) * up_rows]
            put(i, down_rows + block_of * up_rows, at_lane, pair[:up_rows], pair[up_rows:])

    staged(hidden // step, products, bend, collect)

    sums = [jnp.zeros((1, width), f32)] * 3
    experts = dlog.shape[1]
    stats = [[], [], [], []]
    zero = jnp.zeros((lanes, lanes), f32)
    for at in row_blocks(rows):
        second_at = slice(rows + at.start, rows + at.stop)
        first, second = picks[0, at, :], picks[1, at, :]
        layer_out[at, :] = (mid_keep[at, :] + total_y[at, :] + bdown[...]).astype(bf16)
        unit = unit_keep[at, :]
        back, grad_gain, grad_shift = normalized_back(total_n[at, :], unit, wide(inverse_keep[at, :], pairs), gain[...])
        dy = cot[at, :].astype(f32)
        grad_middle = dy + back
        grad_mid[at, :] = grad_middle
        sums = [a + b for a, b in zip(sums, (jnp.sum(dy, axis=0, keepdims=True), grad_gain, grad_shift))]
        grad_low = grad_middle.astype(bf16)
        low_keep[at, :] = grad_low
        one, two = pick_slots(nt(grad_low, wout[...]), first, second)
        slots = jnp.where(low, one, two)
        head_values = heads[at, :]
        gate = gates[at, :]
        grad_heads = (gate * slots).astype(bf16)
        dom[at, :] = grad_heads
        carried = grad_heads.astype(f32)
        turned = swap(carried)
        do_stack[at, :] = jnp.where(low, zero, turned).astype(bf16)
        do_stack[second_at, :] = jnp.where(low, zero, carried).astype(bf16)
        gated_grad = slots * head_values
        gate_one = jnp.sum(jnp.where(low, gated_grad, 0.0), axis=1, keepdims=True)
        gate_two = jnp.sum(jnp.where(low, 0.0, gated_grad), axis=1, keepdims=True)
        grad_gate = jnp.where(low, gate_one, gate_two)
        weighted = gate * grad_gate
        grad_logit = gate * (grad_gate - (weighted + swap(weighted)))
        logit_other = swap(grad_logit)
        logit_one = jnp.where(low, grad_logit, logit_other)
        logit_two = jnp.where(low, logit_other, grad_logit)
        grad_logits = jnp.where(lane == first, logit_one, jnp.where(lane == second, logit_two, 0.0)).astype(bf16)
        logit_keep[at, :] = grad_logits
        dlog[at, :] = grad_logits[:, :experts]
        carried = carried * head_values
        delta_one = jnp.broadcast_to(jnp.sum(jnp.where(low, carried, 0.0), axis=1, keepdims=True), (lanes, lanes))
        delta_two = jnp.broadcast_to(jnp.sum(jnp.where(low, 0.0, carried), axis=1, keepdims=True), (lanes, lanes))
        delta_out[at, :] = delta_one
        delta_out[second_at, :] = delta_two
        for store, values in zip(stats, (lse[at, :], lse[second_at, :], delta_one, delta_two)):
            store.append(jnp.transpose(values, (1, 0))[0:1, :])
    blocks = []
    for store, terms in zip(stats, (3, 3, 2, 2)):
        rest = jnp.concatenate(store + [jnp.zeros((8 - len(store), lanes), f32)], axis=0)
        for _ in range(terms):
            part = rest.astype(bf16).astype(f32)
            blocks.append(part)
            rest = rest - part
    dom[rows : rows + stat_rows, :] = jnp.concatenate(blocks, axis=0).astype(bf16)
    grad_small[...] = jnp.concatenate(sums + [jnp.zeros((5, width), f32)], axis=0)
    grad_route[...] = tn(logit_keep[...], normed[...])[:experts, :]
    grad_out = tn(mixed_keep[...], low_keep[...]).astype(bf16)
    for i in range(parts_of // 2):
        pair = grad_out[2 * i * up_rows : 2 * (i + 1) * up_rows]
        put(i, piece - up_rows, 0, pair[:up_rows], pair[up_rows:])


def final_step(
    tok, normed, grad_n, grad_mid, wkv, gain, grad_route, grad_bup, small_two, core_at, grad_kv,
    grad_tokens, keep, send, whole,
):
    width = tok.shape[1]
    whole[0:width, :] = tn(normed[...], grad_kv[...]).astype(bf16)
    grad_gain = grad_shift = jnp.zeros((1, width), f32)
    for at in row_blocks(tok.shape[0]):
        upstream = grad_n[at, :] + nt(grad_kv[at, :], wkv[...])
        unit, inverse = normalized(tok[at, :].astype(f32))
        back, more_gain, more_shift = normalized_back(upstream, unit, inverse, gain[...])
        grad_tokens[at, :] = grad_mid[at, :] + back
        grad_gain, grad_shift = grad_gain + more_gain, grad_shift + more_shift
    rows = [grad_gain, grad_shift] + [small_two[i : i + 1, :] for i in range(3)]
    rows += [grad_bup[:, i : i + width] for i in range(0, grad_bup.shape[1], width)]
    rows += [grad_route[i : i + 1, :] for i in range(grad_route.shape[0])]
    small = jnp.concatenate([row[:, i : i + lanes] for row in rows for i in range(0, width, lanes)], axis=0)
    last = whole.shape[0] - width
    small = jnp.concatenate([small, jnp.zeros((last - small.shape[0], lanes), f32)], axis=0)
    whole[width:, :] = small.astype(bf16)
    core = core_at
    piece = keep.shape[0]
    keep[...] = whole[block(core, piece), :]
    send[...] = whole[block(1 - core, piece), :]


parts_of = 32


def place(spread_out):
    if not spread_out:
        return 0, 0, 0, 0
    row, seq = lax.axis_index("row"), lax.axis_index("seq")
    return lax.rem(row, 2), row // 2, lax.rem(seq, 2), seq // 2


def gradient_rows(width, hidden):
    return hidden // parts_of + (hidden // width + 1) * (width // parts_of)


def block(index, count):
    return pl.ds(pl.multiple_of(index * count, 16), count)


def plus(*refs):
    def get(at):
        total = refs[0][at].astype(f32)
        for ref in refs[1:]:
            total = total + ref[at].astype(f32)
        return total.astype(bf16)

    return get


def after_core_kernel(keep, received, one_keep, one_send, two_keep, two_send):
    _, x, y, _ = place(True)
    piece, upper, lower = keep.shape[0] // 16, one_keep.shape[0] // 8, two_keep.shape[0] // 8
    total = plus(keep, received)

    def part(index, offset, count):
        return total((pl.ds(pl.multiple_of(index * piece + offset, 16), count), slice(None)))

    for zy in range(8):
        here = slice(zy * upper, (zy + 1) * upper)
        one_keep[here, :] = part(zy * 2 + x, 0, upper)
        one_send[here, :] = part(zy * 2 + 1 - x, 0, upper)
    for z in range(4):
        for at_x in range(2):
            here = slice((z * 2 + at_x) * lower, (z * 2 + at_x + 1) * lower)
            two_keep[here, :] = part((z * 2 + y) * 2 + at_x, upper, lower)
            two_send[here, :] = part((z * 2 + 1 - y) * 2 + at_x, upper, lower)


def split_kernel(keep, received, kept, sent):
    x = place(True)[1]
    piece = kept.shape[0] // 8
    total = plus(keep, received)
    for i in range(8):
        here = slice(i * piece, (i + 1) * piece)
        kept[here, :] = total((block(i * 2 + x, piece), slice(None)))
        sent[here, :] = total((block(i * 2 + 1 - x, piece), slice(None)))


def after_first_kernel(one, one_in, extra, extra_in, two, two_in, one_keep, one_send, two_keep, two_send):
    _, x, y, _ = place(True)
    upper = one.shape[0] // 8
    for total, mine, kept, sent, piece, offset in (
        (plus(one, one_in), y, one_keep, one_send, upper, 0),
        (plus(extra, extra_in), y, one_keep, one_send, extra.shape[0] // 8, upper),
        (plus(two, two_in), x, two_keep, two_send, two.shape[0] // 8, 0),
    ):
        stride = kept.shape[0] // 4
        for z in range(4):
            here = slice(z * stride + offset, z * stride + offset + piece)
            kept[here, :] = total((block(z * 2 + mine, piece), slice(None)))
            sent[here, :] = total((block(z * 2 + 1 - mine, piece), slice(None)))


def after_second_kernel(one, one_in, two, two_in, *outs):
    z = place(True)[3]
    at = 0
    for total, count in ((plus(one, one_in), one.shape[0] // 4), (plus(two, two_in), two.shape[0] // 4)):
        for i, out in enumerate(outs):
            out[at : at + count, :] = total((block(z ^ i, count), slice(None)))
        at += count


def sum_kernel(*refs):
    refs[-1][...] = plus(*refs[:-1])(Ellipsis)


def join_halves_kernel(*refs):
    z = place(True)[3]
    one, two = refs[4:]
    upper, lower = one.shape[0] // 4, two.shape[0] // 4
    for i in range(4):
        one[block(z ^ i, upper), :] = refs[i][:upper, :]
        two[block(z ^ i, lower), :] = refs[i][upper:, :]


def unpack_kernel(spread_out, turns, outer, fresh, *refs):
    core, x, y, _ = place(spread_out)
    count = 2 * len(turns)
    parts, refs = refs[:count], refs[count if fresh else count + 4 :]
    outs, stages, sems = refs[:4], refs[4:8], refs[8]
    grad_up, grad_down, grad_out, grad_wq = outs
    width, hidden = grad_up.shape
    down_rows, up_rows = hidden // parts_of, width // parts_of
    moves = []

    def send(stage, start, rows, out, device):
        target = out.at[block(device, rows), :]
        moves.append(pltpu.make_async_copy(stage.at[start : start + rows, :], target, sems.at[len(moves)]))
        moves[-1].start()

    at = 0
    for n, turn in enumerate(turns):
        one, two = parts[2 * n : 2 * n + 2]
        for inner in range(2):
            for z in range(4):
                row, low, high = inner * 4 + z, at * down_rows, at * up_rows
                at += 1
                device = ((z * 2 + (y ^ inner)) * 2 + (x ^ outer)) * 2 + (core ^ turn)
                base = row * (down_rows + up_rows)
                stages[1][low : low + down_rows, :] = one[base : base + down_rows, :].astype(f32)
                send(stages[1], low, down_rows, grad_down, device)
                base += down_rows
                stages[3][high : high + up_rows, :] = one[base : base + up_rows, :].astype(f32)
                send(stages[3], high, up_rows, grad_wq, device)
                device = ((z * 2 + (y ^ outer)) * 2 + (x ^ inner)) * 2 + (core ^ turn)
                across = hidden // width
                base = row * (across + 1) * up_rows
                for c in range(across):
                    value = two[base + c * up_rows : base + (c + 1) * up_rows, :]
                    stages[0][high : high + up_rows, c * width : (c + 1) * width] = value.astype(f32)
                send(stages[0], high, up_rows, grad_up, device)
                base += across * up_rows
                stages[2][high : high + up_rows, :] = two[base : base + up_rows, :].astype(f32)
                send(stages[2], high, up_rows, grad_out, device)
    for move in moves:
        move.wait()


def unpack(spread_out, turns, outer, parts, so_far, width, hidden):
    outs = (shape((width, hidden), f32), shape((hidden, width), f32)) + (shape((width, width), f32),) * 2
    share = 4 // len(turns)
    hbm = pl.BlockSpec(memory_space=pltpu.HBM)
    whole = pl.BlockSpec(memory_space=pltpu.VMEM)
    return pl.pallas_call(
        functools.partial(unpack_kernel, spread_out, turns, outer, not so_far),
        out_shape=outs,
        in_specs=[whole] * len(parts) + [hbm] * len(so_far),
        out_specs=(hbm,) * 4,
        scratch_shapes=[pltpu.VMEM((out.shape[0] // share, out.shape[1]), f32) for out in outs]
        + [pltpu.SemaphoreType.DMA((32 * len(turns),))],
        input_output_aliases={len(parts) + i: i for i in range(len(so_far))},
        compiler_params=pltpu.CompilerParams(vmem_limit_bytes=16 * mib),
        cost_estimate=pl.CostEstimate(flops=int(2 * unpack_weight * busy), bytes_accessed=0, transcendentals=0),
    )(*parts, *so_far)


def flip_row(x, mask):
    return lax.ppermute(x, "row", [(i, i ^ mask) for i in range(4)])


def flip_seq(x, mask):
    return lax.ppermute(x, "seq", [(i, i ^ mask) for i in range(8)])


def simple(kernel, outs, *operands):
    return call(kernel, outs, [], 10 * mib, 0.5 * small_weight, *operands)


def add(a, b):
    return (a.astype(f32) + b.astype(f32)).astype(bf16)


def finish_sums(large, small, hidden):
    mine, arrived = large
    keep, send = small
    count, width = mine.shape
    total = add(keep, after(flip_row(send, 1), mine))
    part = shape((2 * count, width), bf16)
    one, two = simple(join_halves_kernel, (part,) * 2, mine, *arrived)
    one_in, two_in = flip_seq(one, 1), flip_row(two, 2)
    total = add(total, after(flip_row(total, 2), one))
    one, two = jnp.concatenate([one, one_in]), jnp.concatenate([two, two_in])
    one_in, two_in = flip_row(one, 2), flip_seq(two, 1)
    one_other, two_other = flip_row(one, 1), flip_row(two, 1)
    total = add(total, after(flip_seq(total, 1), one, two))
    done = unpack(True, (0, 1), 0, (one, two, one_other, two_other), (), width, hidden)
    total = add(total, flip_seq(total, 2))
    total = add(total, after(flip_seq(total, 4), done[3]))
    one_in = after(one_in, total)
    other = flip_row(total, 1)
    one_other, two_other = flip_row(one_in, 1), flip_row(two_in, 1)
    done = unpack(True, (0,), 1, (one_in, two_in), done, width, hidden)
    done = unpack(True, (1,), 1, (one_other, two_other), done, width, hidden)
    return done, (total, other)


def unpack_small_kernel(spread_out, mine, other, grad_wkv, grad_route, grad_bup, *rest):
    small, whole = rest[:5], rest[5]
    core = place(spread_out)[0]
    piece = mine.shape[0]
    whole[block(core, piece), :] = mine[...].astype(f32)
    whole[block(1 - core, piece), :] = other[...].astype(f32)
    width = grad_wkv.shape[0]
    across = width // lanes
    grad_wkv[...] = whole[0:width, :]
    at = width
    for i in range(5):
        for g in range(across):
            small[i][:, g * lanes : (g + 1) * lanes] = whole[at : at + 1, :]
            at += 1
    for g in range(grad_bup.shape[1] // lanes):
        grad_bup[:, g * lanes : (g + 1) * lanes] = whole[at : at + 1, :]
        at += 1
    for i in range(grad_route.shape[0]):
        for g in range(across):
            grad_route[i : i + 1, g * lanes : (g + 1) * lanes] = whole[at : at + 1, :]
            at += 1


busy = 400_000_000
key_weight, query_weight, forward_weight, final_weight, unpack_weight, small_weight = 1.0, 1.0, 1.0, 1.0, 1.0, 1.0


def call(kernel, out_shape, scratch, limit, time, *operands):
    whole = pl.BlockSpec(memory_space=pltpu.VMEM)
    return pl.pallas_call(
        kernel,
        out_shape=out_shape,
        in_specs=[whole] * len(operands),
        out_specs=jax.tree.map(lambda _: whole, out_shape),
        scratch_shapes=scratch,
        compiler_params=pltpu.CompilerParams(vmem_limit_bytes=limit),
        cost_estimate=pl.CostEstimate(flops=int(time * busy), bytes_accessed=0, transcendentals=0),
    )(*operands)


def shape(dims, dtype):
    return jax.ShapeDtypeStruct(tuple(dims), dtype)


def after(value, *earlier):
    return lax.optimization_barrier((value,) + earlier)[0]


def local(
    tokens, cotangent, w_query, w_kv, w_route, w_out, w_up, bias_up, w_down, bias_down,
    gain_one, shift_one, gain_two, shift_two, choices, segment_ids,
):
    size = lax.axis_size("seq")
    tok, cot = tokens[0], cotangent[0]
    rows, width = tok.shape
    hidden = w_up.shape[1]
    route = w_route.T
    experts = route.shape[0]
    row = lambda v: v.reshape(1, -1)
    message = shape((rows + pad_rows, lanes), bf16)
    stacked = (2 * rows, lanes)
    stack = shape(stacked, bf16)
    hbm = pl.BlockSpec(memory_space=pltpu.HBM)
    whole = pl.BlockSpec(memory_space=pltpu.VMEM)
    sent_keys, normed = pl.pallas_call(
        keys_kernel,
        out_shape=(message, shape((rows, width), bf16)),
        in_specs=[hbm] * 5,
        out_specs=(whole,) * 2,
        scratch_shapes=[
            pltpu.VMEM((rows, width), bf16), pltpu.VMEM((width, lanes), bf16), pltpu.VMEM((1, width), f32),
            pltpu.VMEM((1, width), f32), pltpu.VMEM((1, rows), jnp.int32), pltpu.SemaphoreType.DMA((5,)),
        ],
        compiler_params=pltpu.CompilerParams(vmem_limit_bytes=60 * mib),
        cost_estimate=pl.CostEstimate(flops=busy, bytes_accessed=0, transcendentals=0),
    )(tok, w_kv, row(gain_one), row(shift_one), segment_ids)
    spread_out = size == 8 and lax.axis_size("row") == 4
    qm, q_stack, k_stack, v_stack, gates, picks, seg, kvm = call(
        queries_kernel,
        (
            message, stack, stack, stack, shape((rows, lanes), f32), shape((2, rows, lanes), jnp.int32),
            shape((rows, lanes), f32), message,
        ),
        [], 12 * mib, 1.6,
        normed, sent_keys, segment_ids, w_query, route, choices[0].T,
    )
    state = (shape(stacked, f32),) * 2
    finished = (shape((rows, lanes), f32), shape(stacked, f32)) + state

    def forward(parts, first, last, *so_far):
        return call(
            functools.partial(forward_kernel, len(parts), first, last), finished if last else state, [], 12 * mib,
            1.4 * forward_weight * len(parts) * parts[0].shape[0], q_stack, seg, kvm, *parts, *so_far,
        )

    if size == 8:
        far_z, near_z, near_y = flip_seq(sent_keys, 4), flip_seq(sent_keys, 2), flip_seq(sent_keys, 1)
        near_y, near_z, far_z, q_stack, kvm = lax.optimization_barrier((near_y, near_z, far_z, q_stack, kvm))
        near = [m[None] for m in (kvm, near_y, near_z, far_z)]
        others = [flip_seq(near_z, 1), flip_seq(far_z, 1), flip_seq(far_z, 2), flip_seq(after(sent_keys, far_z), 7)]
        others = [m[None] for m in others]
        so_far = forward(near, True, False)
        heads, lse, _, _ = forward(others, False, True, *so_far)
        q_two = jnp.stack([qm, after(flip_seq(qm, 1), so_far[0])])
        q_far = [flip_seq(q_two, 2), flip_seq(q_two, 4)]
        heads = after(heads, q_two)
    else:
        all_kv = [lax.all_gather(kvm, "seq", axis=0, tiled=False)]
        heads, lse, _, _ = forward(all_kv, True, True)
    piece = gradient_rows(width, hidden)
    gradients = shape((piece * parts_of // 2, width), bf16)
    (
        layer_out, keep, send, grad_mid, dom, do_stack, delta, dlog, grad_route, grad_bup, small_two,
    ) = call(
        functools.partial(middle_kernel, spread_out),
        (
            shape((rows, width), bf16), gradients, gradients, shape((rows, width), f32), shape((rows + stat_rows, lanes), bf16),
            stack, shape(stacked, f32), shape((rows, experts), bf16), shape((experts, width), f32),
            shape((1, hidden), f32), shape((8, width), f32),
        ),
        [
            pltpu.VMEM((rows, width), bf16), pltpu.VMEM((width, rows), bf16), pltpu.VMEM((rows, width), f32),
            pltpu.VMEM((rows, width), f32), pltpu.VMEM((rows, width), f32), pltpu.VMEM((rows, width), bf16),
            pltpu.VMEM((rows, width), f32), pltpu.VMEM((rows, lanes), f32), pltpu.VMEM((rows, width), bf16),
            pltpu.VMEM((rows, lanes), bf16),
        ],
        34 * mib, 15,
        tok, cot, heads, gates, picks, lse, normed, w_out, w_up, row(bias_up), w_down, row(bias_down),
        row(gain_two), row(shift_two),
    )
    results = {}
    extra_part = shape((width // 2, width), bf16)

    def query_back(parts, first, last, *earlier):
        finish = (normed, picks, w_query, dlog, route) if last else ()
        outs = (extra_part, extra_part, shape((rows, width), f32)) if last else ()
        results["query"] = call(
            functools.partial(query_back_kernel, spread_out, len(parts), first, last),
            outs + (shape(stacked, f32),),
            [pltpu.VMEM((rows, width), bf16)] if last else [],
            14 * mib, 1.6 * query_weight * len(parts) * parts[0].shape[0],
            after(q_stack, *earlier), do_stack, lse, delta, seg, kvm, *parts, *(() if first else results["query"]), *finish,
        )
        return results["query"][-1]

    extra = 5 + hidden // width + experts
    small_rows = extra * (width // lanes) + width
    small_rows = -(-small_rows // 32) * 32

    def key_back(q_parts, do_parts, first, last, *earlier):
        part = shape((small_rows // 2, lanes), bf16)
        final = (
            tok, normed, results["query"][2], grad_mid, w_kv, row(gain_one), grad_route, grad_bup, small_two,
        ) if last else ()
        results["key"] = call(
            functools.partial(key_back_kernel, spread_out, len(q_parts), first, last),
            ((shape((rows, width), f32), part, part) if last else ()) + state,
            [pltpu.VMEM((rows, lanes), bf16), pltpu.VMEM((small_rows, lanes), bf16)] if last else [],
            18 * mib, 2.1 * key_weight * len(q_parts) * q_parts[0].shape[0] + 2.4 * last,
            after(k_stack, *earlier), v_stack, seg, kvm, *q_parts, *do_parts, *(() if first else results["key"]), *final,
        )
        return results["key"][-1]

    if spread_out:
        send, q_near, q_other = lax.optimization_barrier((send, *q_far))
        q_last = flip_seq(q_other, 2)
        received = flip_row(send, 1)
        d_two = jnp.stack([dom, flip_seq(dom, 1)])
        received = after(received, query_back(near, True, False))
        upper, lower = hidden // parts_of, piece - hidden // parts_of
        more = width // parts_of
        part = lambda count, rows: shape((count * rows, width), bf16)
        one, one_send, two, two_send = simple(
            after_core_kernel, (part(8, upper),) * 2 + (part(8, lower),) * 2, keep, received
        )
        one_in, two_in = flip_row(one_send, 2), flip_seq(two_send, 1)
        d_other, d_near = flip_seq(d_two, 4), flip_seq(d_two, 2)
        query_back(others, False, True, one, d_two, q_last)
        extra, extra_send, _, done = results["query"]
        extra, extra_send = simple(split_kernel, (part(8, more),) * 2, extra, flip_row(extra_send, 1))
        extra_in = flip_row(extra_send, 2)
        done = key_back([q_two], [d_two], True, False, extra, d_other)
        d_last = flip_seq(after(d_other, done), 2)
        one, one_send, two, two_send = simple(
            after_first_kernel, (part(4, upper + more),) * 2 + (part(4, lower),) * 2,
            one, after(one_in, done), extra, extra_in, two, two_in,
        )
        one_in, two_in = flip_seq(one_send, 1), flip_row(two_send, 2)
        done = key_back([q_other], [d_other], False, False, one)
        sent = simple(after_second_kernel, (part(1, piece + more),) * 4, one, after(one_in, done), two, two_in)
        planes = [flip_seq(sent[i], 2 * i) for i in (1, 2, 3)]
        key_back([q_near], [d_near], False, False, sent[0])
        key_back([q_last], [d_last], False, True)
        grad_tokens, *small = results["key"][:3]
        mine = simple(sum_kernel, part(1, piece + more), after(sent[0], small[0]), *planes)
        arrived = [flip_seq(mine, 2 * i) for i in (1, 2, 3)]
        large, small = finish_sums((mine, arrived), small, hidden)
    else:
        query_back(all_kv, True, True)
        gathered = [lax.all_gather(m, "seq", axis=0, tiled=False) for m in (qm, dom)]
        key_back(gathered[:1], gathered[1:], True, True)
        grad_tokens, *small = results["key"][:3]
        small = lax.psum(small, ("seq", "row"))
        sums = lax.psum((keep, send, *results["query"][:2]), ("seq", "row"))
        large = []
        upper = hidden // parts_of
        for total, more in zip(sums[:2], sums[2:]):
            cube = total.reshape(4, 2, 2, piece, width)
            more = more.reshape(4, 2, 2, -1, width)
            one = jnp.concatenate([cube[:, :, :, :upper], more], axis=3)
            two = cube[:, :, :, upper:]
            for i in range(2):
                large.append(one[:, :, i].transpose(1, 0, 2, 3).reshape(-1, width))
                large.append(two[:, i].transpose(1, 0, 2, 3).reshape(-1, width))
        done = unpack(False, (0, 1), 0, (large[0], large[1], large[4], large[5]), (), width, hidden)
        done = unpack(False, (0,), 1, large[2:4], done, width, hidden)
        large = unpack(False, (1,), 1, large[6:8], done, width, hidden)
    grad_wkv, grad_route, grad_bup, *grad_small = call(
        functools.partial(unpack_small_kernel, spread_out),
        (
            shape((width, lanes), f32), shape((experts, width), f32), shape((1, hidden), f32),
        ) + (shape((1, width), f32),) * 5,
        [pltpu.VMEM((small_rows, lanes), f32)], 8 * mib, 0.8, *small,
    )
    grad_up, grad_down, grad_out, grad_wq = large
    return (
        layer_out[None],
        grad_tokens[None],
        grad_wq,
        grad_wkv,
        grad_route.T,
        grad_out,
        grad_up,
        grad_bup.reshape(-1),
        grad_down,
        grad_small[2].reshape(-1),
        grad_small[0].reshape(-1),
        grad_small[1].reshape(-1),
        grad_small[3].reshape(-1),
        grad_small[4].reshape(-1),
    )


def solution(mesh):
    split_tokens = P("row", "seq", None)
    placed = (split_tokens, split_tokens) + (P(),) * 12 + (split_tokens, P("row", "seq"))
    return jax.shard_map(
        local,
        mesh=mesh,
        in_specs=placed,
        out_specs=(split_tokens, split_tokens) + (P(),) * 12,
        check_vma=False,
    )
```

```python
import functools

import jax
import jax.numpy as jnp
from jax import lax
from jax.experimental import pallas as pl
from jax.experimental.pallas import tpu as pltpu
from jax.sharding import PartitionSpec as P

f32 = jnp.float32
bf16 = jnp.bfloat16
epsilon = 1e-05
lanes = 128
half = 64
chunk = 160
pad_rows = 16
stat_rows = 80
masked = -2e30
lowest = -1e30
feed_step = 256
mib = 1 << 20


def nn(a, b):
    return lax.dot_general(a, b, (((1,), (0,)), ((), ())), preferred_element_type=f32)


def nt(a, b):
    return lax.dot_general(a, b, (((1,), (1,)), ((), ())), preferred_element_type=f32)


def tn(a, b):
    return lax.dot_general(a, b, (((0,), (0,)), ((), ())), preferred_element_type=f32)


def lane_ids(rows):
    return lax.broadcasted_iota(jnp.int32, (rows, lanes), 1)


def swap(values):
    return pltpu.roll(values, half, 1)


def column(row):
    return jnp.transpose(jnp.broadcast_to(row, (lanes, row.shape[1])), (1, 0))


def to_rows(row):
    count = row.shape[1] // lanes
    pieces = [row[:, i * lanes : (i + 1) * lanes] for i in range(count)]
    return jnp.concatenate(pieces + [jnp.zeros((8 - count, lanes), f32)], axis=0)


def from_rows(block, count):
    return jnp.concatenate([block[i : i + 1] for i in range(count)], axis=1)


def wide(values, count):
    return jnp.concatenate([values] * count, axis=1)


def normalized(x):
    centred = x - jnp.mean(x, axis=-1, keepdims=True)
    inverse = lax.rsqrt(jnp.mean(centred * centred, axis=-1, keepdims=True) + epsilon)
    return centred * inverse, inverse


def normalized_back(upstream, unit, inverse, gain):
    scaled = upstream * gain
    inner = (
        scaled
        - jnp.mean(scaled, axis=-1, keepdims=True)
        - unit * jnp.mean(scaled * unit, axis=-1, keepdims=True)
    )
    grad_gain = jnp.sum(upstream * unit, axis=0, keepdims=True)
    return inverse * inner, grad_gain, jnp.sum(upstream, axis=0, keepdims=True)


def row_blocks(rows):
    return [slice(r, r + lanes) for r in range(0, rows, lanes)]


def keys_kernel(tok_in, wkv_in, gain_in, shift_in, seg_in, kvm, n_out, tok, wkv, gain, shift, seg, sems):
    moves = [
        pltpu.make_async_copy(source, target, sems.at[i])
        for i, (source, target) in enumerate(
            ((tok_in, tok), (wkv_in, wkv), (gain_in, gain), (shift_in, shift), (seg_in, seg))
        )
    ]
    for move in moves:
        move.start()
    for move in moves:
        move.wait()
    rows = tok.shape[0]
    for at in row_blocks(rows):
        unit, _ = normalized(tok[at, :].astype(f32))
        normed = (unit * gain[...] + shift[...]).astype(bf16)
        n_out[at, :] = normed
        kvm[at, :] = nn(normed, wkv[...]).astype(bf16)
    seg_row = seg[...].astype(f32)
    ids = to_rows(seg_row)
    line = lax.broadcasted_iota(jnp.int32, (8, lanes), 0)
    ids = jnp.where(line == rows // lanes, seg_row[:, 0:1], ids)
    ids = jnp.where(line == rows // lanes + 1, seg_row[:, rows - 1 : rows], ids)
    ids = jnp.concatenate([ids, jnp.zeros((pad_rows - 8, lanes), f32)], axis=0).astype(bf16)
    kvm[rows : rows + pad_rows, :] = ids


def queries_kernel(
    normed_in, kvm, seg, wq, wroute, choice, qm, q_stack, k_stack, v_stack, gates, picks, seg_out, kvm_out
):
    rows = normed_in.shape[0]
    experts = wroute.shape[0]
    low = lane_ids(lanes) < half
    slot = lax.broadcasted_iota(jnp.int32, (lanes, experts), 1)
    zero = jnp.zeros((lanes, lanes), f32)
    scale = half ** (-0.5)
    for at in row_blocks(rows):
        second_at = slice(rows + at.start, rows + at.stop)
        normed = normed_in[at, :]
        first = column(choice[0:1, at].astype(f32)).astype(jnp.int32)
        second = column(choice[1:2, at].astype(f32)).astype(jnp.int32)
        picks[0, at, :] = first
        picks[1, at, :] = second
        query_all = nn(normed, wq[...])
        one, two = pick_slots(query_all, first, second)
        one = one.astype(bf16).astype(f32) * scale
        two = two.astype(bf16).astype(f32) * scale
        qm[at, :] = jnp.where(low, one, two).astype(bf16)
        q_stack[at, :] = jnp.where(low, one, zero).astype(bf16)
        q_stack[second_at, :] = jnp.where(low, swap(two), zero).astype(bf16)
        seg_out[at, :] = column(seg[:, at].astype(f32))
        kvm_out[at, :] = kvm[at, :]
        kv = kvm[at, :].astype(f32)
        other = swap(kv)
        k_stack[at, :] = jnp.where(low, kv, zero).astype(bf16)
        k_stack[second_at, :] = jnp.where(low, zero, other).astype(bf16)
        v_stack[at, :] = jnp.where(low, other, zero).astype(bf16)
        v_stack[second_at, :] = jnp.where(low, zero, kv).astype(bf16)
        logits = nt(normed, wroute[...])
        picked_one = jnp.sum(jnp.where(slot == first[:, :experts], logits, 0.0), axis=1, keepdims=True)
        picked_two = jnp.sum(jnp.where(slot == second[:, :experts], logits, 0.0), axis=1, keepdims=True)
        top = jnp.maximum(picked_one, picked_two)
        exp_one = jnp.exp(picked_one - top)
        exp_two = jnp.exp(picked_two - top)
        gates[at, :] = jnp.where(low, exp_one, exp_two) / (exp_one + exp_two)
    qm[rows : rows + pad_rows, :] = kvm[rows : rows + pad_rows, :]
    kvm_out[rows : rows + pad_rows, :] = kvm[rows : rows + pad_rows, :]


def pick_slots(values, first, second):
    one = jnp.zeros(first.shape, f32)
    two = jnp.zeros(first.shape, f32)
    first_pair, second_pair = first // 2, second // 2
    for g in range(values.shape[1] // lanes):
        part = values[:, g * lanes : (g + 1) * lanes]
        one = jnp.where(first_pair == g, part, one)
        two = jnp.where(second_pair == g, part, two)
    one = jnp.where(first % 2 == 0, one, swap(one))
    two = jnp.where(second % 2 == 1, two, swap(two))
    return one, two


def id_range(message, rows):
    block = message[rows : rows + pad_rows, :][0:8].astype(f32)
    count = rows // lanes
    return block[count : count + 1], block[count + 1 : count + 2]


def id_row(message, rows):
    block = message[rows : rows + pad_rows, :][0:8].astype(f32)
    return from_rows(block, rows // lanes)


def over_pieces(parts, rows, own, visit):
    own_low, own_high = id_range(own, rows)

    def kind(message):
        low, high = id_range(message, rows)
        meets = jnp.where((low <= own_high) & (high >= own_low), 1.0, 0.0)
        return meets * jnp.where((low == high) & (own_low == own_high), 2.0, 1.0)

    def one(index, i, message, code):
        @pl.when(code == 2)
        def _():
            visit(index, i, message, True)

        @pl.when(code == 1)
        def _():
            visit(index, i, message, False)

    few = [(index, i, part.at[i]) for index, part in enumerate(parts) for i in range(part.shape[0]) if part.shape[0] <= 8]
    if few:
        codes = sum(kind(message) * 4.0**n for n, (_, _, message) in enumerate(few))
        codes = jnp.max(codes).astype(jnp.int32)
    for n, (index, i, message) in enumerate(few):
        one(index, i, message, lax.rem(codes // 4**n, 4))
    for index, part in enumerate(parts):
        if part.shape[0] > 8:

            @pl.loop(0, part.shape[0])
            def _(i, index=index, part=part):
                message = part.at[i]
                one(index, i, message, jnp.max(kind(message)).astype(jnp.int32))


def places(ref, c):
    rows = ref.shape[0] // 2
    return slice(c * chunk, (c + 1) * chunk), slice(rows + c * chunk, rows + (c + 1) * chunk)


def both(ref, c):
    one, two = places(ref, c)
    return jnp.concatenate([ref[one, :], ref[two, :]], axis=0)


def put_both(ref, c, values):
    one, two = places(ref, c)
    ref[one, :] = values[:chunk]
    ref[two, :] = values[chunk:]


def same(seg, c, ids):
    mine = seg[c * chunk : (c + 1) * chunk, :]
    return wide(jnp.concatenate([mine, mine], axis=0), ids.shape[1] // lanes) == ids


def staged(chunks, products, weigh, collect):
    current, ready = products(0), None
    for c in range(chunks):
        following = products(c + 1) if c + 1 < chunks else None
        if ready is not None:
            collect(c - 1, *ready)
        ready = weigh(c, current)
        current = following
    collect(chunks - 1, *ready)


def forward_kernel(piece_count, first, last, stack, seg, own, *rest):
    parts = rest[:piece_count]
    rest = rest[piece_count:]
    if not first:
        total_in, peak_in = rest[:2]
        rest = rest[2:]
    if last:
        heads, lse, total, peak = rest
    else:
        total, peak = rest
    rows = seg.shape[0]
    across = rows // lanes
    if first:
        peak[...] = jnp.full(peak.shape, lowest, f32)
        total[...] = jnp.zeros(total.shape, f32)
    else:
        peak[...] = peak_in[...]
        total[...] = total_in[...]

    def visit(index, i, message, uniform):
        kv = message[0:rows, :]
        low = lane_ids(rows) < half
        values = jnp.where(low, jnp.ones_like(kv), kv)
        if not uniform:
            key_ids = id_row(message, rows)

        def products(c):
            scores = nt(both(stack, c), kv)
            if not uniform:
                scores = jnp.where(same(seg, c, key_ids), scores, masked)
            return scores

        def weigh(c, scores):
            before = both(peak, c)
            now = jnp.maximum(before, jnp.max(scores, axis=1, keepdims=True))
            put_both(peak, c, now)
            return jnp.exp(scores - wide(now, across)).astype(bf16), jnp.exp(before - now)

        def collect(c, weights, factor):
            put_both(total, c, both(total, c) * factor + nn(weights, values))

        staged(rows // chunk, products, weigh, collect)

    over_pieces(parts, rows, own, visit)
    if not last:
        return
    low = lane_ids(lanes) < half
    for at in row_blocks(rows):
        second_at = slice(rows + at.start, rows + at.stop)
        one, two = total[at, :], total[second_at, :]
        one_other, two_other = swap(one), swap(two)
        heads[at, :] = jnp.where(low, one_other, two) / jnp.where(low, one, two_other)
        lse[at, :] = peak[at, :] + jnp.log(jnp.where(low, one, one_other))
        lse[second_at, :] = peak[second_at, :] + jnp.log(jnp.where(low, two, two_other))


def query_back_kernel(spread_out, piece_count, first, last, stack, stack_do, lse, delta, seg, own, *rest):
    parts = rest[:piece_count]
    rest = rest[piece_count:]
    if not first:
        total_in = rest[0]
        rest = rest[1:]
    if last:
        normed, picks, wq, dlog, wroute, keep, send, grad_n, total, spread_keep = rest
    else:
        total = rest[0]
    rows = seg.shape[0]
    across = rows // lanes
    total[...] = jnp.zeros(total.shape, f32) if first else total_in[...]

    def visit(index, i, message, uniform):
        kv = message[0:rows, :]
        if not uniform:
            key_ids = id_row(message, rows)

        def products(c):
            scores = nt(both(stack, c), kv)
            if not uniform:
                scores = jnp.where(same(seg, c, key_ids), scores, masked)
            return scores, nt(both(stack_do, c), kv)

        def weigh(c, pair):
            scores, grad_prob = pair
            prob = jnp.exp(scores - wide(both(lse, c), across))
            return ((prob * (grad_prob - wide(both(delta, c), across))).astype(bf16),)

        def collect(c, grad_scores):
            put_both(total, c, both(total, c) + nn(grad_scores, kv))

        staged(rows // chunk, products, weigh, collect)

    over_pieces(parts, rows, own, visit)
    if not last:
        return
    low = lane_ids(lanes) < half
    scale = half ** (-0.5)
    for at in row_blocks(rows):
        one = total[at, :] * scale
        two = total[slice(rows + at.start, rows + at.stop), :] * scale
        one = jnp.where(low, one, swap(one))
        two = jnp.where(low, two, swap(two))
        spread = spread_slots(one, two, picks[0, at, :], picks[1, at, :], normed.shape[1] // lanes).astype(bf16)
        spread_keep[at, :] = spread
        grad_n[at, :] = nt(spread, wq[...]) + nn(dlog[at, :], wroute[...])
    whole = tn(normed[...], spread_keep[...]).astype(bf16)
    core = place(spread_out)[0]
    count = whole.shape[0] // parts_of
    for i in range(parts_of // 2):
        at = slice(i * count, (i + 1) * count)
        even = whole[2 * i * count : (2 * i + 1) * count]
        odd = whole[(2 * i + 1) * count : (2 * i + 2) * count]
        keep[at, :] = jnp.where(core == 0, even, odd)
        send[at, :] = jnp.where(core == 0, odd, even)


def spread_slots(one, two, first, second, pairs):
    upper = (lane_ids(one.shape[0]) >= half).astype(jnp.int32)
    out = []
    for g in range(pairs):
        expert = 2 * g + upper
        out.append(jnp.where(first == expert, one, jnp.where(second == expert, two, 0.0)))
    return jnp.concatenate(out, axis=1)


def key_back_kernel(spread_out, piece_count, first, last, keys, values, seg, own, *rest):
    q_parts = rest[:piece_count]
    do_parts = rest[piece_count : 2 * piece_count]
    rest = rest[2 * piece_count :]
    if not first:
        k_in, v_in = rest[:2]
        rest = rest[2:]
    if last:
        final_in, final_out = rest[:9] + (place(spread_out)[0],), rest[9:12]
        total_k, total_v, grad_kv, whole = rest[12:]
    else:
        total_k, total_v = rest
    rows = seg.shape[0]
    across = rows // lanes
    if first:
        total_k[...] = jnp.zeros(total_k.shape, f32)
        total_v[...] = jnp.zeros(total_v.shape, f32)
    else:
        total_k[...] = k_in[...]
        total_v[...] = v_in[...]

    def visit(index, i, message, uniform):
        queries = message[0:rows, :]
        sent = do_parts[index].at[i]
        grads = sent[0:rows, :]
        stats = sent[rows : rows + stat_rows, :].astype(f32)

        def stat(first, terms):
            block = stats[first * 8 : first * 8 + 8]
            for t in range(1, terms):
                block = block + stats[(first + t) * 8 : (first + t) * 8 + 8]
            return from_rows(block, across)

        lse = (stat(0, 3), stat(3, 3))
        delta = (stat(6, 2), stat(8, 2))
        if not uniform:
            query_ids = id_row(message, rows)

        def spread(pair):
            return jnp.concatenate(
                [jnp.broadcast_to(pair[0], (chunk, rows)), jnp.broadcast_to(pair[1], (chunk, rows))],
                axis=0,
            )

        def products(c):
            scores = nt(both(keys, c), queries)
            if not uniform:
                scores = jnp.where(same(seg, c, query_ids), scores, masked)
            return scores, nt(both(values, c), grads)

        def weigh(c, pair):
            scores, grad_prob = pair
            prob = jnp.exp(scores - spread(lse))
            return prob.astype(bf16), (prob * (grad_prob - spread(delta))).astype(bf16)

        def collect(c, prob, grad_scores):
            put_both(total_v, c, both(total_v, c) + nn(prob, grads))
            put_both(total_k, c, both(total_k, c) + nn(grad_scores, queries))

        staged(rows // chunk, products, weigh, collect)

    over_pieces(q_parts, rows, own, visit)
    if not last:
        return
    low = lane_ids(lanes) < half
    for at in row_blocks(rows):
        second_at = slice(rows + at.start, rows + at.stop)
        key_grad = total_k[at, :] + swap(total_k[second_at, :])
        value_grad = swap(total_v[at, :]) + total_v[second_at, :]
        grad_kv[at, :] = jnp.where(low, key_grad, value_grad).astype(bf16)
    final_step(*final_in, grad_kv, *final_out, whole)


def middle_kernel(
    spread_out,
    tok, cot, heads, gates, picks, lse, normed, wout, wup, bup, wdown, bdown, gain, shift,
    layer_out, keep, send, grad_mid, dom, do_stack, delta_out, dlog, grad_route, grad_bup, grad_small,
    second_n, second_t, total_y, total_n, mid_keep, mixed_keep, unit_keep, inverse_keep, low_keep, logit_keep,
):
    rows, width = tok.shape
    hidden = wup.shape[1]
    lane = lane_ids(lanes)
    low = lane < half
    pairs = width // lanes
    for at in row_blocks(rows):
        gated = gates[at, :] * heads[at, :]
        turned = swap(gated)
        mixed = spread_slots(
            jnp.where(low, gated, turned), jnp.where(low, turned, gated), picks[0, at, :], picks[1, at, :], pairs
        ).astype(bf16)
        mixed_keep[at, :] = mixed
        middle = tok[at, :].astype(f32) + nn(mixed, wout[...])
        mid_keep[at, :] = middle
        unit, inverse = normalized(middle)
        unit_keep[at, :] = unit
        inverse_keep[at, :] = jnp.broadcast_to(inverse, (lanes, lanes))
        n_two = (unit * gain[...] + shift[...]).astype(bf16)
        second_n[at, :] = n_two
        second_t[:, at] = n_two.T
    total_y[...] = jnp.zeros(total_y.shape, f32)
    total_n[...] = jnp.zeros(total_n.shape, f32)
    step = feed_step
    root = 0.7978845608028654
    cubic = 0.044715
    core = place(spread_out)[0]
    down_rows = hidden // parts_of
    up_rows = width // parts_of
    piece = gradient_rows(width, hidden)

    def put(index, at_row, at_lane, even, odd):
        count, across = even.shape
        start = index * piece + at_row
        target = (slice(start, start + count), slice(at_lane, at_lane + across))
        keep[target] = jnp.where(core == 0, even, odd)
        send[target] = jnp.where(core == 0, odd, even)

    def products(f):
        at = slice(f * step, (f + 1) * step)
        return nn(second_n[...], wup[:, at]) + bup[:, at], nt(cot[...], wdown[at, :])

    def bend(f, pair):
        pre, grad_act = pair
        square = pre * pre
        bent = jnp.tanh(pre * (root + (root * cubic) * square))
        rise = 0.5 + 0.5 * bent
        act = (pre * rise).astype(bf16)
        slope = rise + (pre * (rise * (1.0 - bent))) * (root + (3.0 * root * cubic) * square)
        grad_pre = (grad_act * slope).astype(bf16)
        grad_bup[:, f * step : (f + 1) * step] = jnp.sum(grad_pre.astype(f32), axis=0, keepdims=True)
        return act, grad_pre

    def collect(f, act, grad_pre):
        at = slice(f * step, (f + 1) * step)
        total_y[...] += nn(act, wdown[at, :])
        total_n[...] += nt(grad_pre, wup[:, at])
        grad_down = tn(act, cot[...]).astype(bf16)
        for i in range(step // (2 * down_rows)):
            pair = grad_down[2 * i * down_rows : 2 * (i + 1) * down_rows]
            put(f * (step // (2 * down_rows)) + i, 0, 0, pair[:down_rows], pair[down_rows:])
        grad_up = nn(second_t[...], grad_pre).astype(bf16)
        block_of, at_lane = divmod(f * step, width)
        for i in range(parts_of // 2):
            pair = grad_up[2 * i * up_rows : 2 * (i + 1) * up_rows]
            put(i, down_rows + block_of * up_rows, at_lane, pair[:up_rows], pair[up_rows:])

    staged(hidden // step, products, bend, collect)

    sums = [jnp.zeros((1, width), f32)] * 3
    experts = dlog.shape[1]
    stats = [[], [], [], []]
    zero = jnp.zeros((lanes, lanes), f32)
    for at in row_blocks(rows):
        second_at = slice(rows + at.start, rows + at.stop)
        first, second = picks[0, at, :], picks[1, at, :]
        layer_out[at, :] = (mid_keep[at, :] + total_y[at, :] + bdown[...]).astype(bf16)
        unit = unit_keep[at, :]
        back, grad_gain, grad_shift = normalized_back(total_n[at, :], unit, wide(inverse_keep[at, :], pairs), gain[...])
        dy = cot[at, :].astype(f32)
        grad_middle = dy + back
        grad_mid[at, :] = grad_middle
        sums = [a + b for a, b in zip(sums, (jnp.sum(dy, axis=0, keepdims=True), grad_gain, grad_shift))]
        grad_low = grad_middle.astype(bf16)
        low_keep[at, :] = grad_low
        one, two = pick_slots(nt(grad_low, wout[...]), first, second)
        slots = jnp.where(low, one, two)
        head_values = heads[at, :]
        gate = gates[at, :]
        grad_heads = (gate * slots).astype(bf16)
        dom[at, :] = grad_heads
        carried = grad_heads.astype(f32)
        turned = swap(carried)
        do_stack[at, :] = jnp.where(low, zero, turned).astype(bf16)
        do_stack[second_at, :] = jnp.where(low, zero, carried).astype(bf16)
        gated_grad = slots * head_values
        gate_one = jnp.sum(jnp.where(low, gated_grad, 0.0), axis=1, keepdims=True)
        gate_two = jnp.sum(jnp.where(low, 0.0, gated_grad), axis=1, keepdims=True)
        grad_gate = jnp.where(low, gate_one, gate_two)
        weighted = gate * grad_gate
        grad_logit = gate * (grad_gate - (weighted + swap(weighted)))
        logit_other = swap(grad_logit)
        logit_one = jnp.where(low, grad_logit, logit_other)
        logit_two = jnp.where(low, logit_other, grad_logit)
        grad_logits = jnp.where(lane == first, logit_one, jnp.where(lane == second, logit_two, 0.0)).astype(bf16)
        logit_keep[at, :] = grad_logits
        dlog[at, :] = grad_logits[:, :experts]
        carried = carried * head_values
        delta_one = jnp.broadcast_to(jnp.sum(jnp.where(low, carried, 0.0), axis=1, keepdims=True), (lanes, lanes))
        delta_two = jnp.broadcast_to(jnp.sum(jnp.where(low, 0.0, carried), axis=1, keepdims=True), (lanes, lanes))
        delta_out[at, :] = delta_one
        delta_out[second_at, :] = delta_two
        for store, values in zip(stats, (lse[at, :], lse[second_at, :], delta_one, delta_two)):
            store.append(jnp.transpose(values, (1, 0))[0:1, :])
    blocks = []
    for store, terms in zip(stats, (3, 3, 2, 2)):
        rest = jnp.concatenate(store + [jnp.zeros((8 - len(store), lanes), f32)], axis=0)
        for _ in range(terms):
            part = rest.astype(bf16).astype(f32)
            blocks.append(part)
            rest = rest - part
    dom[rows : rows + stat_rows, :] = jnp.concatenate(blocks, axis=0).astype(bf16)
    grad_small[...] = jnp.concatenate(sums + [jnp.zeros((5, width), f32)], axis=0)
    grad_route[...] = tn(logit_keep[...], normed[...])[:experts, :]
    grad_out = tn(mixed_keep[...], low_keep[...]).astype(bf16)
    for i in range(parts_of // 2):
        pair = grad_out[2 * i * up_rows : 2 * (i + 1) * up_rows]
        put(i, piece - up_rows, 0, pair[:up_rows], pair[up_rows:])


def final_step(
    tok, normed, grad_n, grad_mid, wkv, gain, grad_route, grad_bup, small_two, core_at, grad_kv,
    grad_tokens, keep, send, whole,
):
    width = tok.shape[1]
    whole[0:width, :] = tn(normed[...], grad_kv[...]).astype(bf16)
    grad_gain = grad_shift = jnp.zeros((1, width), f32)
    for at in row_blocks(tok.shape[0]):
        upstream = grad_n[at, :] + nt(grad_kv[at, :], wkv[...])
        unit, inverse = normalized(tok[at, :].astype(f32))
        back, more_gain, more_shift = normalized_back(upstream, unit, inverse, gain[...])
        grad_tokens[at, :] = grad_mid[at, :] + back
        grad_gain, grad_shift = grad_gain + more_gain, grad_shift + more_shift
    rows = [grad_gain, grad_shift] + [small_two[i : i + 1, :] for i in range(3)]
    rows += [grad_bup[:, i : i + width] for i in range(0, grad_bup.shape[1], width)]
    rows += [grad_route[i : i + 1, :] for i in range(grad_route.shape[0])]
    small = jnp.concatenate([row[:, i : i + lanes] for row in rows for i in range(0, width, lanes)], axis=0)
    last = whole.shape[0] - width
    small = jnp.concatenate([small, jnp.zeros((last - small.shape[0], lanes), f32)], axis=0)
    whole[width:, :] = small.astype(bf16)
    core = core_at
    piece = keep.shape[0]
    keep[...] = whole[block(core, piece), :]
    send[...] = whole[block(1 - core, piece), :]


parts_of = 32


def place(spread_out):
    if not spread_out:
        return 0, 0, 0, 0
    row, seq = lax.axis_index("row"), lax.axis_index("seq")
    return lax.rem(row, 2), row // 2, lax.rem(seq, 2), seq // 2


def gradient_rows(width, hidden):
    return hidden // parts_of + (hidden // width + 1) * (width // parts_of)


def block(index, count):
    return pl.ds(pl.multiple_of(index * count, 16), count)


def plus(*refs):
    def get(at):
        total = refs[0][at].astype(f32)
        for ref in refs[1:]:
            total = total + ref[at].astype(f32)
        return total.astype(bf16)

    return get


def after_core_kernel(keep, received, one_keep, one_send, two_keep, two_send):
    _, x, y, _ = place(True)
    piece, upper, lower = keep.shape[0] // 16, one_keep.shape[0] // 8, two_keep.shape[0] // 8
    total = plus(keep, received)

    def part(index, offset, count):
        return total((pl.ds(pl.multiple_of(index * piece + offset, 16), count), slice(None)))

    for zy in range(8):
        here = slice(zy * upper, (zy + 1) * upper)
        one_keep[here, :] = part(zy * 2 + x, 0, upper)
        one_send[here, :] = part(zy * 2 + 1 - x, 0, upper)
    for z in range(4):
        for at_x in range(2):
            here = slice((z * 2 + at_x) * lower, (z * 2 + at_x + 1) * lower)
            two_keep[here, :] = part((z * 2 + y) * 2 + at_x, upper, lower)
            two_send[here, :] = part((z * 2 + 1 - y) * 2 + at_x, upper, lower)


def split_kernel(keep, received, kept, sent):
    x = place(True)[1]
    piece = kept.shape[0] // 8
    total = plus(keep, received)
    for i in range(8):
        here = slice(i * piece, (i + 1) * piece)
        kept[here, :] = total((block(i * 2 + x, piece), slice(None)))
        sent[here, :] = total((block(i * 2 + 1 - x, piece), slice(None)))


def after_first_kernel(one, one_in, extra, extra_in, two, two_in, one_keep, one_send, two_keep, two_send):
    _, x, y, _ = place(True)
    upper = one.shape[0] // 8
    for total, mine, kept, sent, piece, offset in (
        (plus(one, one_in), y, one_keep, one_send, upper, 0),
        (plus(extra, extra_in), y, one_keep, one_send, extra.shape[0] // 8, upper),
        (plus(two, two_in), x, two_keep, two_send, two.shape[0] // 8, 0),
    ):
        stride = kept.shape[0] // 4
        for z in range(4):
            here = slice(z * stride + offset, z * stride + offset + piece)
            kept[here, :] = total((block(z * 2 + mine, piece), slice(None)))
            sent[here, :] = total((block(z * 2 + 1 - mine, piece), slice(None)))


def after_second_kernel(one, one_in, two, two_in, *outs):
    z = place(True)[3]
    at = 0
    for total, count in ((plus(one, one_in), one.shape[0] // 4), (plus(two, two_in), two.shape[0] // 4)):
        for i, out in enumerate(outs):
            out[at : at + count, :] = total((block(z ^ i, count), slice(None)))
        at += count


def sum_kernel(*refs):
    refs[-1][...] = plus(*refs[:-1])(Ellipsis)


def join_halves_kernel(*refs):
    z = place(True)[3]
    one, two = refs[4:]
    upper, lower = one.shape[0] // 4, two.shape[0] // 4
    for i in range(4):
        one[block(z ^ i, upper), :] = refs[i][:upper, :]
        two[block(z ^ i, lower), :] = refs[i][upper:, :]


def unpack_kernel(spread_out, turns, outer, fresh, *refs):
    core, x, y, _ = place(spread_out)
    count = 2 * len(turns)
    parts, refs = refs[:count], refs[count if fresh else count + 4 :]
    outs, stages, sems = refs[:4], refs[4:8], refs[8]
    grad_up, grad_down, grad_out, grad_wq = outs
    width, hidden = grad_up.shape
    down_rows, up_rows = hidden // parts_of, width // parts_of
    moves = []

    def send(stage, start, rows, out, device):
        target = out.at[block(device, rows), :]
        moves.append(pltpu.make_async_copy(stage.at[start : start + rows, :], target, sems.at[len(moves)]))
        moves[-1].start()

    at = 0
    for n, turn in enumerate(turns):
        one, two = parts[2 * n : 2 * n + 2]
        for inner in range(2):
            for z in range(4):
                row, low, high = inner * 4 + z, at * down_rows, at * up_rows
                at += 1
                device = ((z * 2 + (y ^ inner)) * 2 + (x ^ outer)) * 2 + (core ^ turn)
                base = row * (down_rows + up_rows)
                stages[1][low : low + down_rows, :] = one[base : base + down_rows, :].astype(f32)
                send(stages[1], low, down_rows, grad_down, device)
                base += down_rows
                stages[3][high : high + up_rows, :] = one[base : base + up_rows, :].astype(f32)
                send(stages[3], high, up_rows, grad_wq, device)
                device = ((z * 2 + (y ^ outer)) * 2 + (x ^ inner)) * 2 + (core ^ turn)
                across = hidden // width
                base = row * (across + 1) * up_rows
                for c in range(across):
                    value = two[base + c * up_rows : base + (c + 1) * up_rows, :]
                    stages[0][high : high + up_rows, c * width : (c + 1) * width] = value.astype(f32)
                send(stages[0], high, up_rows, grad_up, device)
                base += across * up_rows
                stages[2][high : high + up_rows, :] = two[base : base + up_rows, :].astype(f32)
                send(stages[2], high, up_rows, grad_out, device)
    for move in moves:
        move.wait()


def unpack(spread_out, turns, outer, parts, so_far, width, hidden):
    outs = (shape((width, hidden), f32), shape((hidden, width), f32)) + (shape((width, width), f32),) * 2
    share = 4 // len(turns)
    hbm = pl.BlockSpec(memory_space=pltpu.HBM)
    whole = pl.BlockSpec(memory_space=pltpu.VMEM)
    return pl.pallas_call(
        functools.partial(unpack_kernel, spread_out, turns, outer, not so_far),
        out_shape=outs,
        in_specs=[whole] * len(parts) + [hbm] * len(so_far),
        out_specs=(hbm,) * 4,
        scratch_shapes=[pltpu.VMEM((out.shape[0] // share, out.shape[1]), f32) for out in outs]
        + [pltpu.SemaphoreType.DMA((32 * len(turns),))],
        input_output_aliases={len(parts) + i: i for i in range(len(so_far))},
        compiler_params=pltpu.CompilerParams(vmem_limit_bytes=16 * mib),
        cost_estimate=pl.CostEstimate(flops=int(2 * unpack_weight * busy), bytes_accessed=0, transcendentals=0),
    )(*parts, *so_far)


def flip_row(x, mask):
    return lax.ppermute(x, "row", [(i, i ^ mask) for i in range(4)])


def flip_seq(x, mask):
    return lax.ppermute(x, "seq", [(i, i ^ mask) for i in range(8)])


def simple(kernel, outs, *operands):
    return call(kernel, outs, [], 10 * mib, 0.5 * small_weight, *operands)


def add(a, b):
    return (a.astype(f32) + b.astype(f32)).astype(bf16)


def finish_sums(large, small, hidden):
    mine, arrived = large
    keep, send = small
    count, width = mine.shape
    total = add(keep, after(flip_row(send, 1), mine))
    part = shape((2 * count, width), bf16)
    one, two = simple(join_halves_kernel, (part,) * 2, mine, *arrived)
    one_in, two_in = flip_seq(one, 1), flip_row(two, 2)
    total = add(total, after(flip_row(total, 2), one))
    one, two = jnp.concatenate([one, one_in]), jnp.concatenate([two, two_in])
    one_in, two_in = flip_row(one, 2), flip_seq(two, 1)
    one_other, two_other = flip_row(one, 1), flip_row(two, 1)
    total = add(total, after(flip_seq(total, 1), one, two))
    done = unpack(True, (0, 1), 0, (one, two, one_other, two_other), (), width, hidden)
    total = add(total, flip_seq(total, 2))
    total = add(total, after(flip_seq(total, 4), done[3]))
    one_in = after(one_in, total)
    other = flip_row(total, 1)
    one_other, two_other = flip_row(one_in, 1), flip_row(two_in, 1)
    done = unpack(True, (0,), 1, (one_in, two_in), done, width, hidden)
    done = unpack(True, (1,), 1, (one_other, two_other), done, width, hidden)
    return done, (total, other)


def unpack_small_kernel(spread_out, mine, other, grad_wkv, grad_route, grad_bup, *rest):
    small, whole = rest[:5], rest[5]
    core = place(spread_out)[0]
    piece = mine.shape[0]
    whole[block(core, piece), :] = mine[...].astype(f32)
    whole[block(1 - core, piece), :] = other[...].astype(f32)
    width = grad_wkv.shape[0]
    across = width // lanes
    grad_wkv[...] = whole[0:width, :]
    at = width
    for i in range(5):
        for g in range(across):
            small[i][:, g * lanes : (g + 1) * lanes] = whole[at : at + 1, :]
            at += 1
    for g in range(grad_bup.shape[1] // lanes):
        grad_bup[:, g * lanes : (g + 1) * lanes] = whole[at : at + 1, :]
        at += 1
    for i in range(grad_route.shape[0]):
        for g in range(across):
            grad_route[i : i + 1, g * lanes : (g + 1) * lanes] = whole[at : at + 1, :]
            at += 1


busy = 550_000_000
key_weight, query_weight, forward_weight, final_weight, unpack_weight, small_weight = 1.0, 1.0, 1.0, 1.0, 1.0, 1.0


def call(kernel, out_shape, scratch, limit, time, *operands):
    whole = pl.BlockSpec(memory_space=pltpu.VMEM)
    return pl.pallas_call(
        kernel,
        out_shape=out_shape,
        in_specs=[whole] * len(operands),
        out_specs=jax.tree.map(lambda _: whole, out_shape),
        scratch_shapes=scratch,
        compiler_params=pltpu.CompilerParams(vmem_limit_bytes=limit),
        cost_estimate=pl.CostEstimate(flops=int(time * busy), bytes_accessed=0, transcendentals=0),
    )(*operands)


def shape(dims, dtype):
    return jax.ShapeDtypeStruct(tuple(dims), dtype)


def after(value, *earlier):
    return lax.optimization_barrier((value,) + earlier)[0]


def local(
    tokens, cotangent, w_query, w_kv, w_route, w_out, w_up, bias_up, w_down, bias_down,
    gain_one, shift_one, gain_two, shift_two, choices, segment_ids,
):
    size = lax.axis_size("seq")
    tok, cot = tokens[0], cotangent[0]
    rows, width = tok.shape
    hidden = w_up.shape[1]
    route = w_route.T
    experts = route.shape[0]
    row = lambda v: v.reshape(1, -1)
    message = shape((rows + pad_rows, lanes), bf16)
    stacked = (2 * rows, lanes)
    stack = shape(stacked, bf16)
    hbm = pl.BlockSpec(memory_space=pltpu.HBM)
    whole = pl.BlockSpec(memory_space=pltpu.VMEM)
    sent_keys, normed = pl.pallas_call(
        keys_kernel,
        out_shape=(message, shape((rows, width), bf16)),
        in_specs=[hbm] * 5,
        out_specs=(whole,) * 2,
        scratch_shapes=[
            pltpu.VMEM((rows, width), bf16), pltpu.VMEM((width, lanes), bf16), pltpu.VMEM((1, width), f32),
            pltpu.VMEM((1, width), f32), pltpu.VMEM((1, rows), jnp.int32), pltpu.SemaphoreType.DMA((5,)),
        ],
        compiler_params=pltpu.CompilerParams(vmem_limit_bytes=60 * mib),
        cost_estimate=pl.CostEstimate(flops=busy, bytes_accessed=0, transcendentals=0),
    )(tok, w_kv, row(gain_one), row(shift_one), segment_ids)
    spread_out = size == 8 and lax.axis_size("row") == 4
    qm, q_stack, k_stack, v_stack, gates, picks, seg, kvm = call(
        queries_kernel,
        (
            message, stack, stack, stack, shape((rows, lanes), f32), shape((2, rows, lanes), jnp.int32),
            shape((rows, lanes), f32), message,
        ),
        [], 12 * mib, 1.6,
        normed, sent_keys, segment_ids, w_query, route, choices[0].T,
    )
    state = (shape(stacked, f32),) * 2
    finished = (shape((rows, lanes), f32), shape(stacked, f32)) + state

    def forward(parts, first, last, *so_far):
        return call(
            functools.partial(forward_kernel, len(parts), first, last), finished if last else state, [], 12 * mib,
            1.4 * forward_weight * len(parts) * parts[0].shape[0], q_stack, seg, kvm, *parts, *so_far,
        )

    if size == 8:
        far_z, near_z, near_y = flip_seq(sent_keys, 4), flip_seq(sent_keys, 2), flip_seq(sent_keys, 1)
        near_y, near_z, far_z, q_stack, kvm = lax.optimization_barrier((near_y, near_z, far_z, q_stack, kvm))
        near = [m[None] for m in (kvm, near_y, near_z, far_z)]
        others = [flip_seq(near_z, 1), flip_seq(far_z, 1), flip_seq(far_z, 2), flip_seq(after(sent_keys, far_z), 7)]
        others = [m[None] for m in others]
        so_far = forward(near, True, False)
        heads, lse, _, _ = forward(others, False, True, *so_far)
        q_two = jnp.stack([qm, after(flip_seq(qm, 1), so_far[0])])
        q_far = [flip_seq(q_two, 2), flip_seq(q_two, 4)]
        heads = after(heads, q_two)
    else:
        all_kv = [lax.all_gather(kvm, "seq", axis=0, tiled=False)]
        heads, lse, _, _ = forward(all_kv, True, True)
    piece = gradient_rows(width, hidden)
    gradients = shape((piece * parts_of // 2, width), bf16)
    (
        layer_out, keep, send, grad_mid, dom, do_stack, delta, dlog, grad_route, grad_bup, small_two,
    ) = call(
        functools.partial(middle_kernel, spread_out),
        (
            shape((rows, width), bf16), gradients, gradients, shape((rows, width), f32), shape((rows + stat_rows, lanes), bf16),
            stack, shape(stacked, f32), shape((rows, experts), bf16), shape((experts, width), f32),
            shape((1, hidden), f32), shape((8, width), f32),
        ),
        [
            pltpu.VMEM((rows, width), bf16), pltpu.VMEM((width, rows), bf16), pltpu.VMEM((rows, width), f32),
            pltpu.VMEM((rows, width), f32), pltpu.VMEM((rows, width), f32), pltpu.VMEM((rows, width), bf16),
            pltpu.VMEM((rows, width), f32), pltpu.VMEM((rows, lanes), f32), pltpu.VMEM((rows, width), bf16),
            pltpu.VMEM((rows, lanes), bf16),
        ],
        34 * mib, 15,
        tok, cot, heads, gates, picks, lse, normed, w_out, w_up, row(bias_up), w_down, row(bias_down),
        row(gain_two), row(shift_two),
    )
    results = {}
    extra_part = shape((width // 2, width), bf16)

    def query_back(parts, first, last, *earlier):
        finish = (normed, picks, w_query, dlog, route) if last else ()
        outs = (extra_part, extra_part, shape((rows, width), f32)) if last else ()
        results["query"] = call(
            functools.partial(query_back_kernel, spread_out, len(parts), first, last),
            outs + (shape(stacked, f32),),
            [pltpu.VMEM((rows, width), bf16)] if last else [],
            14 * mib, 1.6 * query_weight * len(parts) * parts[0].shape[0],
            after(q_stack, *earlier), do_stack, lse, delta, seg, kvm, *parts, *(() if first else results["query"]), *finish,
        )
        return results["query"][-1]

    extra = 5 + hidden // width + experts
    small_rows = extra * (width // lanes) + width
    small_rows = -(-small_rows // 32) * 32

    def key_back(q_parts, do_parts, first, last, *earlier):
        part = shape((small_rows // 2, lanes), bf16)
        final = (
            tok, normed, results["query"][2], grad_mid, w_kv, row(gain_one), grad_route, grad_bup, small_two,
        ) if last else ()
        results["key"] = call(
            functools.partial(key_back_kernel, spread_out, len(q_parts), first, last),
            ((shape((rows, width), f32), part, part) if last else ()) + state,
            [pltpu.VMEM((rows, lanes), bf16), pltpu.VMEM((small_rows, lanes), bf16)] if last else [],
            18 * mib, 2.1 * key_weight * len(q_parts) * q_parts[0].shape[0] + 2.4 * last,
            after(k_stack, *earlier), v_stack, seg, kvm, *q_parts, *do_parts, *(() if first else results["key"]), *final,
        )
        return results["key"][-1]

    if spread_out:
        send, q_near, q_other = lax.optimization_barrier((send, *q_far))
        q_last = flip_seq(q_other, 2)
        received = flip_row(send, 1)
        d_two = jnp.stack([dom, flip_seq(dom, 1)])
        received = after(received, query_back(near, True, False))
        upper, lower = hidden // parts_of, piece - hidden // parts_of
        more = width // parts_of
        part = lambda count, rows: shape((count * rows, width), bf16)
        one, one_send, two, two_send = simple(
            after_core_kernel, (part(8, upper),) * 2 + (part(8, lower),) * 2, keep, received
        )
        one_in, two_in = flip_row(one_send, 2), flip_seq(two_send, 1)
        d_other, d_near = flip_seq(d_two, 4), flip_seq(d_two, 2)
        query_back(others, False, True, one, d_two, q_last)
        extra, extra_send, _, done = results["query"]
        extra, extra_send = simple(split_kernel, (part(8, more),) * 2, extra, flip_row(extra_send, 1))
        extra_in = flip_row(extra_send, 2)
        done = key_back([q_two], [d_two], True, False, extra, d_other)
        d_last = flip_seq(after(d_other, done), 2)
        one, one_send, two, two_send = simple(
            after_first_kernel, (part(4, upper + more),) * 2 + (part(4, lower),) * 2,
            one, after(one_in, done), extra, extra_in, two, two_in,
        )
        one_in, two_in = flip_seq(one_send, 1), flip_row(two_send, 2)
        done = key_back([q_other], [d_other], False, False, one)
        sent = simple(after_second_kernel, (part(1, piece + more),) * 4, one, after(one_in, done), two, two_in)
        planes = [flip_seq(sent[i], 2 * i) for i in (1, 2, 3)]
        key_back([q_near], [d_near], False, False, sent[0])
        key_back([q_last], [d_last], False, True)
        grad_tokens, *small = results["key"][:3]
        mine = simple(sum_kernel, part(1, piece + more), after(sent[0], small[0]), *planes)
        arrived = [flip_seq(mine, 2 * i) for i in (1, 2, 3)]
        large, small = finish_sums((mine, arrived), small, hidden)
    else:
        query_back(all_kv, True, True)
        gathered = [lax.all_gather(m, "seq", axis=0, tiled=False) for m in (qm, dom)]
        key_back(gathered[:1], gathered[1:], True, True)
        grad_tokens, *small = results["key"][:3]
        small = lax.psum(small, ("seq", "row"))
        sums = lax.psum((keep, send, *results["query"][:2]), ("seq", "row"))
        large = []
        upper = hidden // parts_of
        for total, more in zip(sums[:2], sums[2:]):
            cube = total.reshape(4, 2, 2, piece, width)
            more = more.reshape(4, 2, 2, -1, width)
            one = jnp.concatenate([cube[:, :, :, :upper], more], axis=3)
            two = cube[:, :, :, upper:]
            for i in range(2):
                large.append(one[:, :, i].transpose(1, 0, 2, 3).reshape(-1, width))
                large.append(two[:, i].transpose(1, 0, 2, 3).reshape(-1, width))
        done = unpack(False, (0, 1), 0, (large[0], large[1], large[4], large[5]), (), width, hidden)
        done = unpack(False, (0,), 1, large[2:4], done, width, hidden)
        large = unpack(False, (1,), 1, large[6:8], done, width, hidden)
    grad_wkv, grad_route, grad_bup, *grad_small = call(
        functools.partial(unpack_small_kernel, spread_out),
        (
            shape((width, lanes), f32), shape((experts, width), f32), shape((1, hidden), f32),
        ) + (shape((1, width), f32),) * 5,
        [pltpu.VMEM((small_rows, lanes), f32)], 8 * mib, 0.8, *small,
    )
    grad_up, grad_down, grad_out, grad_wq = large
    return (
        layer_out[None],
        grad_tokens[None],
        grad_wq,
        grad_wkv,
        grad_route.T,
        grad_out,
        grad_up,
        grad_bup.reshape(-1),
        grad_down,
        grad_small[2].reshape(-1),
        grad_small[0].reshape(-1),
        grad_small[1].reshape(-1),
        grad_small[3].reshape(-1),
        grad_small[4].reshape(-1),
    )


def solution(mesh):
    split_tokens = P("row", "seq", None)
    placed = (split_tokens, split_tokens) + (P(),) * 12 + (split_tokens, P("row", "seq"))
    return jax.shard_map(
        local,
        mesh=mesh,
        in_specs=placed,
        out_specs=(split_tokens, split_tokens) + (P(),) * 12,
        check_vma=False,
    )
```
